32 devices in a mesh: rep: 4 (over z), fsdp: 8 (over y, x, core).
Axes of the slice: x: 2, y: 2, z: 4, core: 2. Of those that a mesh axis runs over, the one named last changes fastest.
Arguments:
- layer_input: bfloat16 [16, 1024, 768], P('rep', 'fsdp'), may hold values from -40 to 40
- positions: int32 [16, 1024], P('rep', 'fsdp'), may hold values from 0 to 1023, as said below
- cotangent: bfloat16 [16, 1024, 768], P('rep', 'fsdp'), may hold values from -6 to 6
- w_qkv: bfloat16 [768, 2304], P('fsdp'), may hold values from -4 to 4
- w_out: bfloat16 [768, 768], P('fsdp'), may hold values from -1.75 to 1.75
- w_up: bfloat16 [768, 3072], P('fsdp'), may hold values from -0.21875 to 0.21875
- w_down: bfloat16 [768, 3072], P('fsdp'), may hold values from -0.109375 to 0.109375
- ln1_gain: bfloat16 [768], P('fsdp'), may hold values from 0.5 to 1.5
- ln1_bias: bfloat16 [768], P('fsdp'), may hold values from -1.5 to 1.5
- ln2_gain: bfloat16 [768], P('fsdp'), may hold values from 0.5 to 1.5
- ln2_bias: bfloat16 [768], P('fsdp'), may hold values from -1.5 to 1.5
- qkv_bias: bfloat16 [2304], P('fsdp'), may hold values from -2.5 to 2.5
- out_bias: bfloat16 [768], P('fsdp'), may hold values from -2.5 to 2.5
- up_bias: bfloat16 [3072], P('fsdp'), may hold values from -2.5 to 2.5
- down_bias: bfloat16 [768], P('fsdp'), may hold values from -2.5 to 2.5
Outputs:
- output: bfloat16 [16, 1024, 768], P('rep', 'fsdp')
- grad_input: bfloat16 [16, 1024, 768], P('rep', 'fsdp')
- grad_w_qkv: float32 [768, 2304], P('fsdp')
- grad_w_out: float32 [768, 768], P('fsdp')
- grad_w_up: float32 [768, 3072], P('fsdp')
- grad_w_down: float32 [768, 3072], P('fsdp')
- grad_ln1_gain: float32 [768], P('fsdp')
- grad_ln1_bias: float32 [768], P('fsdp')
- grad_ln2_gain: float32 [768], P('fsdp')
- grad_ln2_bias: float32 [768], P('fsdp')
- grad_qkv_bias: float32 [2304], P('fsdp')
- grad_out_bias: float32 [768], P('fsdp')
- grad_up_bias: float32 [3072], P('fsdp')
- grad_down_bias: float32 [768], P('fsdp')
The draws below stay inside these ranges and needn't reach their ends.
Inputs may be any that keep to these rules, and one draw needn't show every extreme that they name: positions[s, 0] is 0, and each later positions[s, t] is either 0 or positions[s, t - 1] + 1; sequence 0 is one document of 1024 tokens.
All inputs are finite; a program needn't handle non-finite values.
Results may differ from the reference program's by a relative error of at most 0.0093.
Values may be sent and summed in bfloat16 or wider, within the bound.
No kernel may reach another device: no remote copies, remote signals or barrier semaphores. Data moves between devices by JAX's collectives and lax.ppermute only.
A program may use at most 320 MiB of HBM per device.

```python
import math
import jax
import jax.numpy as jnp
from jax import lax

D = 768
H = 12
HD = 64
ROT = 16
FF = 3072
LEN = 1024
SEQS = 16


def draw_positions(key, part):
    index = jnp.arange(LEN, dtype=jnp.int32)
    marks = jax.random.randint(key, (SEQS, LEN), 0, max(LEN // 4, 2)) == 0
    marks = marks.at[:, 0].set(True)
    marks = marks.at[0, :].set(index == 0)
    starts = lax.cummax(jnp.where(marks, index[None, :], 0), axis=1)
    return (index[None, :] - starts).astype(jnp.int32)


def draw_layer_input(key, part):
    base = jax.random.normal(jax.random.fold_in(key, 1), (SEQS, LEN, D), jnp.float32)
    return jnp.clip(base, -40.0, 40.0).astype(jnp.bfloat16)


def draw_w_qkv(key, part):
    base = jax.random.normal(jax.random.fold_in(key, 11), (D, 3 * D), jnp.float32) / math.sqrt(D)
    return jnp.clip(base, -4.0, 4.0).astype(jnp.bfloat16)


def block_scale(key, shape, shards, low, largest):
    level, own = 1.0, jax.random.fold_in(key, 6)
    for dim, parts in shards:
        heights = jnp.exp(jax.random.uniform(jax.random.fold_in(own, dim), (parts,), jnp.float32, low / len(shards), largest / len(shards)))
        level = level * jnp.repeat(heights, shape[dim] // parts).reshape([-1 if axis == dim else 1 for axis in range(len(shape))])
    return level


def gaussian(rng, extent, deviation, reach, cuts=(), held_as=jnp.bfloat16):
    values = deviation * jax.random.normal(rng, extent, jnp.float32)
    if cuts:
        values = values * block_scale(rng, extent, cuts, -0.22, 0.18)
    return jnp.clip(values, -reach, reach).astype(held_as)


def setup_inputs(seed: int = 0) -> dict:
    splits = jax.random.split(jax.random.key(seed), 16)
    layer_input = draw_layer_input(jax.random.fold_in(splits[15], 71), 0)
    positions = draw_positions(jax.random.fold_in(splits[15], 71), 0)
    cotangent = gaussian(splits[2], (SEQS, LEN, D), 1.0, 6.0, ((0, 4), (1, 8)))
    w_qkv = draw_w_qkv(jax.random.fold_in(splits[15], 71), 0)
    w_out = gaussian(splits[4], (D, D), (max(D // 64, 1)) ** -0.5, 1.75, ((0, 8),))
    w_up = gaussian(splits[5], (D, FF), D ** -0.5, 0.21875, ((0, 8),))
    w_down = gaussian(splits[6], (D, FF), FF ** -0.5, 0.109375, ((0, 8),))
    ln1_gain = jnp.clip(1.0 + 0.1 * jax.random.normal(splits[7], (D,), jnp.float32), 0.5, 1.5).astype(jnp.bfloat16)
    ln1_bias = gaussian(splits[8], (D,), 0.3, 1.5, ((0, 8),))
    ln2_gain = jnp.clip(1.0 + 0.1 * jax.random.normal(splits[9], (D,), jnp.float32), 0.5, 1.5).astype(jnp.bfloat16)
    ln2_bias = gaussian(splits[10], (D,), 0.3, 1.5, ((0, 8),))
    qkv_bias = gaussian(splits[11], (3 * D,), 0.5, 2.5, ((0, 8),))
    out_bias = gaussian(splits[12], (D,), 0.5, 2.5, ((0, 8),))
    up_bias = gaussian(splits[13], (FF,), 0.5, 2.5, ((0, 8),))
    down_bias = gaussian(splits[14], (D,), 0.5, 2.5, ((0, 8),))
    return dict(layer_input=layer_input, positions=positions, cotangent=cotangent, w_qkv=w_qkv, w_out=w_out, w_up=w_up, w_down=w_down, ln1_gain=ln1_gain, ln1_bias=ln1_bias, ln2_gain=ln2_gain, ln2_bias=ln2_bias, qkv_bias=qkv_bias, out_bias=out_bias, up_bias=up_bias, down_bias=down_bias)


@jax.custom_vjp
def low(v):
    return lax.optimization_barrier(v.astype(jnp.bfloat16)).astype(jnp.float32)

@jax.custom_vjp
def low_back(v):
    return v

def low_keep(v):
    return (low(v), None)

def low_pass(kept, grad):
    return (grad,)

def back_keep(v):
    return (v, None)

def back_low(kept, grad):
    return (low(grad),)
low.defvjp(low_keep, low_pass)
low_back.defvjp(back_keep, back_low)
EPS = 1e-05
NEG = -1e+30
HIGH = lax.Precision.HIGHEST

def norm_rows(values, gain, shift):
    mean = lax.optimization_barrier(jnp.mean(values, axis=-1, keepdims=True))
    centred = values - mean
    spread = lax.optimization_barrier(jnp.mean(centred * centred, axis=-1, keepdims=True))
    return centred * lax.rsqrt(spread + EPS) * gain + shift

def rotate(values, cosine, sine):
    half = ROT // 2
    head = values[..., :ROT]
    turned = jnp.concatenate([-head[..., half:], head[..., :half]], axis=-1)
    return jnp.concatenate([head * cosine + turned * sine, values[..., ROT:]], axis=-1)

def angles(positions):
    inverse = 10000.0 ** (-jnp.arange(0, ROT, 2, dtype=jnp.float32) / ROT)
    phase = positions.astype(jnp.float32)[..., None] * inverse
    phase = jnp.concatenate([phase, phase], axis=-1)[..., None, :]
    return (jnp.cos(phase), jnp.sin(phase))

def attention(query, key, value, first):
    block = min(512, LEN)
    index = jnp.arange(LEN, dtype=jnp.int32)

    def attend(number):
        begin = number * block
        rows_q = lax.dynamic_slice_in_dim(query, begin, block, 0)
        row_first = lax.dynamic_slice_in_dim(first, begin, block, 0)
        row_index = begin + jnp.arange(block, dtype=jnp.int32)
        scores = low_back(jnp.einsum('qhd,khd->hqk', rows_q, key, precision=HIGH) * 0.125)
        seen = (index[None, :] <= row_index[:, None]) & (index[None, :] >= row_first[:, None])
        scores = jnp.where(seen[None], scores, jnp.float32(NEG))
        top = lax.optimization_barrier(jnp.max(scores, axis=-1, keepdims=True))
        weights = jnp.exp(scores - top)
        probs = low(weights / lax.optimization_barrier(jnp.sum(weights, axis=-1, keepdims=True)))
        return jnp.einsum('hqk,khd->qhd', probs, value, precision=HIGH)
    mixed = lax.map(jax.checkpoint(attend), jnp.arange(LEN // block, dtype=jnp.int32))
    return mixed.reshape(LEN, H * HD)

def layer(source, params, cosine, sine, first):
    w_qkv, w_out, w_up, w_down, gain_one, shift_one, gain_two, shift_two, bias_qkv, bias_out, bias_up, bias_down = params
    input_one = low(norm_rows(source, gain_one, shift_one))
    input_two = low(norm_rows(source, gain_two, shift_two))
    qkv = low_back(jnp.dot(input_one, w_qkv, precision=HIGH) + bias_qkv)
    shaped = qkv.reshape(LEN, 3, H, HD)
    query = low(rotate(shaped[:, 0], cosine, sine))
    key = low(rotate(shaped[:, 1], cosine, sine))
    value = low(shaped[:, 2])
    attended = low(low_back(attention(query, key, value, first)))
    attn_branch = jnp.dot(attended, w_out.T, precision=HIGH) + bias_out
    up = low_back(jnp.dot(input_two, w_up, precision=HIGH) + bias_up)
    hidden = low(jax.nn.gelu(up, approximate=False))
    mlp_branch = jnp.dot(hidden, w_down.T, precision=HIGH) + bias_down
    return source + attn_branch + mlp_branch

def reference(layer_input, positions, cotangent, w_qkv, w_out, w_up, w_down, ln1_gain, ln1_bias, ln2_gain, ln2_bias, qkv_bias, out_bias, up_bias, down_bias):
    params = tuple((p.astype(jnp.float32) for p in (w_qkv, w_out, w_up, w_down, ln1_gain, ln1_bias, ln2_gain, ln2_bias, qkv_bias, out_bias, up_bias, down_bias)))

    def one_sequence(carry, item):
        source, place, grad_out = item
        cosine, sine = angles(place)
        first = jnp.arange(LEN, dtype=jnp.int32) - place.astype(jnp.int32)
        result, pull = jax.vjp(lambda v, p: layer(v, p, cosine, sine, first), source.astype(jnp.float32), params)
        grad_source, grad_params = pull(grad_out.astype(jnp.float32))
        carry = jax.tree.map(jnp.add, carry, grad_params)
        return (carry, (result.astype(jnp.bfloat16), grad_source.astype(jnp.bfloat16)))
    zeros = jax.tree.map(jnp.zeros_like, params)
    grads, (output, grad_input) = lax.scan(one_sequence, zeros, (layer_input, positions, cotangent))
    return (output, grad_input) + tuple(grads)
```

```python
import functools

import jax
import jax.numpy as jnp
from jax import lax
from jax.experimental import pallas as pl
from jax.experimental.pallas import tpu as pltpu
from jax.sharding import PartitionSpec as P

H = 12
HD = 64
ROT = 16

EPS = 1e-05
NEG = -1e30

F32 = jnp.float32
BF16 = jnp.bfloat16


def dot(a, b, dims):
    return lax.dot_general(a, b, (dims, ((), ())), preferred_element_type=F32)


def attention_kernel(
    span, heads, slot, q_in, k_in, v_in, g_in, first_in,
    o_out, gq_out, gk_out, gv_out,
    qs, ks, vs, gs, o_turned, gq_turned, gk_sum, gv_sum,
):
    length = q_in.shape[1]
    blocks = length // span
    tile = 256
    for f in range(blocks):
        at = pl.ds(pl.multiple_of(slot[f] * span, span), span)
        to = slice(f * span, (f + 1) * span)
        for source, kept in ((q_in, qs), (k_in, ks), (v_in, vs), (g_in, gs)):
            rows = source[0, at, :]
            for h in range(heads):
                kept[h, to, :] = rows[:, h * HD : (h + 1) * HD]

    def one_head(h, carry):
        keys = ks[h]
        values = vs[h]
        keys_turned = keys.astype(F32).T.astype(BF16)
        values_turned = values.astype(F32).T.astype(BF16)
        for i in range(length // tile):
            seen = (i + 1) * tile
            here = slice(i * tile, seen)
            query = qs[h, here, :]
            grad = gs[h, here, :]
            first = first_in[0, :, here]
            raw = dot(keys[:seen], query, ((1,), (1,))) * 0.125
            key_index = lax.broadcasted_iota(jnp.int32, (seen, tile), 0)
            query_index = i * tile + lax.broadcasted_iota(jnp.int32, (seen, tile), 1)
            raw = jnp.where((key_index >= first) & (key_index <= query_index), raw, NEG)
            weights = jnp.exp(raw - jnp.max(raw, axis=0, keepdims=True))
            probs = weights * (1.0 / jnp.sum(weights, axis=0, keepdims=True))
            grad_probs = dot(values[:seen], grad, ((1,), (1,)))
            carried = jnp.sum(probs * grad_probs, axis=0, keepdims=True)
            grad_scores = (probs * (grad_probs - carried)).astype(BF16)
            low = probs.astype(BF16)
            o_turned[h, :, here] = dot(values_turned[:, :seen], low, ((1,), (0,)))
            gq_turned[h, :, here] = dot(keys_turned[:, :seen], grad_scores, ((1,), (0,)))
            gk_part = dot(grad_scores, query, ((1,), (0,)))
            gv_part = dot(low, grad, ((1,), (0,)))
            if i > 0:
                old = slice(0, i * tile)
                gk_sum[h, old, :] += gk_part[: i * tile]
                gv_sum[h, old, :] += gv_part[: i * tile]
            gk_sum[h, here, :] = gk_part[i * tile :]
            gv_sum[h, here, :] = gv_part[i * tile :]
        return carry

    lax.fori_loop(0, heads, one_head, 0)
    for f in range(blocks):
        at = pl.ds(pl.multiple_of(slot[f] * span, span), span)
        to = slice(f * span, (f + 1) * span)
        o_out[0, at, :] = jnp.concatenate(
            [o_turned[h, :, to].T for h in range(heads)], axis=1
        ).astype(BF16)
        gq_out[0, at, :] = (
            jnp.concatenate([gq_turned[h, :, to].T for h in range(heads)], axis=1) * 0.125
        )
        gk_out[0, at, :] = (
            jnp.concatenate([gk_sum[h, to, :] for h in range(heads)], axis=1) * 0.125
        )
        gv_out[0, at, :] = jnp.concatenate(
            [gv_sum[h, to, :] for h in range(heads)], axis=1
        ).astype(BF16)


def attention(slot, query, key, value, grad, first, span):
    count, length, columns = query.shape
    heads = columns // HD
    block = pl.BlockSpec((1, length, columns), lambda s, slot: (s, 0, 0))
    shape = (count, length, columns)
    return pl.pallas_call(
        functools.partial(attention_kernel, span, heads),
        grid_spec=pltpu.PrefetchScalarGridSpec(
            num_scalar_prefetch=1,
            grid=(count,),
            in_specs=[block] * 4 + [pl.BlockSpec((1, 1, length), lambda s, slot: (s, 0, 0))],
            out_specs=[block] * 4,
            scratch_shapes=[pltpu.VMEM((heads, length, HD), BF16)] * 4
            + [pltpu.VMEM((heads, HD, length), F32)] * 2
            + [pltpu.VMEM((heads, length, HD), F32)] * 2,
        ),
        out_shape=[
            jax.ShapeDtypeStruct(shape, BF16),
            jax.ShapeDtypeStruct(shape, F32),
            jax.ShapeDtypeStruct(shape, F32),
            jax.ShapeDtypeStruct(shape, BF16),
        ],
        compiler_params=pltpu.CompilerParams(vmem_limit_bytes=56 * 2**20),
        cost_estimate=pl.CostEstimate(
            flops=6 * 2 * count * heads * length * length * 160,
            bytes_accessed=count * length * columns * 20,
            transcendentals=count * heads * length * length,
        ),
        name="attention",
    )(slot, query, key, value, grad, first)


def on_device(
    layer_input,
    positions,
    cotangent,
    w_qkv,
    w_out,
    w_up,
    w_down,
    ln1_gain,
    ln1_bias,
    ln2_gain,
    ln2_bias,
    qkv_bias,
    out_bias,
    up_bias,
    down_bias,
):
    seqs, span, width = layer_input.shape
    shards = lax.axis_size("fsdp")
    reps = lax.axis_size("rep")
    low_count = shards // seqs
    pair = 2 if reps % 2 == 0 and H % (2 * low_count) == 0 else 1
    parts = pair * low_count
    me = lax.axis_index("fsdp")
    rep = lax.axis_index("rep")
    chip = me // low_count
    low = me % low_count
    parity = me % 2
    pair_bit = rep % pair
    part = pair_bit * low_count + low
    high_masks = []
    while low_count * 2 ** len(high_masks) < shards:
        high_masks.append(2 ** len(high_masks))
    phases = len(high_masks)
    own_rows = w_qkv.shape[0]
    q_cols = H // parts * HD
    f_cols = w_up.shape[1] // parts

    def swap_fsdp(v, mask):
        return lax.ppermute(v, "fsdp", [(i, i ^ mask) for i in range(shards)])

    def swap_mixed(v, phase):
        def to(i):
            mask = high_masks[phase] if i % 2 == 0 else high_masks[phases - 1 - phase]
            return i ^ (mask * low_count)

        return lax.ppermute(v, "fsdp", [(i, to(i)) for i in range(shards)])

    def swap_rep(v, mask):
        return lax.ppermute(v, "rep", [(i, i ^ mask) for i in range(reps)])

    def pick(v, index, axis=0):
        return lax.dynamic_index_in_dim(v, index, axis, keepdims=False)

    slot_mask = []
    for s in range(seqs):
        even = sum(high_masks[p] for p in range(phases) if s >> p & 1)
        odd = sum(high_masks[phases - 1 - p] for p in range(phases) if s >> p & 1)
        slot_mask.append(jnp.where(parity == 0, even, odd))
    inverse_slot = jnp.zeros((seqs,), jnp.int32)
    for s in range(seqs):
        inverse_slot = inverse_slot.at[slot_mask[s]].set(s)

    def gather_rows(block):
        slots = [block]
        for p in range(phases):
            slots = slots + [swap_mixed(v, p) for v in slots]
        stacked = jnp.stack(slots)
        return jnp.concatenate([pick(stacked, inverse_slot[i ^ chip]) for i in range(seqs)])

    def take_part(w, index, groups):
        rows = w.shape[0]
        step = w.shape[1] // groups // parts
        return jnp.concatenate(
            [
                lax.dynamic_slice(
                    w, (0, g * (w.shape[1] // groups) + index * step), (rows, step)
                )
                for g in range(groups)
            ],
            axis=1,
        )

    def take_chunk(index):
        return [
            jnp.concatenate([take_part(w_qkv, index, 3), take_part(w_out, index, 1)], axis=1),
            take_part(w_up, index, 1),
            take_part(w_down, index, 1),
        ]

    def gather_low(own, messages):
        blocks = [own] + [swap_fsdp(m, o) for o, m in zip(range(1, low_count), messages)]
        stacked = jnp.stack(blocks)
        return jnp.concatenate([pick(stacked, i ^ low) for i in range(low_count)])

    def spread_tokens(v):
        mine = [pick(v, chip)]
        for j in range(1, seqs):
            mine.append(swap_fsdp(pick(v, chip ^ j), j * low_count))
        mine = jnp.stack(mine)
        both = [mine]
        if pair == 2:
            both.append(swap_rep(mine, 1))
        both = jnp.stack(both)
        cores = [both] + [swap_fsdp(both, o) for o in range(1, low_count)]
        return jnp.stack(cores, axis=1)

    def collect_tokens(v):
        total = v[:, 0].astype(F32)
        for o in range(1, low_count):
            total = total + swap_fsdp(v[:, o], o).astype(F32)
        total = total.astype(BF16)
        mine = total[0]
        if pair == 2:
            mine = (mine.astype(F32) + swap_rep(total[1], 1).astype(F32)).astype(BF16)
        blocks = [mine[0]] + [swap_fsdp(mine[j], j * low_count) for j in range(1, seqs)]
        stacked = jnp.stack(blocks)
        return jnp.stack([pick(stacked, s ^ chip) for s in range(seqs)])

    own_chunks = take_chunk(part)
    sent_chunks = [take_chunk(pair_bit * low_count + (low ^ o)) for o in range(1, low_count)]

    def weight(number):
        return gather_rows(gather_low(own_chunks[number], [m[number] for m in sent_chunks]))

    packed = jnp.concatenate(
        [ln1_gain, ln1_bias, ln2_gain, ln2_bias, qkv_bias, out_bias, up_bias, down_bias]
    )[None]
    mask = 1
    vectors = packed
    while mask < shards:
        other = swap_fsdp(vectors, mask)
        bit = (me & mask) != 0
        vectors = jnp.concatenate(
            [jnp.where(bit, other, vectors), jnp.where(bit, vectors, other)]
        )
        mask *= 2
    small = []
    at = 0
    for v in (ln1_gain, ln1_bias, ln2_gain, ln2_bias, qkv_bias, out_bias, up_bias, down_bias):
        small.append(vectors[:, at : at + v.shape[0]].reshape(-1).astype(F32))
        at += v.shape[0]
    gain_one, shift_one, gain_two, shift_two, bias_qkv, bias_out, bias_up, bias_down = small

    where = spread_tokens(positions)
    tokens = spread_tokens(layer_input)
    grads = spread_tokens(cotangent)
    rows = pair * shards * span
    source = tokens.reshape(rows, width).astype(F32)
    grad_out = grads.reshape(rows, width)

    block_index = jnp.arange(shards, dtype=jnp.int32)
    slot = ((block_index % low_count) ^ low) * seqs + ((block_index // low_count) ^ chip)
    length = shards * span
    blocks = where.reshape(pair, shards, span)
    in_order = jnp.concatenate([pick(blocks, slot[f], 1) for f in range(shards)], axis=1)
    in_order = in_order.reshape(pair, 1, length)
    first_seen = jnp.arange(length, dtype=jnp.int32) - in_order

    inverse = 10000.0 ** (-jnp.arange(0, ROT, 2, dtype=F32) / ROT)
    phase = where.reshape(rows).astype(F32)[:, None] * inverse
    cosine = jnp.cos(phase)
    sine = jnp.sin(phase)
    half = ROT // 2
    still = jnp.zeros((rows, HD - ROT), F32)
    one_cos = jnp.concatenate([cosine, cosine, still + 1.0], axis=1)
    one_sin = jnp.concatenate([-sine, sine, still], axis=1)
    cos_cols = jnp.tile(one_cos, (1, q_cols // HD))
    sin_cols = jnp.tile(one_sin, (1, q_cols // HD))
    in_first = (jnp.arange(q_cols) % HD) < half

    def turned(v):
        return jnp.where(in_first, jnp.roll(v, -half, axis=1), jnp.roll(v, half, axis=1))

    def rotate(v):
        return v * cos_cols + turned(v) * sin_cols

    def rotate_back(v):
        return v * cos_cols - turned(v) * sin_cols

    mean = jnp.mean(source, axis=1, keepdims=True)
    centred = source - mean
    scale = lax.rsqrt(jnp.mean(centred * centred, axis=1, keepdims=True) + EPS)
    normed = centred * scale
    input_one = (normed * gain_one + shift_one).astype(BF16)
    input_two = (normed * gain_two + shift_two).astype(BF16)

    chunk = weight(0)
    part_qkv = chunk[:, : 3 * q_cols]
    part_out = chunk[:, 3 * q_cols :]
    part_up = weight(1)
    part_down = weight(2)

    qkv_part_bias = take_part(bias_qkv[None], part, 3)
    up_part_bias = take_part(bias_up[None], part, 1)
    qkv = dot(input_one, part_qkv, ((1,), (0,))) + qkv_part_bias
    query = rotate(qkv[:, :q_cols]).astype(BF16)
    key = rotate(qkv[:, q_cols : 2 * q_cols]).astype(BF16)
    value = qkv[:, 2 * q_cols :].astype(BF16)
    grad_mixed = dot(grad_out, part_out, ((1,), (0,))).astype(BF16)

    up = dot(input_two, part_up, ((1,), (0,))) + up_part_bias
    grad_hidden = dot(grad_out, part_down, ((1,), (0,)))
    bell = 0.5 * (1.0 + lax.erf(up * (0.5**0.5)))
    hidden = (up * bell).astype(BF16)
    slope = bell + up * jnp.exp(-0.5 * up * up) * 0.3989422804014327
    grad_up = (grad_hidden * slope).astype(BF16)

    per_seq = lambda v: v.reshape(pair, length, q_cols)
    mixed, grad_query, grad_key, grad_value = attention(
        slot, per_seq(query), per_seq(key), per_seq(value), per_seq(grad_mixed), first_seen, span
    )
    flat = lambda v: v.reshape(rows, q_cols)
    attended = flat(mixed)
    grad_qkv = jnp.concatenate(
        [
            rotate_back(flat(grad_query)).astype(BF16),
            rotate_back(flat(grad_key)).astype(BF16),
            flat(grad_value),
        ],
        axis=1,
    )

    shaped = (pair, low_count, seqs, span, width)
    out_part = dot(attended, part_out, ((1,), (1,))) + dot(hidden, part_down, ((1,), (1,)))
    out_sum = collect_tokens(out_part.astype(BF16).reshape(shaped))
    output = (
        layer_input.astype(F32) + out_sum.astype(F32) + bias_out + bias_down
    ).astype(BF16)

    grad_one = dot(grad_qkv, part_qkv, ((1,), (1,)))
    grad_two = dot(grad_up, part_up, ((1,), (1,)))
    both = grad_one * gain_one + grad_two * gain_two
    grad_sum = collect_tokens(both.astype(BF16).reshape(shaped)).astype(F32)
    mine = layer_input.astype(F32)
    mine_mean = jnp.mean(mine, axis=-1, keepdims=True)
    mine_centred = mine - mine_mean
    mine_scale = lax.rsqrt(jnp.mean(mine_centred * mine_centred, axis=-1, keepdims=True) + EPS)
    mine_normed = mine_centred * mine_scale
    pulled = (
        grad_sum
        - jnp.mean(grad_sum, axis=-1, keepdims=True)
        - mine_normed * jnp.mean(grad_sum * mine_normed, axis=-1, keepdims=True)
    ) * mine_scale
    grad_input = (cotangent.astype(F32) + pulled).astype(BF16)

    def scatter_rows(v):
        blocks = v.reshape(seqs, width // seqs, v.shape[1])
        slots = [pick(blocks, chip ^ slot_mask[s]) for s in range(seqs)]
        for p in reversed(range(phases)):
            half_count = len(slots) // 2
            slots = [
                (kept.astype(F32) + swap_mixed(sent, p).astype(F32)).astype(BF16)
                for kept, sent in zip(slots[:half_count], slots[half_count:])
            ]
        return slots[0]

    def finish(v):
        v = scatter_rows(v.astype(BF16))
        mask = pair
        while mask < reps:
            v = (v.astype(F32) + swap_rep(v, mask).astype(F32)).astype(BF16)
            mask *= 2
        v = v.reshape(low_count, own_rows, v.shape[1])
        blocks = [pick(v, low)]
        for o in range(1, low_count):
            blocks.append(swap_fsdp(pick(v, low ^ o), o))
        blocks = jnp.stack(blocks)
        if pair == 2:
            blocks = jnp.concatenate([blocks, swap_rep(blocks, 1)])
        return [pick(blocks, i ^ part) for i in range(parts)]

    chunk_grads = finish(
        jnp.concatenate(
            [dot(input_one, grad_qkv, ((0,), (0,))), dot(grad_out, attended, ((0,), (0,)))], axis=1
        )
    )
    up_grads = finish(dot(input_two, grad_up, ((0,), (0,))))
    down_grads = finish(dot(grad_out, hidden, ((0,), (0,))))
    grad_w_qkv = jnp.concatenate(
        [c[:, g * q_cols : (g + 1) * q_cols] for g in range(3) for c in chunk_grads], axis=1
    ).astype(F32)
    grad_w_out = jnp.concatenate([c[:, 3 * q_cols :] for c in chunk_grads], axis=1).astype(F32)
    grad_w_up = jnp.concatenate(up_grads, axis=1).astype(F32)
    grad_w_down = jnp.concatenate(down_grads, axis=1).astype(F32)

    def place(v, groups):
        total = jnp.zeros((groups, parts, v.shape[0] // groups), F32)
        return lax.dynamic_update_slice(
            total, v.reshape(groups, 1, v.shape[0] // groups), (0, part, 0)
        ).reshape(-1)

    local = [
        jnp.sum(grad_one * normed, axis=0),
        jnp.sum(grad_one, axis=0),
        jnp.sum(grad_two * normed, axis=0),
        jnp.sum(grad_two, axis=0),
        place(jnp.sum(grad_qkv.astype(F32), axis=0), 3),
        jnp.sum(cotangent.astype(F32), axis=(0, 1)),
        place(jnp.sum(grad_up.astype(F32), axis=0), 1),
    ]
    owned = jnp.concatenate([v.reshape(shards, -1) for v in local], axis=1)
    mask = shards // 2
    while mask:
        count = owned.shape[0] // 2
        bit = (me & mask) != 0
        sent = jnp.where(bit, owned[:count], owned[count:])
        kept = jnp.where(bit, owned[count:], owned[:count])
        owned = kept + swap_fsdp(sent, mask)
        mask //= 2
    mask = 1
    while mask < reps:
        owned = owned + swap_rep(owned, mask)
        mask *= 2
    owned = owned[0]
    vector_outs = []
    at = 0
    for v in local:
        size = v.shape[0] // shards
        vector_outs.append(owned[at : at + size])
        at += size
    return (
        output,
        grad_input,
        grad_w_qkv,
        grad_w_out,
        grad_w_up,
        grad_w_down,
        *vector_outs,
        vector_outs[5],
    )


def solution(mesh):
    tokens = P("rep", "fsdp", None)
    matrix = P("fsdp", None)
    vector = P("fsdp")
    return jax.shard_map(
        on_device,
        mesh=mesh,
        in_specs=(tokens, P("rep", "fsdp"), tokens) + (matrix,) * 4 + (vector,) * 8,
        out_specs=(tokens, tokens) + (matrix,) * 4 + (vector,) * 8,
        check_vma=False,
    )
```

```python
import functools

import jax
import jax.numpy as jnp
from jax import lax
from jax.experimental import pallas as pl
from jax.experimental.pallas import tpu as pltpu
from jax.sharding import PartitionSpec as P

H = 12
HD = 64
ROT = 16
TILE = 256
VEC = 16
HEADS = 3

COST = {
    "split_input": 1.0,
    "split_cotangent": 1.0,
    "split_weights": 1.0,
    "tables_second": 0.1,
    "middle_1": 0.1,
    "back_1": 0.1,
    "middle_0": 10.0,
    "second_grads": 0.1,
    "tables_first": 0.1,
    "front": 0.1,
    "attention_0": 10.0,
    "first_grads_0": 0.1,
    "attention_1": 10.0,
    "back_0": 10.0,
    "first_grads_1": 0.1,
    "finish_tokens": 1.0,
    "second_end": 1.0,
    "first_end": 1.0,
}
FLOPS = 1.15e9
BYTES = 3.6e6

EPS = 1e-05
NEG = -1e30

F32 = jnp.float32
BF16 = jnp.bfloat16
I32 = jnp.int32

NN = ((1,), (0,))
NT = ((1,), (1,))
TN = ((0,), (0,))


def dot(a, b, dims):
    return lax.dot_general(a, b, (dims, ((), ())), preferred_element_type=F32)


def at(start, size, multiple):
    return pl.ds(pl.multiple_of(start, multiple), size)


class Place:
    def __init__(self, seqs, shards, reps):
        self.seqs, self.shards, self.reps = seqs, shards, reps
        self.low_count = shards // seqs
        self.pair = 2 if reps % 2 == 0 and H % (2 * self.low_count) == 0 else 1
        self.parts = self.pair * self.low_count
        self.line = Line()
        self.groups = H // self.low_count // HEADS
        self.masks = []
        while 2 ** len(self.masks) < seqs:
            self.masks.append(2 ** len(self.masks))
        self.phases = len(self.masks)

    def chip(self):
        return lax.axis_index("fsdp") // self.low_count

    def low(self):
        return lax.axis_index("fsdp") % self.low_count

    def part(self):
        return (lax.axis_index("rep") % self.pair) * self.low_count + self.low()

    def owner(self, slot):
        even = sum(self.masks[p] for p in range(self.phases) if slot >> p & 1)
        odd = sum(self.masks[self.phases - 1 - p] for p in range(self.phases) if slot >> p & 1)
        if even == odd:
            return self.chip() ^ even
        return self.chip() ^ jnp.where(lax.axis_index("fsdp") % 2 == 0, even, odd)

    def slot(self, block):
        j = (block // self.low_count) ^ self.chip()
        other = sum((j >> p & 1) << (self.phases - 1 - p) for p in range(self.phases))
        even = lax.axis_index("fsdp") % 2 == 0 if self.low_count == 1 else block % self.low_count % 2 == 0
        return jnp.where(even, j, other)

    def swap_low(self, v, mask):
        return lax.ppermute(v, "fsdp", [(i, i ^ mask) for i in range(self.shards)])

    def swap_slot(self, v, slot):
        def to(i):
            order = self.masks if i % 2 == 0 else self.masks[::-1]
            return i ^ (sum(m for p, m in enumerate(order) if slot >> p & 1) * self.low_count)

        return lax.ppermute(v, "fsdp", [(i, to(i)) for i in range(self.shards)])

    def swap_phase(self, v, phase):
        def to(i):
            mask = self.masks[phase] if i % 2 == 0 else self.masks[self.phases - 1 - phase]
            return i ^ (mask * self.low_count)

        return lax.ppermute(v, "fsdp", [(i, to(i)) for i in range(self.shards)])

    def swap_rep(self, v, mask):
        return lax.ppermute(v, "rep", [(i, i ^ mask) for i in range(self.reps)])


def after(v, *others):
    return lax.optimization_barrier((v, *others))[0]


def whole(shape):
    return pl.BlockSpec(shape, lambda *_: (0,) * len(shape))


class Line:
    def __init__(self):
        self.ahead = []

    def take(self, *arrays):
        found = lax.optimization_barrier((*arrays, *self.ahead))[: len(arrays)]
        self.ahead = [min(found, key=lambda v: v.size)]
        return found

    def hold(self, *arrays):
        self.ahead.extend(arrays)

    def call(self, kernel, name, grid, in_specs, out_specs, out_shape, scratch, args, vmem=40):
        args = list(args)
        if self.ahead:
            args[0] = after(args[0], *self.ahead)
        outs = pl.pallas_call(
            kernel,
            grid=grid,
            in_specs=in_specs,
            out_specs=out_specs,
            out_shape=out_shape,
            scratch_shapes=scratch,
            compiler_params=pltpu.CompilerParams(vmem_limit_bytes=vmem * 2**20),
            cost_estimate=pl.CostEstimate(
                flops=int(COST[name] * FLOPS), bytes_accessed=int(COST[name] * BYTES),
                transcendentals=0,
            ),
            name=name,
        )(*args)
        self.ahead = [min(jax.tree.leaves(outs), key=lambda v: v.size)]
        return outs


def split_kernel(place, source, *outs):
    for j, out in enumerate(outs):
        out[...] = source[place.owner(j)]


def split_tokens(place, v, name):
    seqs, span, width = v.shape
    return place.line.call(
        functools.partial(split_kernel, place),
        name,
        (1,),
        [whole(v.shape)],
        [whole((span, width))] * seqs,
        [jax.ShapeDtypeStruct((span, width), v.dtype)] * seqs,
        [],
        (v,),
        vmem=58,
    )


def weights_kernel(place, w_qkv, w_out, w_up, w_down, *rest):
    vectors, pos, outs = rest[:8], rest[8], rest[9:]
    rows = w_qkv.shape[0]
    parts, low_count = place.parts, place.low_count
    width = w_out.shape[1]
    step = HEADS * HD
    hidden = w_up.shape[1] // parts
    firsts, seconds = outs[:low_count], outs[low_count:]
    for k in range(low_count):

        @pl.when(place.low() == k)
        def _():
            for o in range(low_count):
                for h in range(place.groups):
                    begin = ((k ^ o) * place.groups + h) * step
                    for g in range(3):
                        to = (3 * h + g) * step
                        firsts[o][:, to : to + step] = w_qkv[
                            :, g * width + begin : g * width + begin + step
                        ]
                    to = (3 * place.groups + h) * step
                    firsts[o][:, to : to + step] = w_out[:, begin : begin + step]

    for o in range(low_count):
        lanes = at((place.part() ^ o) * hidden, hidden, 128)
        seconds[o][:rows, :hidden] = w_up[:, lanes]
        seconds[o][:rows, hidden:] = w_down[:, lanes]

    lanes = seconds[0].shape[1]
    lines = []
    for v in vectors:
        lines.append(
            jnp.concatenate([v[...].astype(F32), jnp.zeros((1, lanes - v.shape[1]), F32)], axis=1)
        )
    span = pos.shape[1]
    for values in (
        [(pos[s : s + 1, :] // 64).astype(F32) for s in range(pos.shape[0])],
        [(pos[s : s + 1, :] % 64).astype(F32) for s in range(pos.shape[0])],
    ):
        lines.append(
            jnp.concatenate(values + [jnp.zeros((1, lanes - span * pos.shape[0]), F32)], axis=1)
        )
    lines.append(jnp.zeros((VEC - len(lines), lanes), F32))
    block = jnp.concatenate(lines, axis=0).astype(BF16)
    for o in range(low_count):
        seconds[o][rows:, :] = block


def split_weights(place, w_qkv, w_out, w_up, w_down, vectors, pos):
    rows = w_qkv.shape[0]
    args = [w_qkv, w_out, w_up, w_down] + [v.reshape(1, -1) for v in vectors] + [pos]
    first = (rows, (w_qkv.shape[1] + w_out.shape[1]) // place.low_count)
    second = (rows + VEC, (w_up.shape[1] + w_down.shape[1]) // place.parts)
    shapes = [first] * place.low_count + [second] * place.low_count
    outs = place.line.call(
        functools.partial(weights_kernel, place),
        "split_weights",
        (1,),
        [whole(v.shape) for v in args],
        [whole(s) for s in shapes],
        [jax.ShapeDtypeStruct(s, BF16) for s in shapes],
        [],
        args,
        vmem=58,
    )
    return outs[: place.low_count], outs[place.low_count :]


def second_tables_kernel(place, rows, *rest):
    slots = rest[: place.seqs]
    w_out, vec_out, bias, lines_kept = rest[place.seqs :]
    seqs, low_count, parts = place.seqs, place.low_count, place.parts
    block = rows + VEC
    width = w_out.shape[0]
    step = HEADS * HD
    low = place.low()
    for s in range(seqs):
        owner = place.owner(s)
        for o in range(low_count):
            found = slots[s][o * block : (o + 1) * block, :]
            l = low ^ o
            w_out[at((owner * low_count + l) * rows, rows, 16), :] = found[:rows]
            lines_kept[owner * low_count + l] = found[rows:].astype(F32)

    def line(row, size):
        return jnp.concatenate(
            [lines_kept[n, row : row + 1, :size] for n in range(place.shards)], axis=1
        )

    for row in range(4):
        vec_out[row : row + 1, :] = line(row, rows)
    vec_out[4:5, :] = line(5, rows) + line(7, rows)
    all_up = line(6, 4 * rows)
    all_qkv = line(4, 3 * rows)
    for k in range(parts):

        @pl.when(place.part() == k)
        def _():
            vec_out[5:6, :] = all_up[:, k * width : (k + 1) * width]

    for k in range(low_count):

        @pl.when(low == k)
        def _():
            for h in range(place.groups):
                for g in range(3):
                    begin = g * width + (k * place.groups + h) * step
                    bias[h : h + 1, g * step : (g + 1) * step] = all_qkv[:, begin : begin + step]

    vec_out[6:, :] = jnp.zeros((2, width), F32)


def second_tables(place, slots, rows, width):
    shapes = [
        jax.ShapeDtypeStruct((width, slots[0].shape[1]), BF16),
        jax.ShapeDtypeStruct((8, width), F32),
        jax.ShapeDtypeStruct((8, 3 * HEADS * HD), F32),
        jax.ShapeDtypeStruct((place.shards, VEC, slots[0].shape[1]), F32),
    ]
    return place.line.call(
        functools.partial(second_tables_kernel, place, rows),
        "tables_second",
        (1,),
        [whole(v.shape) for v in slots],
        [whole(v.shape) for v in shapes],
        shapes,
        [],
        slots,
        vmem=16,
    )


def first_tables_kernel(place, rows, span, inverse, lines_kept, *rest):
    slots = rest[: place.seqs]
    w_out, first_out, cos_out, sin_out = rest[place.seqs :]
    low_count = place.low_count
    low, chip = place.low(), place.chip()
    for s in range(place.seqs):
        owner = place.owner(s)
        for o in range(low_count):
            w_out[at((owner * low_count + (low ^ o)) * rows, rows, 16), :] = slots[s][
                o * rows : (o + 1) * rows, :
            ]
    still = jnp.zeros((HD - ROT, span), F32)
    for f in range(place.shards):
        lanes = at(chip * span, span, 128)
        value = lines_kept[f, 8:9, lanes] * 64.0 + lines_kept[f, 9:10, lanes]
        index = f * span + lax.broadcasted_iota(I32, (1, span), 1)
        first_out[:, f * span : (f + 1) * span] = index - value.astype(I32)
        phase = inverse[...] * value
        cosine, sine = jnp.cos(phase), jnp.sin(phase)
        crel, j = (f % low_count) ^ low, place.slot(f)
        to = at(j * span, span, 128)
        cos_out[crel, to, :] = jnp.concatenate([cosine, cosine, still + 1.0] * 2, axis=0).T
        sin_out[crel, to, :] = jnp.concatenate([-sine, sine, still] * 2, axis=0).T


def first_tables(place, slots, lines_kept, rows, width, span):
    inverse = (10000.0 ** (-jnp.arange(0, ROT, 2, dtype=F32) / ROT)).reshape(-1, 1)
    shapes = [
        jax.ShapeDtypeStruct((width, slots[0].shape[1]), BF16),
        jax.ShapeDtypeStruct((1, place.shards * span), I32),
        jax.ShapeDtypeStruct((place.low_count, place.seqs * span, 128), F32),
        jax.ShapeDtypeStruct((place.low_count, place.seqs * span, 128), F32),
    ]
    args = [inverse, lines_kept] + slots
    return place.line.call(
        functools.partial(first_tables_kernel, place, rows, span),
        "tables_first",
        (1,),
        [whole(v.shape) for v in args],
        [whole(v.shape) for v in shapes],
        shapes,
        [],
        args,
        vmem=16,
    )


def piece_specs(pieces, lines):
    split = pieces[0].shape[0] // lines

    def spec(i, width):
        return pl.BlockSpec(
            (lines, width), lambda g: (jnp.clip(g - i * split, 0, split - 1), 0)
        )

    return [spec(i, v.shape[1]) for i, v in enumerate(pieces)]


def piece_now(refs, steps):
    found = refs[0][...]
    for i in range(1, len(refs)):
        found = jnp.where(pl.program_id(0) >= i * (steps // len(refs)), refs[i][...], found)
    return found


def norm(source):
    source = source.astype(F32)
    centred = source - jnp.mean(source, axis=1, keepdims=True)
    return centred * lax.rsqrt(jnp.mean(centred * centred, axis=1, keepdims=True) + EPS)


def turned(v):
    half = ROT // 2
    columns = v.shape[1]
    lane = lax.broadcasted_iota(I32, v.shape, 1) % HD
    ahead = pltpu.roll(v, columns - half, 1)
    behind = pltpu.roll(v, half, 1)
    return jnp.where(lane < half, ahead, behind)


def front_kernel(place, steps, *refs):
    tokens, refs = refs[: place.low_count], refs[place.low_count :]
    weight, vec, bias, cosine, sine, one_out, *outs = refs
    step = HEADS * HD
    one = (norm(piece_now(tokens, steps)) * vec[0:1, :] + vec[1:2, :]).astype(BF16)
    one_out[0] = one
    copies = 2 * step // 128
    cos_cols = jnp.concatenate([cosine[0]] * copies, axis=1)
    sin_cols = jnp.concatenate([sine[0]] * copies, axis=1)
    for h in range(place.groups):
        q_out, k_out, v_out = outs[3 * h : 3 * h + 3]
        qkv = dot(one, weight[:, 3 * step * h : 3 * step * (h + 1)], NN) + bias[h : h + 1, :]
        both = qkv[:, : 2 * step]
        both = both * cos_cols + turned(both) * sin_cols
        q_out[0] = both[:, :step].astype(BF16)
        k_out[0] = both[:, step:].astype(BF16)
        v_out[0] = qkv[:, 2 * step :].astype(BF16)


def front(place, tokens, weight, vec, bias, cosine, sine):
    groups = len(tokens)
    count, width = tokens[0].shape
    step = HEADS * HD
    split = 2
    lines = count // split
    by_step = lambda cols: pl.BlockSpec((1, lines, cols), lambda g: (g // split, g % split, 0))
    shaped = lambda cols: jax.ShapeDtypeStruct((groups, count, cols), BF16)
    outs = place.line.call(
        functools.partial(front_kernel, place, groups * split),
        "front",
        (groups * split,),
        piece_specs(tokens, lines)
        + [whole(weight.shape), whole(vec.shape), whole(bias.shape)] + [by_step(128)] * 2,
        [by_step(width)] + [by_step(step)] * (3 * place.groups),
        [shaped(width)] + [shaped(step)] * (3 * place.groups),
        [],
        [*tokens, weight, vec, bias, cosine, sine],
        vmem=24,
    )
    return outs[0], [outs[1 + 3 * h : 4 + 3 * h] for h in range(place.groups)]


def middle_kernel(count, steps, *refs):
    tokens, grads, refs = refs[:count], refs[count : 2 * count], refs[2 * count :]
    vec, weight, two_out, normed_out, hidden_out, grad_out, sums = refs

    @pl.when(pl.program_id(0) == 0)
    def _():
        sums[...] = jnp.zeros_like(sums)

    width = weight.shape[0]
    normed = norm(piece_now(tokens, steps))
    normed_out[0] = normed.astype(BF16)
    two = (normed * vec[2:3, :] + vec[3:4, :]).astype(BF16)
    two_out[0] = two
    up = dot(two, weight[:, :width], NN) + vec[5:6, :]
    grad = piece_now(grads, steps)
    grad_hidden = dot(grad, weight[:, width:], NN)
    bell = jnp.exp(-0.5 * up * up)
    below = 1.0 + (0.3275911 * 0.5**0.5) * jnp.abs(up)
    t = pl.reciprocal(below, approx=True)
    t = t * (2.0 - below * t)
    series = t * (
        0.127414796 + t * (-0.142248368 + t * (0.7107068705 + t * (-0.7265760135 + t * 0.5307027145)))
    )
    tail = series * bell
    share = jnp.where(up >= 0.0, 1.0 - tail, tail)
    hidden_out[0] = (up * share).astype(BF16)
    slope = share + up * (bell * 0.3989422804014327)
    grad_up = (grad_hidden * slope).astype(BF16)
    grad_out[0] = grad_up
    sums[0:1, :] += jnp.sum(grad_up.astype(F32), axis=0, keepdims=True)
    sums[1:2, :] += jnp.sum(grad.astype(F32), axis=0, keepdims=True)


def middle(place, z, tokens, grads, vec, weight):
    groups = len(tokens)
    count, width = tokens[0].shape
    split = 2
    lines = count // split
    by_step = pl.BlockSpec((1, lines, width), lambda g: (g // split, g % split, 0))
    return place.line.call(
        functools.partial(middle_kernel, groups, groups * split),
        f"middle_{z}",
        (groups * split,),
        piece_specs(tokens, lines)
        + piece_specs(grads, lines)
        + [whole(vec.shape), whole(weight.shape)],
        [by_step] * 4 + [whole((8, width))],
        [jax.ShapeDtypeStruct((groups, count, width), BF16)] * 4 + [jax.ShapeDtypeStruct((8, width), F32)],
        [],
        [*tokens, *grads, vec, weight],
        vmem=24,
    )


def attention_kernel(
    place, group, span, q_in, k_in, v_in, w_in, first_in, cos_in, sin_in, *refs
):
    cot_in, refs = refs[: place.low_count], refs[place.low_count :]
    o_out, g_out, sums, qs, ks, vs, gs, o_turned, gq_turned, gk_sum, gv_sum = refs
    low_count = place.low_count
    count, columns = q_in.shape[1:]
    heads = columns // HD
    length = low_count * count
    begin = (3 * place.groups + group) * columns
    w_out = w_in[:, begin : begin + columns]

    def slot(f):
        crel = (f % low_count) ^ place.low()
        j = place.slot(f)
        return crel, at(j * span, span, 128)

    for f in range(length // span):
        to = slice(f * span, (f + 1) * span)
        crel, lines = slot(f)
        for source, kept in ((q_in, qs), (k_in, ks), (v_in, vs)):
            found = source[crel, lines, :]
            for h in range(heads):
                kept[h, to, :] = found[:, h * HD : (h + 1) * HD]
        cot = cot_in[0][lines, :]
        for o in range(1, low_count):
            cot = jnp.where(crel == o, cot_in[o][lines, :], cot)
        found = dot(cot, w_out, NN).astype(BF16)
        for h in range(heads):
            gs[h, to, :] = found[:, h * HD : (h + 1) * HD]

    def one_head(h, carry):
        keys = ks[h]
        values = vs[h]
        keys_turned = keys.astype(F32).T.astype(BF16)
        values_turned = values.astype(F32).T.astype(BF16)
        for i in range(length // TILE):
            seen = (i + 1) * TILE
            here = slice(i * TILE, seen)
            query = qs[h, here, :]
            grad = gs[h, here, :]
            first = first_in[:, here]
            raw = dot(keys[:seen], query, NT) * 0.125
            key_index = lax.broadcasted_iota(I32, (seen, TILE), 0)
            query_index = i * TILE + lax.broadcasted_iota(I32, (seen, TILE), 1)
            raw = jnp.where((key_index >= first) & (key_index <= query_index), raw, NEG)
            weights = jnp.exp(raw - jnp.max(raw, axis=0, keepdims=True))
            probs = weights * (1.0 / jnp.sum(weights, axis=0, keepdims=True))
            grad_probs = dot(values[:seen], grad, NT)
            carried = jnp.sum(probs * grad_probs, axis=0, keepdims=True)
            grad_scores = (probs * (grad_probs - carried)).astype(BF16)
            low = probs.astype(BF16)
            o_turned[h, :, here] = dot(values_turned[:, :seen], low, NN)
            gq_turned[h, :, here] = dot(keys_turned[:, :seen], grad_scores, NN)
            gk_part = dot(grad_scores, query, NN)
            gv_part = dot(low, grad, NN)
            if i > 0:
                old = slice(0, i * TILE)
                gk_sum[h, old, :] += gk_part[: i * TILE]
                gv_sum[h, old, :] += gv_part[: i * TILE]
            gk_sum[h, here, :] = gk_part[i * TILE :]
            gv_sum[h, here, :] = gv_part[i * TILE :]
        return carry

    lax.fori_loop(0, heads, one_head, 0)
    total = jnp.zeros((1, 3 * columns), F32)
    for f in range(length // span):
        crel, lines = slot(f)
        to = slice(f * span, (f + 1) * span)
        o_out[crel, lines, :] = jnp.concatenate(
            [o_turned[h, :, to].T for h in range(heads)], axis=1
        ).astype(BF16)
        both = jnp.concatenate(
            [gq_turned[h, :, to].T for h in range(heads)] + [gk_sum[h, to, :] for h in range(heads)],
            axis=1,
        )
        both = both * 0.125
        copies = 2 * columns // 128
        cos_cols = jnp.concatenate([cos_in[crel, lines, :]] * copies, axis=1)
        sin_cols = jnp.concatenate([sin_in[crel, lines, :]] * copies, axis=1)
        both = both * cos_cols - turned(both) * sin_cols
        value = jnp.concatenate([gv_sum[h, to, :] for h in range(heads)], axis=1)
        grad = jnp.concatenate([both, value], axis=1).astype(BF16)
        g_out[crel, lines, :] = grad
        total = total + jnp.sum(grad.astype(F32), axis=0, keepdims=True)
    sums[...] = jnp.concatenate([total, jnp.zeros((7, 3 * columns), F32)], axis=0)


def attention(place, group, span, q, k, v, cot, w, first, cosine, sine):
    count, columns = q.shape[1:]
    low_count = place.low_count
    heads = columns // HD
    length = low_count * count
    outs = [
        jax.ShapeDtypeStruct((low_count, count, columns), BF16),
        jax.ShapeDtypeStruct((low_count, count, 3 * columns), BF16),
        jax.ShapeDtypeStruct((8, 3 * columns), F32),
    ]
    args = [q, k, v, w, first, cosine, sine, *cot]
    return place.line.call(
        functools.partial(attention_kernel, place, group, span),
        f"attention_{group}",
        (1,),
        [whole(a.shape) for a in args],
        [whole(a.shape) for a in outs],
        outs,
        [pltpu.VMEM((heads, length, HD), BF16)] * 4
        + [pltpu.VMEM((heads, HD, length), F32)] * 2
        + [pltpu.VMEM((heads, length, HD), F32)] * 2,
        args,
    )


def back_kernel(place, groups, *refs):
    normed, hidden, grad_up = refs[:3]
    attended, grad_qkv = refs[3 : 3 + groups], refs[3 + groups : 3 + 2 * groups]
    vec, second = refs[3 + 2 * groups : 5 + 2 * groups]
    keep, send, sums = refs[-3:]
    step = pl.program_id(0)
    width = normed.shape[2]

    @pl.when(step == 0)
    def _():
        sums[...] = jnp.zeros_like(sums)

    two = dot(grad_up[0], second[:, :width], NT)
    out = dot(hidden[0], second[:, width:], NT)
    both = two * vec[2:3, :]
    source = normed[0].astype(F32)
    sums[2:3, :] += jnp.sum(two * source, axis=0, keepdims=True)
    sums[3:4, :] += jnp.sum(two, axis=0, keepdims=True)
    if groups:
        first = refs[5 + 2 * groups]
        cols = HEADS * HD
        one = None
        for h in range(groups):
            term = dot(grad_qkv[h][0], first[:, 3 * cols * h : 3 * cols * (h + 1)], NT)
            one = term if one is None else one + term
            begin = (3 * groups + h) * cols
            out = out + dot(attended[h][0], first[:, begin : begin + cols], NT)
        both = both + one * vec[0:1, :]
        sums[0:1, :] += jnp.sum(one * source, axis=0, keepdims=True)
        sums[1:2, :] += jnp.sum(one, axis=0, keepdims=True)
    split = pl.num_programs(0) // place.low_count

    @pl.when(step < split)
    def _():
        keep[0] = out.astype(BF16)
        keep[1] = both.astype(BF16)

    @pl.when(step >= split)
    def _():
        send[0, 0] = out.astype(BF16)
        send[0, 1] = both.astype(BF16)


def back(place, z, normed, hidden, grad_up, attended, grad_qkv, vec, second, first):
    low_count = place.low_count
    groups, count, width = normed.shape
    split = 2
    lines = count // split
    by_step = lambda cols: pl.BlockSpec((1, lines, cols), lambda g: (g // split, g % split, 0))
    args = [normed, hidden, grad_up, *attended, *grad_qkv]
    fixed = [vec, second] + ([first] if attended else [])

    def sent(g):
        later = jnp.maximum(g - split, 0)
        return (later // split, 0, later % split, 0)

    return place.line.call(
        functools.partial(back_kernel, place, len(attended)),
        f"back_{z}",
        (groups * split,),
        [by_step(v.shape[2]) for v in args] + [whole(v.shape) for v in fixed],
        [
            pl.BlockSpec((2, lines, width), lambda g: (0, jnp.minimum(g, split - 1), 0)),
            pl.BlockSpec((1, 2, lines, width), sent),
            whole((8, width)),
        ],
        [
            jax.ShapeDtypeStruct((2, count, width), BF16),
            jax.ShapeDtypeStruct((low_count - 1, 2, count, width), BF16),
            jax.ShapeDtypeStruct((8, width), F32),
        ],
        [],
        args + fixed,
        vmem=32,
    )


def store_rows(place, rows, block, value, scratch, columns):
    low_count = place.low_count
    for s in range(place.seqs):
        owner = place.owner(s)
        for o in range(low_count):
            begin = owner * (low_count * rows) + (place.low() ^ o) * rows
            scratch[s, o * block : o * block + rows, columns] = value[at(begin, rows, 16), :].astype(BF16)


def product(lefts, rights):
    each = len(lefts) // len(rights)
    total = None
    for i, left in enumerate(lefts):
        lines = left.shape[0]
        right = rights[i // each][(i % each) * lines : (i % each + 1) * lines, :]
        term = dot(left[...], right, TN)
        total = term if total is None else total + term
    return total


def second_grads_kernel(place, rows, count, *refs):
    two, grad_up, hidden = [refs[k * count : (k + 1) * count] for k in range(3)]
    cot, (keep, send, total, turned_rows) = refs[3 * count : -4], refs[-4:]
    step = pl.program_id(0)
    width = two[0].shape[1]
    half = place.seqs // 2

    def one(left, right, columns):
        total[...] = product(left, right)
        store_rows(place, rows, rows, total, turned_rows, columns)

    @pl.when(step == 0)
    def _():
        one(two, grad_up, slice(0, width))

    @pl.when(step == 1)
    def _():
        one(cot, hidden, slice(width, 2 * width))
        keep[...] = turned_rows[:half]
        send[...] = turned_rows[half:]


def second_grads(place, rows, two, grad_up, cot, hidden):
    width = two[0].shape[2]
    flat = [v.reshape(-1, width) for v in (*two, *grad_up, *hidden)] + [p for c in cot for p in c]
    half = (place.seqs // 2, place.low_count * rows, 2 * width)
    return place.line.call(
        functools.partial(second_grads_kernel, place, rows, len(two)),
        "second_grads",
        (2,),
        [whole(v.shape) for v in flat],
        [whole(half)] * 2,
        [jax.ShapeDtypeStruct(half, BF16)] * 2,
        [pltpu.VMEM((width, width), F32), pltpu.VMEM((2 * half[0],) + half[1:], BF16)],
        flat,
    )


def first_grads_kernel(place, rows, last, *refs):
    one, grad_qkv, attended = refs[:3]
    cot, refs = refs[3 : 3 + place.low_count], (None,) * 4 + refs[3 + place.low_count :]
    keep, send, total, turned_rows = refs[-4:]
    seqs, low_count, parts = place.seqs, place.low_count, place.parts
    width = one.shape[1]
    step = HEADS * HD
    block = rows + (VEC if last else 0)
    half = seqs // 2
    total[:, : 3 * step] = dot(one[...], grad_qkv[...], TN)
    total[:, 3 * step :] = product(cot, [attended])
    store_rows(place, rows, block, total, turned_rows, slice(0, width))
    if last:
        at_qkv = 4 + place.groups
        sums_qkv, sums_back, sums_middle = (
            refs[4:at_qkv],
            refs[at_qkv : at_qkv + place.pair],
            refs[at_qkv + place.pair : -4],
        )
        back = sum(s[...] for s in sums_back)
        up = sum(s[0:1, :] for s in sums_middle)
        grad = sums_middle[0][1:2, :] * (1.0 / low_count)
        zero = jnp.zeros((1, step), F32)
        all_qkv = jnp.concatenate(
            [
                jnp.where(place.low() == k, sums_qkv[h][0:1, g * step : (g + 1) * step], zero)
                for g in range(3)
                for k in range(low_count)
                for h in range(place.groups)
            ],
            axis=1,
        )
        all_up = jnp.concatenate(
            [jnp.where(place.part() == k, up, 0.0) for k in range(parts)], axis=1
        )
        lines = [(back[r : r + 1], rows) for r in range(4)]
        lines += [(all_qkv, 3 * rows), (grad, rows), (all_up, 4 * rows)]
        for i in range(seqs):
            for l in range(low_count):
                n = i * low_count + l
                made = [
                    jnp.concatenate(
                        [v[:, n * size : (n + 1) * size], jnp.zeros((1, width - size), F32)], axis=1
                    )
                    for v, size in lines
                ]
                made.append(jnp.zeros((VEC - len(made), width), F32))
                made = jnp.concatenate(made, axis=0).astype(BF16)
                for s in range(seqs):
                    for o in range(low_count):

                        @pl.when((place.owner(s) == i) & ((place.low() ^ o) == l))
                        def _():
                            turned_rows[s, o * block + rows : (o + 1) * block, :] = made

    keep[...] = turned_rows[:half]
    send[...] = turned_rows[half:]


def first_grads(place, group, rows, one, cot, grad_qkv, attended, sums):
    width = one.shape[2]
    args = [v.reshape(-1, v.shape[2]) for v in (one, grad_qkv, attended)] + list(cot) + list(sums)
    half = (place.seqs // 2, place.low_count * (rows + (VEC if sums else 0)), width)
    return place.line.call(
        functools.partial(first_grads_kernel, place, rows, bool(sums)),
        f"first_grads_{group}",
        (1,),
        [whole(v.shape) for v in args],
        [whole(half)] * 2,
        [jax.ShapeDtypeStruct(half, BF16)] * 2,
        [pltpu.VMEM((width, width), F32), pltpu.VMEM((2 * half[0],) + half[1:], BF16)],
        args,
    )


def tokens_kernel(place, source, cot, vec, *rest):
    blocks, (out, grad_in) = rest[: place.seqs], rest[place.seqs :]
    for j in range(place.seqs):
        s = place.owner(j)
        x = source[s].astype(F32)
        out[s] = (x + blocks[j][0].astype(F32) + vec[4:5, :]).astype(BF16)
        mean = jnp.mean(x, axis=1, keepdims=True)
        centred = x - mean
        scale = lax.rsqrt(jnp.mean(centred * centred, axis=1, keepdims=True) + EPS)
        normed = centred * scale
        e = blocks[j][1].astype(F32)
        pulled = (
            e
            - jnp.mean(e, axis=1, keepdims=True)
            - normed * jnp.mean(e * normed, axis=1, keepdims=True)
        ) * scale
        grad_in[s] = (cot[s].astype(F32) + pulled).astype(BF16)


def finish_tokens(place, source, cot, vec, blocks):
    return place.line.call(
        functools.partial(tokens_kernel, place),
        "finish_tokens",
        (1,),
        [whole(source.shape)] * 2 + [whole(vec.shape)] + [whole(b.shape) for b in blocks],
        [whole(source.shape)] * 2,
        [jax.ShapeDtypeStruct(source.shape, BF16)] * 2,
        [],
        [source, cot, vec] + blocks,
    )


def first_end_kernel(place, rows, *refs):
    w_qkv, w_out, lines = refs[-3:]
    low_count, groups = place.low_count, place.groups
    width = w_out.shape[1]
    step = HEADS * HD
    found = refs[:-3]
    even = (lax.axis_index("rep") % 2) == 0
    count = len(found) // groups
    total = None
    for h in range(groups):
        ours = found[h * count : (h + 1) * count]
        for o in range(low_count):
            if count == 1:
                piece = ours[0][o].astype(F32)
            else:
                mine, other = ours[0][o].astype(F32), ours[1][o].astype(F32)
                piece = jnp.concatenate(
                    [jnp.where(even, mine, other), jnp.where(even, other, mine)], axis=1
                )
            for k in range(low_count):

                @pl.when(place.low() == k)
                def _():
                    begin = ((k ^ o) * groups + h) * step
                    for g in range(3):
                        to = g * width + begin
                        w_qkv[:, to : to + step] = piece[:rows, g * step : (g + 1) * step]
                    w_out[:, begin : begin + step] = piece[:rows, 3 * step :]

            if h == groups - 1:
                total = piece[rows:] if total is None else total + piece[rows:]
    lines[...] = total


def first_end(place, rows, width, pieces):
    return place.line.call(
        functools.partial(first_end_kernel, place, rows),
        "first_end",
        (1,),
        [whole(p.shape) for p in pieces],
        [whole((rows, 3 * width)), whole((rows, width)), whole((VEC, width))],
        [
            jax.ShapeDtypeStruct((rows, 3 * width), F32),
            jax.ShapeDtypeStruct((rows, width), F32),
            jax.ShapeDtypeStruct((VEC, width), F32),
        ],
        [],
        pieces,
    )


def second_end_kernel(place, *refs):
    pieces = refs[: place.parts]
    w_up, w_down = refs[place.parts :]
    parts = place.parts
    step = w_up.shape[1] // parts
    for r in range(parts):
        t = place.part() ^ r
        w_up[:, at(t * step, step, 128)] = pieces[r][:, :step].astype(F32)
        w_down[:, at(t * step, step, 128)] = pieces[r][:, step:].astype(F32)


def second_end(place, pieces):
    rows, columns = pieces[0].shape
    shape = (rows, columns // 2 * place.parts)
    return place.line.call(
        functools.partial(second_end_kernel, place),
        "second_end",
        (1,),
        [whole(p.shape) for p in pieces],
        [whole(shape)] * 2,
        [jax.ShapeDtypeStruct(shape, F32)] * 2,
        [],
        pieces,
    )


def add(a, b):
    return (a.astype(F32) + b.astype(F32)).astype(BF16)


def on_device(
    layer_input,
    positions,
    cotangent,
    w_qkv,
    w_out,
    w_up,
    w_down,
    ln1_gain,
    ln1_bias,
    ln2_gain,
    ln2_bias,
    qkv_bias,
    out_bias,
    up_bias,
    down_bias,
):
    seqs, span, width = layer_input.shape
    place = Place(seqs, lax.axis_size("fsdp"), lax.axis_size("rep"))
    low_count, pair = place.low_count, place.pair
    rows = w_qkv.shape[0]

    line = place.line
    lows = range(1, low_count)

    def to_low(v):
        return [place.swap_low(v, o) for o in lows]

    class Gather:
        def __init__(self, block):
            self.slots = [block]
            self.coming = [[place.swap_phase(block, p)] for p in range(place.phases)]

        def step(self, more=0):
            count = len(self.coming[0])
            ahead = self.coming[1][:more] if more else []
            got = line.take(*self.coming.pop(0), *ahead)
            if more:
                self.coming[0][:more] = got[count:]
            for later, p in zip(self.coming, range(place.phases - len(self.coming), place.phases)):
                later.extend(place.swap_phase(v, p) for v in got[:count])
            self.slots.extend(got[:count])

    class Scatter:
        def __init__(self, keep, send):
            self.phase = place.phases - 1
            self.kept = [keep[s] for s in range(keep.shape[0])]
            self.got = place.swap_phase(send, self.phase)

        def step(self):
            got = line.take(self.got)[0]
            self.phase -= 1
            half = len(self.kept) // 2
            sums = [add(v, got[s]) for s, v in enumerate(self.kept)]
            if self.phase >= 0:
                self.kept = sums[:half]
                sent = sums[half] if half == 1 else jnp.stack(sums[half:])
                line.hold(sent)
                got = place.swap_phase(sent, self.phase)
                self.got = got[None] if half == 1 else got
            else:
                block = sums[0].reshape(low_count, sums[0].shape[0] // low_count, -1)
                self.kept = [block[0]]
                line.hold(sums[0])
                self.got = [place.swap_low(block[o], o) for o in lows]

        def end(self):
            return jnp.stack(self.kept + list(line.take(*self.got)))

    masks = [m for m in (1, 2, 4, 8, 16) if m < place.reps]
    even = lax.axis_index("rep") % 2 == 0

    class Reps:
        def __init__(self, mine):
            columns = mine.shape[2] // 2
            low_half, high_half = mine[..., :columns], mine[..., columns:]
            self.held = jnp.where(even, low_half, high_half)
            sent = jnp.where(even, high_half, low_half)
            line.hold(sent)
            self.masks = masks[1:]
            self.got = place.swap_rep(sent, 1)

        def step(self):
            self.held = add(self.held, line.take(self.got)[0])
            line.hold(self.held)
            self.got = place.swap_rep(self.held, self.masks.pop(0) if self.masks else 1)

        def end(self):
            return [self.held, line.take(self.got)[0]]

    class Pairs:
        def __init__(self, mine):
            self.mine = mine
            self.masks = masks[1:] + masks[:1]
            self.got = place.swap_rep(mine, self.masks.pop(0))

        def step(self):
            self.mine = add(self.mine, line.take(self.got)[0])
            line.hold(self.mine)
            self.got = place.swap_rep(self.mine, self.masks.pop(0))

        def end(self):
            return self.mine, line.take(self.got)[0]

    split_x = split_tokens(place, layer_input, "split_input")
    coming = [place.swap_slot(split_x[j], j) for j in range(1, seqs)]
    if pair == 2:
        coming.append(place.swap_rep(split_x[0], 1))
    split_c = split_tokens(place, cotangent, "split_cotangent")
    vectors = (ln1_gain, ln1_bias, ln2_gain, ln2_bias, qkv_bias, out_bias, up_bias, down_bias)
    firsts, seconds = split_weights(place, w_qkv, w_out, w_up, w_down, vectors, positions)
    coming_second = [place.swap_low(seconds[o], o) for o in lows]
    coming = line.take(*coming)
    block_x = jnp.concatenate([split_x[0], *coming[: seqs - 1]], axis=0)
    tokens, grads = [[block_x]], []
    coming_x = to_low(block_x)
    if pair == 2:
        rest = jnp.concatenate(coming[: seqs - 1], axis=0)
        line.hold(rest)
        later_x = place.swap_rep(rest, 1)
    coming_second = line.take(*coming_second)
    block_second = jnp.concatenate([seconds[0], *coming_second], axis=0)
    line.hold(block_x, block_second)
    sent = line.take(*split_c[1:])
    coming_c = [place.swap_slot(v, j) for v, j in zip(sent, range(1, seqs))]
    tokens[0].extend(line.take(*coming_x))
    coming_c = line.take(*coming_c)
    block_c = jnp.concatenate([split_c[0], *coming_c], axis=0)
    line.hold(block_c)
    second = Gather(line.take(block_second)[0])
    grads.append([block_c])
    coming_c = to_low(block_c)
    if pair == 2:
        later_x = line.take(later_x)[0]
        other_x = jnp.concatenate([coming[seqs - 1], later_x], axis=0)
        line.hold(other_x)
        coming_x = to_low(other_x)
        other_c = place.swap_rep(after(block_c, later_x), 1)
    grads[0].extend(line.take(*coming_c))
    second.step()
    if pair == 2:
        tokens.append([other_x, *line.take(*coming_x)])
    coming_first = [place.swap_low(v, o) for v, o in zip(line.take(*firsts[1:]), lows)]
    coming_first = line.take(*coming_first)
    block_first = jnp.concatenate([firsts[0], *coming_first], axis=0)
    line.hold(block_first)
    second.step()
    first = Gather(after(block_first, *second.slots))
    if pair == 2:
        other_c = line.take(other_c)[0]
        coming_c = to_low(other_c)

    w_second, vec, bias, lines_kept = second_tables(place, second.slots, rows, width)
    two, normed, hidden, grad_up, sums_middle, sums_back = [[None] * pair for _ in range(6)]

    def forward(z):
        two[z], normed[z], hidden[z], grad_up[z], sums_middle[z] = middle(
            place, z, tokens[z], grads[z], vec, w_second
        )

    def backward(z, attended, grad_qkv, w_first):
        keep, send, sums_back[z] = back(
            place, z, normed[z], hidden[z], grad_up[z], attended, grad_qkv, vec, w_second, w_first
        )
        return keep, [place.swap_low(send[o - 1], o) for o in lows]

    def low_sum(keep, coming):
        total = keep.astype(F32)
        for v in line.take(*coming):
            total = total + v.astype(F32)
        return total

    if pair == 2:
        grads.append([other_c, *line.take(*coming_c)])
        forward(1)
        keep, coming = backward(1, [], [], None)
    first.step(more=1)
    forward(0)
    out_pieces, out_found = [], []

    def next_piece():
        if out_pieces:
            out_found.append(line.take(out_coming.pop())[0])
            out_pieces.pop(0)
        if out_pieces:
            out_coming.append(place.swap_rep(after(out_pieces[0], out_found[-1]), 1))

    out_coming = []
    if pair == 2:
        out_other = low_sum(keep, coming).astype(BF16).reshape(2 * seqs, span, width)
        cuts = [2 * seqs * k // 8 for k in (0, 3, 6, 8)]
        out_pieces = [out_other[a:b] for a, b in zip(cuts, cuts[1:])]
        line.hold(*out_pieces)
        out_coming.append(place.swap_rep(out_pieces[0], 1))
    second_sums = Scatter(*second_grads(place, rows, two, grad_up, grads, hidden))

    first.step()
    w_first, seen, cosine, sine = first_tables(place, first.slots, lines_kept, rows, width, span)
    one, heads = front(place, tokens[0], w_first, vec, bias, cosine, sine)
    attended, grad_qkv, sums_qkv, first_sums = [[None] * place.groups for _ in range(4)]
    cot = grads[0]
    for h in range(place.groups):
        next_piece()
        attended[h], grad_qkv[h], sums_qkv[h] = attention(
            place, h, span, *heads[h], cot, w_first, seen, cosine, sine
        )
        second_sums.step()
        if h > 0:
            first_sums[h - 1].step()
        if h < place.groups - 1:
            first_sums[h] = Scatter(
                *first_grads(place, h, rows, one, cot, grad_qkv[h], attended[h], [])
            )
    while second_sums.phase >= 0:
        second_sums.step()
    second_mine = second_sums.end()
    line.hold(second_mine)
    while out_pieces:
        next_piece()
    second_reps = Pairs(second_mine[0]) if pair == 2 else Reps(second_mine)
    keep, coming = backward(0, attended, grad_qkv, w_first)
    if place.groups > 1:
        first_sums[0].step()
    h = place.groups - 1
    first_sums[h] = Scatter(
        *first_grads(
            place, h, rows, one, cot, grad_qkv[h], attended[h], sums_qkv + sums_back + sums_middle
        )
    )

    reps = []
    for h in range(place.groups - 1):
        mine = first_sums[h].end()
        line.hold(mine)
        reps.append(Reps(mine))
    if pair == 2:
        more_reps = []
        for o in lows:
            (more_reps or [second_reps])[-1].step()
            more_reps.append(Pairs(after(second_mine[o], *line.ahead)))
    last = first_sums[-1]
    last.step()
    for r in reps:
        r.step()
    out_sum = low_sum(keep, coming)
    if pair == 2:
        out_sum = out_sum + jnp.concatenate(out_found).reshape(out_sum.shape).astype(F32)
    out_sum = out_sum.astype(BF16).reshape(2, seqs, span, width)
    line.hold(out_sum)
    blocks = [out_sum[:, s] for s in range(seqs)]

    def pass_on(phase):
        chosen = [s for s in range(seqs) if s >> phase & 1]
        got = place.swap_phase(jnp.stack([blocks[s] for s in chosen]), phase)
        return chosen, got

    chosen, got = pass_on(0)
    last.step()
    mine = last.end()
    line.hold(mine)
    reps.append(Reps(mine))
    for phase in range(1, place.phases + 1):
        got = line.take(got)[0]
        for k, s in enumerate(chosen):
            blocks[s] = got[k]
        if phase < place.phases:
            chosen, got = pass_on(phase)
    if pair == 2:
        more_reps[-1].step()
    else:
        while second_reps.masks:
            second_reps.step()
        second_reps.step()
    for r in reps:
        while r.masks:
            r.step()
    for r in reps:
        r.step()
    output, grad_input = finish_tokens(place, layer_input, cotangent, vec, blocks)
    if pair == 2:
        ends = [second_reps.end()] + [r.end() for r in more_reps]
        pieces = [e[0] for e in ends] + [e[1] for e in ends]
    else:
        pieces = second_reps.end()
        pieces = jnp.where(even, pieces[0], pieces[1]), jnp.where(even, pieces[1], pieces[0])
        pieces = list(jnp.concatenate(pieces, axis=2))
    grad_w_up, grad_w_down = second_end(place, pieces)
    pieces = [p for r in reps for p in r.end()]
    grad_w_qkv, grad_w_out, lines = first_end(place, rows, width, pieces)
    ln1_gain_g, ln1_bias_g, ln2_gain_g, ln2_bias_g = [lines[r, :rows] for r in range(4)]
    qkv_g = lines[4, : 3 * rows]
    out_g = lines[5, :rows]
    up_g = lines[6, : 4 * rows]
    return (
        output,
        grad_input,
        grad_w_qkv,
        grad_w_out,
        grad_w_up,
        grad_w_down,
        ln1_gain_g,
        ln1_bias_g,
        ln2_gain_g,
        ln2_bias_g,
        qkv_g,
        out_g,
        up_g,
        out_g,
    )


def solution(mesh):
    tokens = P("rep", "fsdp", None)
    matrix = P("fsdp", None)
    vector = P("fsdp")
    return jax.shard_map(
        on_device,
        mesh=mesh,
        in_specs=(tokens, P("rep", "fsdp"), tokens) + (matrix,) * 4 + (vector,) * 8,
        out_specs=(tokens, tokens) + (matrix,) * 4 + (vector,) * 8,
        check_vma=False,
    )
```

```python
import functools

import jax
import jax.numpy as jnp
from jax import lax
from jax.experimental import pallas as pl
from jax.experimental.pallas import tpu as pltpu
from jax.sharding import PartitionSpec as P

H = 12
HD = 64
ROT = 16
TILE = 256
VEC = 16
COSTS = {
    "tables_second": 0.1,
    "middle_1": 0.1,
    "back_1": 0.1,
    "second_grads": 0.1,
    "back_0": 2,
    "vector_grads": 10,
    "second_end": 0.3,
    "pause_7": 0.3,
    "pause_8": 0.3,
    "pause_9": 0.3,
    "pause_10": 0.3,
    "pause_11": 0.3,
    "pause_12": 0.3,
    "pause_13": 0.3,
    "tables_first": 0.1,
    "front": 0.1,
}
DEFAULT = 20

EPS = 1e-05
NEG = -1e30

F32 = jnp.float32
BF16 = jnp.bfloat16
I32 = jnp.int32

NN = ((1,), (0,))
NT = ((1,), (1,))
TN = ((0,), (0,))


def dot(a, b, dims):
    return lax.dot_general(a, b, (dims, ((), ())), preferred_element_type=F32)


def at(start, size, multiple):
    return pl.ds(pl.multiple_of(start, multiple), size)


class Place:
    def __init__(self, seqs, shards, reps):
        self.seqs, self.shards, self.reps = seqs, shards, reps
        self.low_count = shards // seqs
        self.pair = 2 if reps % 2 == 0 and H % (2 * self.low_count) == 0 else 1
        self.parts = self.pair * self.low_count
        self.line = Line()
        self.heads = 2 if H // self.low_count % 2 == 0 else 3
        self.groups = H // self.low_count // self.heads
        self.masks = []
        while 2 ** len(self.masks) < seqs:
            self.masks.append(2 ** len(self.masks))
        self.phases = len(self.masks)

    def chip(self):
        return lax.axis_index("fsdp") // self.low_count

    def low(self):
        return lax.axis_index("fsdp") % self.low_count

    def part(self):
        return (lax.axis_index("rep") % self.pair) * self.low_count + self.low()

    def owner(self, slot):
        even = sum(self.masks[p] for p in range(self.phases) if slot >> p & 1)
        odd = sum(self.masks[self.phases - 1 - p] for p in range(self.phases) if slot >> p & 1)
        if even == odd:
            return self.chip() ^ even
        return self.chip() ^ jnp.where(lax.axis_index("fsdp") % 2 == 0, even, odd)

    def slot(self, block):
        j = (block // self.low_count) ^ self.chip()
        other = sum((j >> p & 1) << (self.phases - 1 - p) for p in range(self.phases))
        even = lax.axis_index("fsdp") % 2 == 0 if self.low_count == 1 else block % self.low_count % 2 == 0
        return jnp.where(even, j, other)

    def swap_low(self, v, mask):
        return lax.ppermute(v, "fsdp", [(i, i ^ mask) for i in range(self.shards)])

    def swap_slot(self, v, slot):
        def to(i):
            order = self.masks if i % 2 == 0 else self.masks[::-1]
            return i ^ (sum(m for p, m in enumerate(order) if slot >> p & 1) * self.low_count)

        return lax.ppermute(v, "fsdp", [(i, to(i)) for i in range(self.shards)])

    def swap_phase(self, v, phase):
        def to(i):
            mask = self.masks[phase] if i % 2 == 0 else self.masks[self.phases - 1 - phase]
            return i ^ (mask * self.low_count)

        return lax.ppermute(v, "fsdp", [(i, to(i)) for i in range(self.shards)])

    def swap_rep(self, v, mask):
        return lax.ppermute(v, "rep", [(i, i ^ mask) for i in range(self.reps)])


def after(v, *others):
    return lax.optimization_barrier((v, *others))[0]


def whole(shape):
    return pl.BlockSpec(shape, lambda *_: (0,) * len(shape))


def pause_kernel(source, out):
    out[...] = source[...] + 1.0


class Line:
    def __init__(self):
        self.ahead = []
        self.count = jnp.zeros((8, 128), F32)
        self.pauses = 0

    def take(self, *arrays):
        found = lax.optimization_barrier((*arrays, *self.ahead))[: len(arrays)]
        self.ahead = [min(found, key=lambda v: v.size)]
        return found

    def hold(self, *arrays):
        self.ahead.extend(arrays)

    def pause(self):
        small = jax.ShapeDtypeStruct((8, 128), F32)
        block = whole(small.shape)
        self.pauses += 1
        name = f"pause_{self.pauses}"
        self.count = self.call(pause_kernel, name, (1,), [block], block, small, [], [self.count], 4)

    def call(self, kernel, name, grid, in_specs, out_specs, out_shape, scratch, args, vmem=40):
        args = list(args)
        if self.ahead:
            args[0] = after(args[0], *self.ahead)
        outs = pl.pallas_call(
            kernel,
            grid=grid,
            in_specs=in_specs,
            out_specs=out_specs,
            out_shape=out_shape,
            scratch_shapes=scratch,
            compiler_params=pltpu.CompilerParams(vmem_limit_bytes=vmem * 2**20),
            cost_estimate=pl.CostEstimate(
                flops=(cost := int(COSTS.get(name, DEFAULT) * 1.15e9)),
                bytes_accessed=int(cost // 320),
                transcendentals=0,
            ),
            name=name,
        )(*args)
        self.ahead = [min(jax.tree.leaves(outs), key=lambda v: v.size)]
        return outs


def split_kernel(place, source, *outs):
    for j, out in enumerate(outs):
        out[...] = source[place.owner(j)]


def split_tokens(place, v, name):
    seqs, span, width = v.shape
    return place.line.call(
        functools.partial(split_kernel, place),
        name,
        (1,),
        [whole(v.shape)],
        [whole((span, width))] * seqs,
        [jax.ShapeDtypeStruct((span, width), v.dtype)] * seqs,
        [],
        (v,),
        vmem=58,
    )


def weights_kernel(place, w_qkv, w_out, w_up, w_down, *rest):
    vectors, pos, outs = rest[:8], rest[8], rest[9:]
    rows = w_qkv.shape[0]
    parts, low_count = place.parts, place.low_count
    width = w_out.shape[1]
    step = place.heads * HD
    hidden = w_up.shape[1] // parts
    firsts, seconds = outs[:low_count], outs[low_count:]
    for k in range(low_count):

        @pl.when(place.low() == k)
        def _():
            for o in range(low_count):
                for h in range(place.groups):
                    begin = ((k ^ o) * place.groups + h) * step
                    for g in range(3):
                        to = (3 * h + g) * step
                        firsts[o][:, to : to + step] = w_qkv[
                            :, g * width + begin : g * width + begin + step
                        ]
                    to = (3 * place.groups + h) * step
                    firsts[o][:, to : to + step] = w_out[:, begin : begin + step]

    for o in range(low_count):
        lanes = at((place.part() ^ o) * hidden, hidden, 128)
        seconds[o][:rows, :hidden] = w_up[:, lanes]
        seconds[o][:rows, hidden:] = w_down[:, lanes]

    lanes = seconds[0].shape[1]
    lines = []
    for v in vectors:
        lines.append(
            jnp.concatenate([v[...].astype(F32), jnp.zeros((1, lanes - v.shape[1]), F32)], axis=1)
        )
    span = pos.shape[1]
    for values in (
        [(pos[s : s + 1, :] // 64).astype(F32) for s in range(pos.shape[0])],
        [(pos[s : s + 1, :] % 64).astype(F32) for s in range(pos.shape[0])],
    ):
        lines.append(
            jnp.concatenate(values + [jnp.zeros((1, lanes - span * pos.shape[0]), F32)], axis=1)
        )
    lines.append(jnp.zeros((VEC - len(lines), lanes), F32))
    block = jnp.concatenate(lines, axis=0).astype(BF16)
    for o in range(low_count):
        seconds[o][rows:, :] = block


def split_weights(place, w_qkv, w_out, w_up, w_down, vectors, pos):
    rows = w_qkv.shape[0]
    args = [w_qkv, w_out, w_up, w_down] + [v.reshape(1, -1) for v in vectors] + [pos]
    first = (rows, (w_qkv.shape[1] + w_out.shape[1]) // place.low_count)
    second = (rows + VEC, (w_up.shape[1] + w_down.shape[1]) // place.parts)
    shapes = [first] * place.low_count + [second] * place.low_count
    outs = place.line.call(
        functools.partial(weights_kernel, place),
        "split_weights",
        (1,),
        [whole(v.shape) for v in args],
        [whole(s) for s in shapes],
        [jax.ShapeDtypeStruct(s, BF16) for s in shapes],
        [],
        args,
        vmem=58,
    )
    return outs[: place.low_count], outs[place.low_count :]


def second_tables_kernel(place, rows, *rest):
    slots = rest[: place.seqs]
    w_out, vec_out, bias, lines_kept = rest[place.seqs :]
    seqs, low_count, parts = place.seqs, place.low_count, place.parts
    block = rows + VEC
    width = w_out.shape[0]
    step = place.heads * HD
    low = place.low()
    for s in range(seqs):
        owner = place.owner(s)
        for o in range(low_count):
            found = slots[s][o * block : (o + 1) * block, :]
            l = low ^ o
            w_out[at((owner * low_count + l) * rows, rows, 16), :] = found[:rows]
            lines_kept[owner * low_count + l] = found[rows:].astype(F32)

    def line(row, size):
        return jnp.concatenate(
            [lines_kept[n, row : row + 1, :size] for n in range(place.shards)], axis=1
        )

    for row in range(4):
        vec_out[row : row + 1, :] = line(row, rows)
    vec_out[4:5, :] = line(5, rows) + line(7, rows)
    all_up = line(6, 4 * rows)
    all_qkv = line(4, 3 * rows)
    for k in range(parts):

        @pl.when(place.part() == k)
        def _():
            vec_out[5:6, :] = all_up[:, k * width : (k + 1) * width]

    for k in range(low_count):

        @pl.when(low == k)
        def _():
            for h in range(place.groups):
                for g in range(3):
                    begin = g * width + (k * place.groups + h) * step
                    bias[h : h + 1, g * step : (g + 1) * step] = all_qkv[:, begin : begin + step]

    vec_out[6:, :] = jnp.zeros((2, width), F32)


def second_tables(place, slots, rows, width):
    shapes = [
        jax.ShapeDtypeStruct((width, slots[0].shape[1]), BF16),
        jax.ShapeDtypeStruct((8, width), F32),
        jax.ShapeDtypeStruct((8, 3 * place.heads * HD), F32),
        jax.ShapeDtypeStruct((place.shards, VEC, slots[0].shape[1]), F32),
    ]
    return place.line.call(
        functools.partial(second_tables_kernel, place, rows),
        "tables_second",
        (1,),
        [whole(v.shape) for v in slots],
        [whole(v.shape) for v in shapes],
        shapes,
        [],
        slots,
        vmem=40,
    )


def first_tables_kernel(place, rows, span, inverse, lines_kept, *rest):
    slots = rest[: place.seqs]
    w_out, first_out, cos_out, sin_out = rest[place.seqs :]
    low_count = place.low_count
    low, chip = place.low(), place.chip()
    for s in range(place.seqs):
        owner = place.owner(s)
        for o in range(low_count):
            w_out[at((owner * low_count + (low ^ o)) * rows, rows, 16), :] = slots[s][
                o * rows : (o + 1) * rows, :
            ]
    still = jnp.zeros((HD - ROT, span), F32)
    for f in range(place.shards):
        lanes = at(chip * span, span, 128)
        value = lines_kept[f, 8:9, lanes] * 64.0 + lines_kept[f, 9:10, lanes]
        index = f * span + lax.broadcasted_iota(I32, (1, span), 1)
        first_out[:, f * span : (f + 1) * span] = index - value.astype(I32)
        phase = inverse[...] * value
        cosine, sine = jnp.cos(phase), jnp.sin(phase)
        crel, j = (f % low_count) ^ low, place.slot(f)
        to = at(j * span, span, 128)
        cos_out[crel, to, :] = jnp.concatenate([cosine, cosine, still + 1.0] * 2, axis=0).T
        sin_out[crel, to, :] = jnp.concatenate([-sine, sine, still] * 2, axis=0).T


def first_tables(place, slots, lines_kept, rows, width, span):
    inverse = (10000.0 ** (-jnp.arange(0, ROT, 2, dtype=F32) / ROT)).reshape(-1, 1)
    shapes = [
        jax.ShapeDtypeStruct((width, slots[0].shape[1]), BF16),
        jax.ShapeDtypeStruct((1, place.shards * span), I32),
        jax.ShapeDtypeStruct((place.low_count, place.seqs * span, 128), F32),
        jax.ShapeDtypeStruct((place.low_count, place.seqs * span, 128), F32),
    ]
    args = [inverse, lines_kept] + slots
    return place.line.call(
        functools.partial(first_tables_kernel, place, rows, span),
        "tables_first",
        (1,),
        [whole(v.shape) for v in args],
        [whole(v.shape) for v in shapes],
        shapes,
        [],
        args,
        vmem=16,
    )


def piece_specs(pieces, lines):
    split = pieces[0].shape[0] // lines

    def spec(i, width):
        return pl.BlockSpec(
            (lines, width), lambda g: (jnp.clip(g - i * split, 0, split - 1), 0)
        )

    return [spec(i, v.shape[1]) for i, v in enumerate(pieces)]


def piece_now(refs, steps):
    found = refs[0][...]
    for i in range(1, len(refs)):
        found = jnp.where(pl.program_id(0) >= i * (steps // len(refs)), refs[i][...], found)
    return found


def norm(source):
    source = source.astype(F32)
    centred = source - jnp.mean(source, axis=1, keepdims=True)
    return centred * lax.rsqrt(jnp.mean(centred * centred, axis=1, keepdims=True) + EPS)


def turned(v):
    half = ROT // 2
    columns = v.shape[1]
    lane = lax.broadcasted_iota(I32, v.shape, 1) % HD
    ahead = pltpu.roll(v, columns - half, 1)
    behind = pltpu.roll(v, half, 1)
    return jnp.where(lane < half, ahead, behind)


def front_kernel(place, steps, *refs):
    tokens, refs = refs[: place.low_count], refs[place.low_count :]
    weight, vec, bias, cosine, sine, one_out, *outs = refs
    step = place.heads * HD
    one = (norm(piece_now(tokens, steps)) * vec[0:1, :] + vec[1:2, :]).astype(BF16)
    one_out[0] = one
    copies = 2 * step // 128
    cos_cols = jnp.concatenate([cosine[0]] * copies, axis=1)
    sin_cols = jnp.concatenate([sine[0]] * copies, axis=1)
    for h in range(place.groups):
        q_out, k_out, v_out = outs[3 * h : 3 * h + 3]
        qkv = dot(one, weight[:, 3 * step * h : 3 * step * (h + 1)], NN) + bias[h : h + 1, :]
        both = qkv[:, : 2 * step]
        both = both * cos_cols + turned(both) * sin_cols
        q_out[0] = both[:, :step].astype(BF16)
        k_out[0] = both[:, step:].astype(BF16)
        v_out[0] = qkv[:, 2 * step :].astype(BF16)


def front(place, tokens, weight, vec, bias, cosine, sine):
    groups = len(tokens)
    count, width = tokens[0].shape
    step = place.heads * HD
    split = 2
    lines = count // split
    by_step = lambda cols: pl.BlockSpec((1, lines, cols), lambda g: (g // split, g % split, 0))
    shaped = lambda cols: jax.ShapeDtypeStruct((groups, count, cols), BF16)
    outs = place.line.call(
        functools.partial(front_kernel, place, groups * split),
        "front",
        (groups * split,),
        piece_specs(tokens, lines)
        + [whole(weight.shape), whole(vec.shape), whole(bias.shape)] + [by_step(128)] * 2,
        [by_step(width)] + [by_step(step)] * (3 * place.groups),
        [shaped(width)] + [shaped(step)] * (3 * place.groups),
        [],
        [*tokens, weight, vec, bias, cosine, sine],
        vmem=20,
    )
    return outs[0], [outs[1 + 3 * h : 4 + 3 * h] for h in range(place.groups)]


def middle_kernel(count, steps, *refs):
    tokens, grads, refs = refs[:count], refs[count : 2 * count], refs[2 * count :]
    vec, weight, two_out, normed_out, hidden_out, grad_out, sums = refs

    @pl.when(pl.program_id(0) == 0)
    def _():
        sums[...] = jnp.zeros_like(sums)

    width = weight.shape[0]
    normed = norm(piece_now(tokens, steps))
    normed_out[0] = normed.astype(BF16)
    two = (normed * vec[2:3, :] + vec[3:4, :]).astype(BF16)
    two_out[0] = two
    up = dot(two, weight[:, :width], NN) + vec[5:6, :]
    grad = piece_now(grads, steps)
    grad_hidden = dot(grad, weight[:, width:], NN)
    bell = jnp.exp(-0.5 * up * up)
    below = 1.0 + (0.3275911 * 0.5**0.5) * jnp.abs(up)
    t = pl.reciprocal(below, approx=True)
    t = t * (2.0 - below * t)
    series = t * (
        0.127414796 + t * (-0.142248368 + t * (0.7107068705 + t * (-0.7265760135 + t * 0.5307027145)))
    )
    tail = series * bell
    share = jnp.where(up >= 0.0, 1.0 - tail, tail)
    hidden_out[0] = (up * share).astype(BF16)
    slope = share + up * (bell * 0.3989422804014327)
    grad_up = (grad_hidden * slope).astype(BF16)
    grad_out[0] = grad_up
    sums[0:1, :] += jnp.sum(grad_up.astype(F32), axis=0, keepdims=True)
    sums[1:2, :] += jnp.sum(grad.astype(F32), axis=0, keepdims=True)


def middle(place, z, tokens, grads, vec, weight):
    groups = len(tokens)
    count, width = tokens[0].shape
    split = 2
    lines = count // split
    by_step = pl.BlockSpec((1, lines, width), lambda g: (g // split, g % split, 0))
    return place.line.call(
        functools.partial(middle_kernel, groups, groups * split),
        f"middle_{z}",
        (groups * split,),
        piece_specs(tokens, lines)
        + piece_specs(grads, lines)
        + [whole(vec.shape), whole(weight.shape)],
        [by_step] * 4 + [whole((8, width))],
        [jax.ShapeDtypeStruct((groups, count, width), BF16)] * 4 + [jax.ShapeDtypeStruct((8, width), F32)],
        [],
        [*tokens, *grads, vec, weight],
        vmem=20,
    )


def attention_kernel(
    place, group, span, q_in, k_in, v_in, w_in, first_in, cos_in, sin_in, *refs
):
    cot_in, refs = refs[: place.low_count], refs[place.low_count :]
    o_out, g_out, sums, qs, ks, vs, gs, o_turned, gq_turned, gk_sum, gv_sum = refs
    low_count = place.low_count
    count, columns = q_in.shape[1:]
    heads = columns // HD
    length = low_count * count
    begin = (3 * place.groups + group) * columns
    w_out = w_in[:, begin : begin + columns]

    def slot(f):
        crel = (f % low_count) ^ place.low()
        j = place.slot(f)
        return crel, at(j * span, span, 128)

    for f in range(length // span):
        to = slice(f * span, (f + 1) * span)
        crel, lines = slot(f)
        for source, kept in ((q_in, qs), (k_in, ks), (v_in, vs)):
            found = source[crel, lines, :]
            for h in range(heads):
                kept[h, to, :] = found[:, h * HD : (h + 1) * HD]
        cot = cot_in[0][lines, :]
        for o in range(1, low_count):
            cot = jnp.where(crel == o, cot_in[o][lines, :], cot)
        found = dot(cot, w_out, NN).astype(BF16)
        for h in range(heads):
            gs[h, to, :] = found[:, h * HD : (h + 1) * HD]

    def one_head(h, carry):
        keys = ks[h]
        values = vs[h]
        keys_turned = keys.astype(F32).T.astype(BF16)
        values_turned = values.astype(F32).T.astype(BF16)
        for i in range(length // TILE):
            here = slice(i * TILE, (i + 1) * TILE)
            query = qs[h, here, :]
            grad = gs[h, here, :]
            first = first_in[:, here]
            tiles = [slice(j * TILE, (j + 1) * TILE) for j in range(i + 1)]
            scores, grads = [], []
            for j, tile in enumerate(tiles):
                raw = dot(keys[tile], query, NT) * (0.125 * 1.4426950408889634)
                key_index = j * TILE + lax.broadcasted_iota(I32, (TILE, TILE), 0)
                seen = key_index >= first
                if j == i:
                    query_index = i * TILE + lax.broadcasted_iota(I32, (TILE, TILE), 1)
                    seen = seen & (key_index <= query_index)
                scores.append(jnp.where(seen, raw, NEG))
            top = functools.reduce(
                jnp.maximum, [jnp.max(raw, axis=0, keepdims=True) for raw in scores]
            )
            weights = [jnp.exp2(raw - top) for raw in scores]
            share = 1.0 / sum(jnp.sum(w, axis=0, keepdims=True) for w in weights)
            grads = [dot(values[tile], grad, NT) for tile in tiles]
            carried = share * sum(
                jnp.sum(w * g, axis=0, keepdims=True) for w, g in zip(weights, grads)
            )
            out, gq = None, None
            for j, tile in enumerate(tiles):
                probs = weights[j] * share
                low = probs.astype(BF16)
                grad_scores = (probs * (grads[j] - carried)).astype(BF16)
                out_part = dot(values_turned[:, tile], low, NN)
                gq_part = dot(keys_turned[:, tile], grad_scores, NN)
                gk_part = dot(grad_scores, query, NN)
                gv_part = dot(low, grad, NN)
                out = out_part if j == 0 else out + out_part
                gq = gq_part if j == 0 else gq + gq_part
                if j < i:
                    gk_sum[h, tile, :] += gk_part
                    gv_sum[h, tile, :] += gv_part
                else:
                    gk_sum[h, tile, :] = gk_part
                    gv_sum[h, tile, :] = gv_part
            o_turned[h, :, here] = out
            gq_turned[h, :, here] = gq
        return carry

    lax.fori_loop(0, heads, one_head, 0)
    total = jnp.zeros((1, 3 * columns), F32)
    for f in range(length // span):
        crel, lines = slot(f)
        to = slice(f * span, (f + 1) * span)
        o_out[crel, lines, :] = jnp.concatenate(
            [o_turned[h, :, to].T for h in range(heads)], axis=1
        ).astype(BF16)
        both = jnp.concatenate(
            [gq_turned[h, :, to].T for h in range(heads)] + [gk_sum[h, to, :] for h in range(heads)],
            axis=1,
        )
        both = both * 0.125
        copies = 2 * columns // 128
        cos_cols = jnp.concatenate([cos_in[crel, lines, :]] * copies, axis=1)
        sin_cols = jnp.concatenate([sin_in[crel, lines, :]] * copies, axis=1)
        both = both * cos_cols - turned(both) * sin_cols
        value = jnp.concatenate([gv_sum[h, to, :] for h in range(heads)], axis=1)
        grad = jnp.concatenate([both, value], axis=1).astype(BF16)
        g_out[crel, lines, :] = grad
        total = total + jnp.sum(grad.astype(F32), axis=0, keepdims=True)
    sums[...] = jnp.concatenate([total, jnp.zeros((7, 3 * columns), F32)], axis=0)


def attention(place, group, span, q, k, v, cot, w, first, cosine, sine):
    count, columns = q.shape[1:]
    low_count = place.low_count
    heads = columns // HD
    length = low_count * count
    outs = [
        jax.ShapeDtypeStruct((low_count, count, columns), BF16),
        jax.ShapeDtypeStruct((low_count, count, 3 * columns), BF16),
        jax.ShapeDtypeStruct((8, 3 * columns), F32),
    ]
    args = [q, k, v, w, first, cosine, sine, *cot]
    return place.line.call(
        functools.partial(attention_kernel, place, group, span),
        f"attention_{group}",
        (1,),
        [whole(a.shape) for a in args],
        [whole(a.shape) for a in outs],
        outs,
        [pltpu.VMEM((heads, length, HD), BF16)] * 4
        + [pltpu.VMEM((heads, HD, length), F32)] * 2
        + [pltpu.VMEM((heads, length, HD), F32)] * 2,
        args,
        vmem=16 * (length // 1024),
    )


def back_kernel(place, groups, *refs):
    normed, hidden, grad_up = refs[:3]
    attended, grad_qkv = refs[3 : 3 + groups], refs[3 + groups : 3 + 2 * groups]
    vec, second = refs[3 + 2 * groups : 5 + 2 * groups]
    keep, send, sums = refs[-3:]
    step = pl.program_id(0)
    width = normed.shape[2]

    @pl.when(step == 0)
    def _():
        sums[...] = jnp.zeros_like(sums)

    two = dot(grad_up[0], second[:, :width], NT)
    out = dot(hidden[0], second[:, width:], NT)
    both = two * vec[2:3, :]
    source = normed[0].astype(F32)
    sums[2:3, :] += jnp.sum(two * source, axis=0, keepdims=True)
    sums[3:4, :] += jnp.sum(two, axis=0, keepdims=True)
    if groups:
        first = refs[5 + 2 * groups]
        cols = place.heads * HD
        one = None
        for h in range(groups):
            term = dot(grad_qkv[h][0], first[:, 3 * cols * h : 3 * cols * (h + 1)], NT)
            one = term if one is None else one + term
            begin = (3 * groups + h) * cols
            out = out + dot(attended[h][0], first[:, begin : begin + cols], NT)
        both = both + one * vec[0:1, :]
        sums[0:1, :] += jnp.sum(one * source, axis=0, keepdims=True)
        sums[1:2, :] += jnp.sum(one, axis=0, keepdims=True)
    split = pl.num_programs(0) // place.low_count

    @pl.when(step < split)
    def _():
        keep[0] = out.astype(BF16)
        keep[1] = both.astype(BF16)

    @pl.when(step >= split)
    def _():
        send[0, 0] = out.astype(BF16)
        send[0, 1] = both.astype(BF16)


def back(place, z, normed, hidden, grad_up, attended, grad_qkv, vec, second, first):
    low_count = place.low_count
    groups, count, width = normed.shape
    split = 2
    lines = count // split
    by_step = lambda cols: pl.BlockSpec((1, lines, cols), lambda g: (g // split, g % split, 0))
    args = [normed, hidden, grad_up, *attended, *grad_qkv]
    fixed = [vec, second] + ([first] if attended else [])

    def sent(g):
        later = jnp.maximum(g - split, 0)
        return (later // split, 0, later % split, 0)

    return place.line.call(
        functools.partial(back_kernel, place, len(attended)),
        f"back_{z}",
        (groups * split,),
        [by_step(v.shape[2]) for v in args] + [whole(v.shape) for v in fixed],
        [
            pl.BlockSpec((2, lines, width), lambda g: (0, jnp.minimum(g, split - 1), 0)),
            pl.BlockSpec((1, 2, lines, width), sent),
            whole((8, width)),
        ],
        [
            jax.ShapeDtypeStruct((2, count, width), BF16),
            jax.ShapeDtypeStruct((low_count - 1, 2, count, width), BF16),
            jax.ShapeDtypeStruct((8, width), F32),
        ],
        [],
        args + fixed,
        vmem=24,
    )


def store_rows(place, rows, block, value, scratch, columns):
    low_count = place.low_count
    for s in range(place.seqs):
        owner = place.owner(s)
        for o in range(low_count):
            begin = owner * (low_count * rows) + (place.low() ^ o) * rows
            scratch[s, o * block : o * block + rows, columns] = value[at(begin, rows, 16), :].astype(BF16)


def product(lefts, rights):
    each = len(lefts) // len(rights)
    total = None
    for i, left in enumerate(lefts):
        lines = left.shape[0]
        right = rights[i // each][(i % each) * lines : (i % each + 1) * lines, :]
        term = dot(left[...], right, TN)
        total = term if total is None else total + term
    return total


def second_grads_kernel(place, rows, count, *refs):
    two, grad_up, hidden = [refs[k * count : (k + 1) * count] for k in range(3)]
    cot, (keep, send, total, turned_rows) = refs[3 * count : -4], refs[-4:]
    step = pl.program_id(0)
    width = two[0].shape[1]
    half = place.seqs // 2

    def one(left, right, columns):
        total[...] = product(left, right)
        store_rows(place, rows, rows, total, turned_rows, columns)

    @pl.when(step == 0)
    def _():
        one(two, grad_up, slice(0, width))

    @pl.when(step == 1)
    def _():
        one(cot, hidden, slice(width, 2 * width))
        keep[...] = turned_rows[:half]
        send[...] = turned_rows[half:]


def second_grads(place, rows, two, grad_up, cot, hidden):
    width = two[0].shape[2]
    flat = [v.reshape(-1, width) for v in (*two, *grad_up, *hidden)] + [p for c in cot for p in c]
    half = (place.seqs // 2, place.low_count * rows, 2 * width)
    return place.line.call(
        functools.partial(second_grads_kernel, place, rows, len(two)),
        "second_grads",
        (2,),
        [whole(v.shape) for v in flat],
        [whole(half)] * 2,
        [jax.ShapeDtypeStruct(half, BF16)] * 2,
        [pltpu.VMEM((width, width), F32), pltpu.VMEM((2 * half[0],) + half[1:], BF16)],
        flat,
        vmem=20,
    )


def first_grads_kernel(place, rows, count, one, *refs):
    grad_qkv, attended, refs = refs[:count], refs[count : 2 * count], refs[2 * count :]
    cot, (keep, send, total, ordered) = refs[:-4], refs[-4:]
    half = place.seqs // 2
    step = place.heads * HD
    for h in range(count):
        total[:, : 3 * step] = dot(one[...], grad_qkv[h][...], TN)
        total[:, 3 * step :] = product(cot, [attended[h]])
        store_rows(place, rows, rows, total, ordered, slice(4 * step * h, 4 * step * (h + 1)))
    keep[...] = ordered[:half]
    send[...] = ordered[half:]


def first_grads(place, number, rows, one, cot, grad_qkv, attended):
    width = one.shape[2]
    step = place.heads * HD
    count = len(attended)
    args = [v.reshape(-1, v.shape[2]) for v in (one, *grad_qkv, *attended)] + list(cot)
    half = (place.seqs // 2, place.low_count * rows, 4 * step * count)
    return place.line.call(
        functools.partial(first_grads_kernel, place, rows, count),
        f"first_grads_{number}",
        (1,),
        [whole(v.shape) for v in args],
        [whole(half)] * 2,
        [jax.ShapeDtypeStruct(half, BF16)] * 2,
        [pltpu.VMEM((width, 4 * step), F32), pltpu.VMEM((2 * half[0],) + half[1:], BF16)],
        args,
        vmem=16,
    )


def vectors_kernel(place, rows, *refs):
    sums_qkv = refs[: place.groups]
    sums_back = refs[place.groups : place.groups + place.pair]
    sums_middle = refs[place.groups + place.pair : -4]
    keep, send, lines_kept, ordered = refs[-4:]
    seqs, low_count, parts = place.seqs, place.low_count, place.parts
    width = keep.shape[2]
    step = place.heads * HD
    half = seqs // 2
    back = sum(s[...] for s in sums_back)
    up = sum(s[0:1, :] for s in sums_middle)
    grad = sums_middle[0][1:2, :] * (1.0 / low_count)
    zero = jnp.zeros((1, step), F32)
    all_qkv = jnp.concatenate(
        [
            jnp.where(place.low() == k, sums_qkv[h][0:1, g * step : (g + 1) * step], zero)
            for g in range(3)
            for k in range(low_count)
            for h in range(place.groups)
        ],
        axis=1,
    )
    all_up = jnp.concatenate([jnp.where(place.part() == k, up, 0.0) for k in range(parts)], axis=1)
    lines = [(back[r : r + 1], rows) for r in range(4)]
    lines += [(all_qkv, 3 * rows), (grad, rows), (all_up, 4 * rows)]
    for n in range(place.shards):
        made = [
            jnp.concatenate(
                [v[:, n * size : (n + 1) * size], jnp.zeros((1, width - size), F32)], axis=1
            )
            for v, size in lines
        ]
        made.append(jnp.zeros((VEC - len(made), width), F32))
        lines_kept[n] = jnp.concatenate(made, axis=0)
    for s in range(seqs):
        for o in range(low_count):
            n = place.owner(s) * low_count + (place.low() ^ o)
            ordered[s, o * VEC : (o + 1) * VEC, :] = lines_kept[n].astype(BF16)
    keep[...] = ordered[:half]
    send[...] = ordered[half:]


def vector_grads(place, rows, width, sums_qkv, sums_back, sums_middle):
    half = (place.seqs // 2, place.low_count * VEC, width)
    args = [*sums_qkv, *sums_back, *sums_middle]
    return place.line.call(
        functools.partial(vectors_kernel, place, rows),
        "vector_grads",
        (1,),
        [whole(v.shape) for v in args],
        [whole(half)] * 2,
        [jax.ShapeDtypeStruct(half, BF16)] * 2,
        [
            pltpu.VMEM((place.shards, VEC, width), F32),
            pltpu.VMEM((2 * half[0],) + half[1:], BF16),
        ],
        args,
        vmem=16,
    )


def tokens_kernel(place, source, cot, vec, *rest):
    blocks, (out, grad_in) = rest[: place.seqs], rest[place.seqs :]
    for j in range(place.seqs):
        s = place.owner(j)
        x = source[s].astype(F32)
        out[s] = (x + blocks[j][0].astype(F32) + vec[4:5, :]).astype(BF16)
        mean = jnp.mean(x, axis=1, keepdims=True)
        centred = x - mean
        scale = lax.rsqrt(jnp.mean(centred * centred, axis=1, keepdims=True) + EPS)
        normed = centred * scale
        e = blocks[j][1].astype(F32)
        pulled = (
            e
            - jnp.mean(e, axis=1, keepdims=True)
            - normed * jnp.mean(e * normed, axis=1, keepdims=True)
        ) * scale
        grad_in[s] = (cot[s].astype(F32) + pulled).astype(BF16)


def finish_tokens(place, source, cot, vec, blocks):
    return place.line.call(
        functools.partial(tokens_kernel, place),
        "finish_tokens",
        (1,),
        [whole(source.shape)] * 2 + [whole(vec.shape)] + [whole(b.shape) for b in blocks],
        [whole(source.shape)] * 2,
        [jax.ShapeDtypeStruct(source.shape, BF16)] * 2,
        [],
        [source, cot, vec] + blocks,
    )


def first_end_kernel(place, rows, counts, *refs):
    found, refs = refs[: 2 * len(counts)], refs[2 * len(counts) + 1 :]
    w_qkv, w_out, vectors = refs[0], refs[1], refs[2:]
    low_count, groups = place.low_count, place.groups
    width = w_out.shape[1]
    step = place.heads * HD
    even = (lax.axis_index("rep") % 2) == 0
    total = None
    first = 0
    for i, count in enumerate(counts):
        for o in range(low_count):
            mine, other = found[2 * i][o].astype(F32), found[2 * i + 1][o].astype(F32)
            piece = jnp.concatenate(
                [jnp.where(even, mine, other), jnp.where(even, other, mine)], axis=1
            )
            for k in range(low_count):

                @pl.when(place.low() == k)
                def _():
                    for h in range(count):
                        begin = ((k ^ o) * groups + first + h) * step
                        for g in range(3):
                            to = g * width + begin
                            part = (4 * h + g) * step
                            w_qkv[:, to : to + step] = piece[:rows, part : part + step]
                        part = (4 * h + 3) * step
                        w_out[:, begin : begin + step] = piece[:rows, part : part + step]

            if i == len(counts) - 1:
                total = piece[rows:] if total is None else total + piece[rows:]
        first += count
    for r, out in enumerate(vectors):
        out[...] = total[r : r + 1, : out.shape[1]]


def first_end(place, rows, width, counts, pieces):
    shapes = [(rows, 3 * width), (rows, width)]
    shapes += [(1, n * rows) for n in (1, 1, 1, 1, 3, 1, 4)]
    pieces = pieces + [place.line.count]
    return place.line.call(
        functools.partial(first_end_kernel, place, rows, counts),
        "first_end",
        (1,),
        [whole(p.shape) for p in pieces],
        [whole(v) for v in shapes],
        [jax.ShapeDtypeStruct(v, F32) for v in shapes],
        [],
        pieces,
    )


def second_end_kernel(place, *refs):
    pieces = refs[: place.parts]
    w_up, w_down = refs[place.parts :]
    parts = place.parts
    step = w_up.shape[1] // parts
    for r in range(parts):
        t = place.part() ^ r
        w_up[:, at(t * step, step, 128)] = pieces[r][:, :step].astype(F32)
        w_down[:, at(t * step, step, 128)] = pieces[r][:, step:].astype(F32)


def second_end(place, pieces):
    rows, columns = pieces[0].shape
    shape = (rows, columns // 2 * place.parts)
    return place.line.call(
        functools.partial(second_end_kernel, place),
        "second_end",
        (1,),
        [whole(p.shape) for p in pieces],
        [whole(shape)] * 2,
        [jax.ShapeDtypeStruct(shape, F32)] * 2,
        [],
        pieces,
    )


def add(a, b):
    return (a.astype(F32) + b.astype(F32)).astype(BF16)


def on_device(
    layer_input,
    positions,
    cotangent,
    w_qkv,
    w_out,
    w_up,
    w_down,
    ln1_gain,
    ln1_bias,
    ln2_gain,
    ln2_bias,
    qkv_bias,
    out_bias,
    up_bias,
    down_bias,
):
    seqs, span, width = layer_input.shape
    place = Place(seqs, lax.axis_size("fsdp"), lax.axis_size("rep"))
    low_count, pair = place.low_count, place.pair
    rows = w_qkv.shape[0]

    line = place.line
    lows = range(1, low_count)

    def to_low(v):
        return [place.swap_low(v, o) for o in lows]

    class Gather:
        def __init__(self, block):
            self.slots = [block]
            self.coming = [[place.swap_phase(block, p)] for p in range(place.phases)]

        def step(self, more=0):
            count = len(self.coming[0])
            ahead = self.coming[1][:more] if more else []
            got = line.take(*self.coming.pop(0), *ahead)
            if more:
                self.coming[0][:more] = got[count:]
            for later, p in zip(self.coming, range(place.phases - len(self.coming), place.phases)):
                later.extend(place.swap_phase(v, p) for v in got[:count])
            self.slots.extend(got[:count])

    class Scatter:
        def __init__(self, keep, send):
            self.phase = place.phases - 1
            self.kept = [keep[s] for s in range(keep.shape[0])]
            self.got = place.swap_phase(send, self.phase)

        def step(self):
            got = line.take(self.got)[0]
            self.phase -= 1
            half = len(self.kept) // 2
            sums = [add(v, got[s]) for s, v in enumerate(self.kept)]
            if self.phase >= 0:
                self.kept = sums[:half]
                sent = sums[half] if half == 1 else jnp.stack(sums[half:])
                line.hold(sent)
                got = place.swap_phase(sent, self.phase)
                self.got = got[None] if half == 1 else got
            else:
                block = sums[0].reshape(low_count, sums[0].shape[0] // low_count, -1)
                self.kept = [block[0]]
                line.hold(sums[0])
                self.got = [place.swap_low(block[o], o) for o in lows]

        def end(self):
            return jnp.stack(self.kept + list(line.take(*self.got)))

    masks = [m for m in (1, 2, 4, 8, 16) if m < place.reps]
    even = lax.axis_index("rep") % 2 == 0

    class Reps:
        def __init__(self, mine):
            columns = mine.shape[2] // 2
            low_half, high_half = mine[..., :columns], mine[..., columns:]
            self.held = jnp.where(even, low_half, high_half)
            sent = jnp.where(even, high_half, low_half)
            line.hold(sent)
            self.masks = masks[1:]
            self.got = place.swap_rep(sent, 1)

        def step(self):
            self.held = add(self.held, line.take(self.got)[0])
            line.hold(self.held)
            self.got = place.swap_rep(self.held, self.masks.pop(0) if self.masks else 1)

        def end(self):
            return [self.held, line.take(self.got)[0]]

    class Pairs:
        def __init__(self, mine):
            self.mine = mine
            self.masks = masks[1:] + masks[:1]
            self.got = place.swap_rep(mine, self.masks.pop(0))

        def step(self):
            self.mine = add(self.mine, line.take(self.got)[0])
            line.hold(self.mine)
            self.got = place.swap_rep(self.mine, self.masks.pop(0))

        def end(self):
            return self.mine, line.take(self.got)[0]

    split_x = split_tokens(place, layer_input, "split_input")
    coming = [place.swap_slot(split_x[j], j) for j in range(1, seqs)]
    if pair == 2:
        coming.append(place.swap_rep(split_x[0], 1))
    split_c = split_tokens(place, cotangent, "split_cotangent")
    vectors = (ln1_gain, ln1_bias, ln2_gain, ln2_bias, qkv_bias, out_bias, up_bias, down_bias)
    firsts, seconds = split_weights(place, w_qkv, w_out, w_up, w_down, vectors, positions)
    coming_second = [place.swap_low(seconds[o], o) for o in lows]
    coming = line.take(*coming)
    block_x = jnp.concatenate([split_x[0], *coming[: seqs - 1]], axis=0)
    tokens, grads = [[block_x]], []
    coming_x = to_low(block_x)
    if pair == 2:
        rest = jnp.concatenate(coming[: seqs - 1], axis=0)
        line.hold(rest)
        later_x = place.swap_rep(rest, 1)
    sent = lax.optimization_barrier((*split_c[1:], *coming))[: seqs - 1]
    coming_c = [place.swap_slot(v, j) for v, j in zip(sent, range(1, seqs))]
    line.hold(block_x)
    coming_second = line.take(*coming_second)
    block_second = jnp.concatenate([seconds[0], *coming_second], axis=0)
    line.hold(block_second)
    tokens[0].extend(line.take(*coming_x))
    coming_c = line.take(*coming_c)
    second = Gather(line.take(block_second)[0])
    block_c = jnp.concatenate([split_c[0], *coming_c], axis=0)
    line.hold(block_c)
    grads.append([block_c])
    coming_c = to_low(block_c)
    if pair == 2:
        later_x = line.take(later_x)[0]
        other_x = jnp.concatenate([coming[seqs - 1], later_x], axis=0)
        line.hold(other_x)
        coming_x = to_low(other_x)
        other_c = place.swap_rep(after(block_c, later_x), 1)
    grads[0].extend(line.take(*coming_c))
    second.step()
    if pair == 2:
        tokens.append([other_x, *line.take(*coming_x)])
    coming_first = [place.swap_low(v, o) for v, o in zip(line.take(*firsts[1:]), lows)]
    coming_first = line.take(*coming_first)
    block_first = jnp.concatenate([firsts[0], *coming_first], axis=0)
    line.hold(block_first)
    second.step()
    first = Gather(after(block_first, *second.slots))
    if pair == 2:
        other_c = line.take(other_c)[0]
        coming_c = to_low(other_c)

    w_second, vec, bias, lines_kept = second_tables(place, second.slots, rows, width)
    two, normed, hidden, grad_up, sums_middle, sums_back = [[None] * pair for _ in range(6)]

    def forward(z):
        two[z], normed[z], hidden[z], grad_up[z], sums_middle[z] = middle(
            place, z, tokens[z], grads[z], vec, w_second
        )

    def backward(z, attended, grad_qkv, w_first):
        keep, send, sums_back[z] = back(
            place, z, normed[z], hidden[z], grad_up[z], attended, grad_qkv, vec, w_second, w_first
        )
        return keep, [place.swap_low(send[o - 1][r], o) for o in lows for r in range(2)]

    def low_sum(keep, coming):
        coming = line.take(*coming)
        return jnp.stack(
            [sum([v.astype(F32) for v in coming[r::2]], keep[r].astype(F32)) for r in range(2)]
        )

    if pair == 2:
        grads.append([other_c, *line.take(*coming_c)])
        forward(1)
        keep, coming = backward(1, [], [], None)
    first.step(more=1)
    out_pieces, out_found, out_coming = [], [], []

    def next_piece():
        if out_coming:
            out_found.append(line.take(out_coming.pop())[0])
        if out_pieces:
            out_coming.append(place.swap_rep(after(out_pieces.pop(0), *line.ahead), 1))

    if pair == 2:
        line.pause()
        coming = line.take(*coming)
        sums = [
            sum(v.astype(F32) for v in [keep[r]] + list(coming[r::2])).astype(BF16) for r in range(2)
        ]
        cut = 3 * sums[0].shape[0] // 4
        out_pieces += [sums[0][:cut], jnp.concatenate([sums[0][cut:], sums[1]])]
        line.hold(*out_pieces)
        next_piece()
    forward(0)
    second_sums = Scatter(*second_grads(place, rows, two, grad_up, grads, hidden))

    next_piece()
    first.step()
    w_first, seen, cosine, sine = first_tables(place, first.slots, lines_kept, rows, width, span)
    one, heads = front(place, tokens[0], w_first, vec, bias, cosine, sine)
    attended, grad_qkv, sums_qkv = [[None] * place.groups for _ in range(3)]
    cot = grads[0]

    def attend(h):
        attended[h], grad_qkv[h], sums_qkv[h] = attention(
            place, h, span, *heads[h], cot, w_first, seen, cosine, sine
        )

    first_sums, counts = [], []

    def close(number, chosen):
        counts.append(len(chosen))
        first_sums.append(
            Scatter(
                *first_grads(
                    place, number, rows, one, cot,
                    [grad_qkv[h] for h in chosen], [attended[h] for h in chosen],
                )
            )
        )

    last_group = place.groups - 1
    for h in range(last_group):
        attend(h)
        if second_sums.phase >= 0:
            second_sums.step()
        if h == 1:
            next_piece()
    if last_group:
        close(0, list(range(last_group)))
    while second_sums.phase >= 0:
        second_sums.step()
    second_mine = second_sums.end()
    line.hold(second_mine)
    while out_coming:
        next_piece()
    second_reps = Pairs(second_mine) if pair == 2 else Reps(second_mine)
    attend(last_group)
    for v in first_sums:
        v.step()
    close(1, [last_group])
    keep, coming = backward(0, attended, grad_qkv, w_first)

    earlier, last = first_sums[:-1], first_sums[-1]
    for v in earlier:
        v.step()
    last.step()
    if pair == 2:
        second_reps.step()
    vector_sums = Scatter(
        *vector_grads(place, rows, 4 * place.heads * HD, sums_qkv, sums_back, sums_middle)
    )
    line.pause()
    reps = []
    for v in earlier:
        mine = v.end()
        line.hold(mine)
        reps.append(Reps(mine))
    while out_coming:
        next_piece()
    out_sum = low_sum(keep, coming)
    if pair == 2:
        out_sum = out_sum + jnp.concatenate(out_found).reshape(out_sum.shape).astype(F32)
    out_sum = out_sum.astype(BF16).reshape(2, seqs, span, width)
    line.hold(out_sum)
    blocks = [out_sum[:, s] for s in range(seqs)]

    def pass_on(phase):
        chosen = [s for s in range(seqs) if s >> phase & 1]
        got = place.swap_phase(jnp.stack([blocks[s] for s in chosen]), phase)
        return chosen, got

    def passed(chosen, got):
        got = line.take(got)[0]
        for k, s in enumerate(chosen):
            blocks[s] = got[k]

    going = pass_on(0)
    line.pause()
    vector_sums.step()
    last.step()
    line.pause()
    vector_sums.step()
    line.pause()
    mine = jnp.concatenate([last.end(), vector_sums.end()], axis=1)
    line.hold(mine)
    reps.append(Reps(mine))
    line.pause()
    for r in reps[:-1]:
        r.step()
        line.pause()
    reps[-1].step()
    for phase in range(1, place.phases):
        passed(*going)
        going = pass_on(phase)
    line.pause()
    for r in reps:
        while r.masks:
            r.step()
            line.pause()
    for r in reps:
        r.step()
    if pair == 1:
        while second_reps.masks:
            second_reps.step()
            line.pause()
        second_reps.step()
        line.pause()
    if pair == 2:
        pieces = [v[o] for v in second_reps.end() for o in range(low_count)]
    else:
        pieces = second_reps.end()
        pieces = jnp.where(even, pieces[0], pieces[1]), jnp.where(even, pieces[1], pieces[0])
        pieces = list(jnp.concatenate(pieces, axis=2))
    grad_w_up, grad_w_down = second_end(place, pieces)
    passed(*going)
    output, grad_input = finish_tokens(place, layer_input, cotangent, vec, blocks)
    pieces = [p for r in reps for p in r.end()]
    grad_w_qkv, grad_w_out, *vector_outs = first_end(place, rows, width, counts, pieces)
    vector_outs = [v.reshape(-1) for v in vector_outs]
    return (
        output,
        grad_input,
        grad_w_qkv,
        grad_w_out,
        grad_w_up,
        grad_w_down,
        *vector_outs,
        vector_outs[5],
    )


def solution(mesh):
    tokens = P("rep", "fsdp", None)
    matrix = P("fsdp", None)
    vector = P("fsdp")
    return jax.shard_map(
        on_device,
        mesh=mesh,
        in_specs=(tokens, P("rep", "fsdp"), tokens) + (matrix,) * 4 + (vector,) * 8,
        out_specs=(tokens, tokens) + (matrix,) * 4 + (vector,) * 8,
        check_vma=False,
    )
```

```python
import functools

import jax
import jax.numpy as jnp
from jax import lax
from jax.experimental import pallas as pl
from jax.experimental.pallas import tpu as pltpu
from jax.sharding import PartitionSpec as P

H = 12
HD = 64
ROT = 16
TILE = 256
VEC = 16
COSTS = {
    "tables_second": 0.1,
    "middle_1": 0.1,
    "back_1": 0.1,
    "second_grads": 0.1,
    "back_0": 2,
    "vector_grads": 10,
    "second_end": 0.3,
    "pause_7": 0.3,
    "pause_8": 0.3,
    "pause_9": 0.3,
    "pause_10": 0.3,
    "pause_11": 0.3,
    "pause_12": 0.3,
    "pause_13": 0.3,
    "tables_first": 0.1,
    "front": 0.1,
}
DEFAULT = 20

EPS = 1e-05
NEG = -1e30

F32 = jnp.float32
BF16 = jnp.bfloat16
I32 = jnp.int32

NN = ((1,), (0,))
NT = ((1,), (1,))
TN = ((0,), (0,))


def dot(a, b, dims):
    return lax.dot_general(a, b, (dims, ((), ())), preferred_element_type=F32)


def at(start, size, multiple):
    return pl.ds(pl.multiple_of(start, multiple), size)


class Place:
    def __init__(self, seqs, shards, reps):
        self.seqs, self.shards, self.reps = seqs, shards, reps
        self.low_count = shards // seqs
        self.pair = 2 if reps % 2 == 0 and H % (2 * self.low_count) == 0 else 1
        self.parts = self.pair * self.low_count
        self.line = Line()
        self.heads = 2 if H // self.low_count % 2 == 0 else 3
        self.groups = H // self.low_count // self.heads
        self.masks = []
        while 2 ** len(self.masks) < seqs:
            self.masks.append(2 ** len(self.masks))
        self.phases = len(self.masks)

    def chip(self):
        return lax.axis_index("fsdp") // self.low_count

    def low(self):
        return lax.axis_index("fsdp") % self.low_count

    def part(self):
        return (lax.axis_index("rep") % self.pair) * self.low_count + self.low()

    def owner(self, slot):
        even = sum(self.masks[p] for p in range(self.phases) if slot >> p & 1)
        odd = sum(self.masks[self.phases - 1 - p] for p in range(self.phases) if slot >> p & 1)
        if even == odd:
            return self.chip() ^ even
        return self.chip() ^ jnp.where(lax.axis_index("fsdp") % 2 == 0, even, odd)

    def slot(self, block):
        j = (block // self.low_count) ^ self.chip()
        other = sum((j >> p & 1) << (self.phases - 1 - p) for p in range(self.phases))
        even = lax.axis_index("fsdp") % 2 == 0 if self.low_count == 1 else block % self.low_count % 2 == 0
        return jnp.where(even, j, other)

    def swap_low(self, v, mask):
        return lax.ppermute(v, "fsdp", [(i, i ^ mask) for i in range(self.shards)])

    def swap_slot(self, v, slot):
        def to(i):
            order = self.masks if i % 2 == 0 else self.masks[::-1]
            return i ^ (sum(m for p, m in enumerate(order) if slot >> p & 1) * self.low_count)

        return lax.ppermute(v, "fsdp", [(i, to(i)) for i in range(self.shards)])

    def swap_phase(self, v, phase):
        def to(i):
            mask = self.masks[phase] if i % 2 == 0 else self.masks[self.phases - 1 - phase]
            return i ^ (mask * self.low_count)

        return lax.ppermute(v, "fsdp", [(i, to(i)) for i in range(self.shards)])

    def swap_rep(self, v, mask):
        return lax.ppermute(v, "rep", [(i, i ^ mask) for i in range(self.reps)])


def after(v, *others):
    return lax.optimization_barrier((v, *others))[0]


def whole(shape):
    return pl.BlockSpec(shape, lambda *_: (0,) * len(shape))


def pause_kernel(source, out):
    out[...] = source[...] + 1.0


class Line:
    def __init__(self):
        self.ahead = []
        self.count = jnp.zeros((8, 128), F32)
        self.pauses = 0

    def take(self, *arrays):
        found = lax.optimization_barrier((*arrays, *self.ahead))[: len(arrays)]
        self.ahead = [min(found, key=lambda v: v.size)]
        return found

    def hold(self, *arrays):
        self.ahead.extend(arrays)

    def pause(self):
        small = jax.ShapeDtypeStruct((8, 128), F32)
        block = whole(small.shape)
        self.pauses += 1
        name = f"pause_{self.pauses}"
        self.count = self.call(pause_kernel, name, (1,), [block], block, small, [], [self.count], 4)

    def call(self, kernel, name, grid, in_specs, out_specs, out_shape, scratch, args, vmem=40):
        args = list(args)
        if self.ahead:
            args[0] = after(args[0], *self.ahead)
        outs = pl.pallas_call(
            kernel,
            grid=grid,
            in_specs=in_specs,
            out_specs=out_specs,
            out_shape=out_shape,
            scratch_shapes=scratch,
            compiler_params=pltpu.CompilerParams(vmem_limit_bytes=vmem * 2**20),
            cost_estimate=pl.CostEstimate(
                flops=(cost := int(COSTS.get(name, DEFAULT) * 1.15e9)),
                bytes_accessed=int(cost // 320),
                transcendentals=0,
            ),
            name=name,
        )(*args)
        self.ahead = [min(jax.tree.leaves(outs), key=lambda v: v.size)]
        return outs


def split_kernel(place, source, *outs):
    for j, out in enumerate(outs):
        out[...] = source[place.owner(j)]


def split_tokens(place, v, name):
    seqs, span, width = v.shape
    return place.line.call(
        functools.partial(split_kernel, place),
        name,
        (1,),
        [whole(v.shape)],
        [whole((span, width))] * seqs,
        [jax.ShapeDtypeStruct((span, width), v.dtype)] * seqs,
        [],
        (v,),
        vmem=58,
    )


def weights_kernel(place, w_qkv, w_out, w_up, w_down, *rest):
    vectors, pos, outs = rest[:8], rest[8], rest[9:]
    rows = w_qkv.shape[0]
    parts, low_count = place.parts, place.low_count
    width = w_out.shape[1]
    step = place.heads * HD
    hidden = w_up.shape[1] // parts
    firsts, seconds = outs[:low_count], outs[low_count:]
    for k in range(low_count):

        @pl.when(place.low() == k)
        def _():
            for o in range(low_count):
                for h in range(place.groups):
                    begin = ((k ^ o) * place.groups + h) * step
                    for g in range(3):
                        to = (3 * h + g) * step
                        firsts[o][:, to : to + step] = w_qkv[
                            :, g * width + begin : g * width + begin + step
                        ]
                    to = (3 * place.groups + h) * step
                    firsts[o][:, to : to + step] = w_out[:, begin : begin + step]

    for o in range(low_count):
        lanes = at((place.part() ^ o) * hidden, hidden, 128)
        seconds[o][:rows, :hidden] = w_up[:, lanes]
        seconds[o][:rows, hidden:] = w_down[:, lanes]

    lanes = seconds[0].shape[1]
    lines = []
    for v in vectors:
        lines.append(
            jnp.concatenate([v[...].astype(F32), jnp.zeros((1, lanes - v.shape[1]), F32)], axis=1)
        )
    span = pos.shape[1]
    for values in (
        [(pos[s : s + 1, :] // 64).astype(F32) for s in range(pos.shape[0])],
        [(pos[s : s + 1, :] % 64).astype(F32) for s in range(pos.shape[0])],
    ):
        lines.append(
            jnp.concatenate(values + [jnp.zeros((1, lanes - span * pos.shape[0]), F32)], axis=1)
        )
    lines.append(jnp.zeros((VEC - len(lines), lanes), F32))
    block = jnp.concatenate(lines, axis=0).astype(BF16)
    for o in range(low_count):
        seconds[o][rows:, :] = block


def split_weights(place, w_qkv, w_out, w_up, w_down, vectors, pos):
    rows = w_qkv.shape[0]
    args = [w_qkv, w_out, w_up, w_down] + [v.reshape(1, -1) for v in vectors] + [pos]
    first = (rows, (w_qkv.shape[1] + w_out.shape[1]) // place.low_count)
    second = (rows + VEC, (w_up.shape[1] + w_down.shape[1]) // place.parts)
    shapes = [first] * place.low_count + [second] * place.low_count
    outs = place.line.call(
        functools.partial(weights_kernel, place),
        "split_weights",
        (1,),
        [whole(v.shape) for v in args],
        [whole(s) for s in shapes],
        [jax.ShapeDtypeStruct(s, BF16) for s in shapes],
        [],
        args,
        vmem=58,
    )
    return outs[: place.low_count], outs[place.low_count :]


def second_tables_kernel(place, rows, *rest):
    slots = rest[: place.seqs]
    w_out, vec_out, bias, lines_kept = rest[place.seqs :]
    seqs, low_count, parts = place.seqs, place.low_count, place.parts
    block = rows + VEC
    width = w_out.shape[0]
    step = place.heads * HD
    low = place.low()
    for s in range(seqs):
        owner = place.owner(s)
        for o in range(low_count):
            found = slots[s][o * block : (o + 1) * block, :]
            l = low ^ o
            w_out[at((owner * low_count + l) * rows, rows, 16), :] = found[:rows]
            lines_kept[owner * low_count + l] = found[rows:].astype(F32)

    def line(row, size):
        return jnp.concatenate(
            [lines_kept[n, row : row + 1, :size] for n in range(place.shards)], axis=1
        )

    for row in range(4):
        vec_out[row : row + 1, :] = line(row, rows)
    vec_out[4:5, :] = line(5, rows) + line(7, rows)
    all_up = line(6, 4 * rows)
    all_qkv = line(4, 3 * rows)
    for k in range(parts):

        @pl.when(place.part() == k)
        def _():
            vec_out[5:6, :] = all_up[:, k * width : (k + 1) * width]

    for k in range(low_count):

        @pl.when(low == k)
        def _():
            for h in range(place.groups):
                for g in range(3):
                    begin = g * width + (k * place.groups + h) * step
                    bias[h : h + 1, g * step : (g + 1) * step] = all_qkv[:, begin : begin + step]

    vec_out[6:, :] = jnp.zeros((2, width), F32)


def second_tables(place, slots, rows, width):
    shapes = [
        jax.ShapeDtypeStruct((width, slots[0].shape[1]), BF16),
        jax.ShapeDtypeStruct((8, width), F32),
        jax.ShapeDtypeStruct((8, 3 * place.heads * HD), F32),
        jax.ShapeDtypeStruct((place.shards, VEC, slots[0].shape[1]), F32),
    ]
    return place.line.call(
        functools.partial(second_tables_kernel, place, rows),
        "tables_second",
        (1,),
        [whole(v.shape) for v in slots],
        [whole(v.shape) for v in shapes],
        shapes,
        [],
        slots,
        vmem=40,
    )


def first_tables_kernel(place, rows, span, inverse, lines_kept, *rest):
    slots = rest[: place.seqs]
    w_out, first_out, cos_out, sin_out = rest[place.seqs :]
    low_count = place.low_count
    low, chip = place.low(), place.chip()
    for s in range(place.seqs):
        owner = place.owner(s)
        for o in range(low_count):
            w_out[at((owner * low_count + (low ^ o)) * rows, rows, 16), :] = slots[s][
                o * rows : (o + 1) * rows, :
            ]
    still = jnp.zeros((HD - ROT, span), F32)
    for f in range(place.shards):
        lanes = at(chip * span, span, 128)
        value = lines_kept[f, 8:9, lanes] * 64.0 + lines_kept[f, 9:10, lanes]
        index = f * span + lax.broadcasted_iota(I32, (1, span), 1)
        first_out[:, f * span : (f + 1) * span] = index - value.astype(I32)
        phase = inverse[...] * value
        cosine, sine = jnp.cos(phase), jnp.sin(phase)
        crel, j = (f % low_count) ^ low, place.slot(f)
        to = at(j * span, span, 128)
        cos_out[crel, to, :] = jnp.concatenate([cosine, cosine, still + 1.0] * 2, axis=0).T
        sin_out[crel, to, :] = jnp.concatenate([-sine, sine, still] * 2, axis=0).T


def first_tables(place, slots, lines_kept, rows, width, span):
    inverse = (10000.0 ** (-jnp.arange(0, ROT, 2, dtype=F32) / ROT)).reshape(-1, 1)
    shapes = [
        jax.ShapeDtypeStruct((width, slots[0].shape[1]), BF16),
        jax.ShapeDtypeStruct((1, place.shards * span), I32),
        jax.ShapeDtypeStruct((place.low_count, place.seqs * span, 128), F32),
        jax.ShapeDtypeStruct((place.low_count, place.seqs * span, 128), F32),
    ]
    args = [inverse, lines_kept] + slots
    return place.line.call(
        functools.partial(first_tables_kernel, place, rows, span),
        "tables_first",
        (1,),
        [whole(v.shape) for v in args],
        [whole(v.shape) for v in shapes],
        shapes,
        [],
        args,
        vmem=16,
    )


def piece_specs(pieces, lines):
    split = pieces[0].shape[0] // lines

    def spec(i, width):
        return pl.BlockSpec(
            (lines, width), lambda g: (jnp.clip(g - i * split, 0, split - 1), 0)
        )

    return [spec(i, v.shape[1]) for i, v in enumerate(pieces)]


def piece_now(refs, steps):
    found = refs[0][...]
    for i in range(1, len(refs)):
        found = jnp.where(pl.program_id(0) >= i * (steps // len(refs)), refs[i][...], found)
    return found


def norm(source):
    source = source.astype(F32)
    centred = source - jnp.mean(source, axis=1, keepdims=True)
    return centred * lax.rsqrt(jnp.mean(centred * centred, axis=1, keepdims=True) + EPS)


def turned(v):
    half = ROT // 2
    columns = v.shape[1]
    lane = lax.broadcasted_iota(I32, v.shape, 1) % HD
    ahead = pltpu.roll(v, columns - half, 1)
    behind = pltpu.roll(v, half, 1)
    return jnp.where(lane < half, ahead, behind)


def front_kernel(place, steps, *refs):
    tokens, refs = refs[: place.low_count], refs[place.low_count :]
    weight, vec, bias, cosine, sine, one_out, *outs = refs
    step = place.heads * HD
    one = (norm(piece_now(tokens, steps)) * vec[0:1, :] + vec[1:2, :]).astype(BF16)
    one_out[0] = one
    copies = 2 * step // 128
    cos_cols = jnp.concatenate([cosine[0]] * copies, axis=1)
    sin_cols = jnp.concatenate([sine[0]] * copies, axis=1)
    for h in range(place.groups):
        q_out, k_out, v_out = outs[3 * h : 3 * h + 3]
        qkv = dot(one, weight[:, 3 * step * h : 3 * step * (h + 1)], NN) + bias[h : h + 1, :]
        both = qkv[:, : 2 * step]
        both = both * cos_cols + turned(both) * sin_cols
        q_out[0] = both[:, :step].astype(BF16)
        k_out[0] = both[:, step:].astype(BF16)
        v_out[0] = qkv[:, 2 * step :].astype(BF16)


def front(place, tokens, weight, vec, bias, cosine, sine):
    groups = len(tokens)
    count, width = tokens[0].shape
    step = place.heads * HD
    split = 2
    lines = count // split
    by_step = lambda cols: pl.BlockSpec((1, lines, cols), lambda g: (g // split, g % split, 0))
    shaped = lambda cols: jax.ShapeDtypeStruct((groups, count, cols), BF16)
    outs = place.line.call(
        functools.partial(front_kernel, place, groups * split),
        "front",
        (groups * split,),
        piece_specs(tokens, lines)
        + [whole(weight.shape), whole(vec.shape), whole(bias.shape)] + [by_step(128)] * 2,
        [by_step(width)] + [by_step(step)] * (3 * place.groups),
        [shaped(width)] + [shaped(step)] * (3 * place.groups),
        [],
        [*tokens, weight, vec, bias, cosine, sine],
        vmem=20,
    )
    return outs[0], [outs[1 + 3 * h : 4 + 3 * h] for h in range(place.groups)]


def middle_kernel(count, steps, *refs):
    tokens, grads, refs = refs[:count], refs[count : 2 * count], refs[2 * count :]
    vec, weight, two_out, normed_out, hidden_out, grad_out, sums = refs

    @pl.when(pl.program_id(0) == 0)
    def _():
        sums[...] = jnp.zeros_like(sums)

    width = weight.shape[0]
    normed = norm(piece_now(tokens, steps))
    normed_out[0] = normed.astype(BF16)
    two = (normed * vec[2:3, :] + vec[3:4, :]).astype(BF16)
    two_out[0] = two
    up = dot(two, weight[:, :width], NN) + vec[5:6, :]
    grad = piece_now(grads, steps)
    grad_hidden = dot(grad, weight[:, width:], NN)
    bell = jnp.exp(-0.5 * up * up)
    below = 1.0 + (0.3275911 * 0.5**0.5) * jnp.abs(up)
    t = pl.reciprocal(below, approx=True)
    t = t * (2.0 - below * t)
    series = t * (
        0.127414796 + t * (-0.142248368 + t * (0.7107068705 + t * (-0.7265760135 + t * 0.5307027145)))
    )
    tail = series * bell
    share = jnp.where(up >= 0.0, 1.0 - tail, tail)
    hidden_out[0] = (up * share).astype(BF16)
    slope = share + up * (bell * 0.3989422804014327)
    grad_up = (grad_hidden * slope).astype(BF16)
    grad_out[0] = grad_up
    sums[0:1, :] += jnp.sum(grad_up.astype(F32), axis=0, keepdims=True)
    sums[1:2, :] += jnp.sum(grad.astype(F32), axis=0, keepdims=True)


def middle(place, z, tokens, grads, vec, weight):
    groups = len(tokens)
    count, width = tokens[0].shape
    split = 2
    lines = count // split
    by_step = pl.BlockSpec((1, lines, width), lambda g: (g // split, g % split, 0))
    return place.line.call(
        functools.partial(middle_kernel, groups, groups * split),
        f"middle_{z}",
        (groups * split,),
        piece_specs(tokens, lines)
        + piece_specs(grads, lines)
        + [whole(vec.shape), whole(weight.shape)],
        [by_step] * 4 + [whole((8, width))],
        [jax.ShapeDtypeStruct((groups, count, width), BF16)] * 4 + [jax.ShapeDtypeStruct((8, width), F32)],
        [],
        [*tokens, *grads, vec, weight],
        vmem=20,
    )


def attention_kernel(
    place, group, span, q_in, k_in, v_in, w_in, first_in, cos_in, sin_in, *refs
):
    cot_in, refs = refs[: place.low_count], refs[place.low_count :]
    o_out, g_out, sums, qs, ks, vs, gs, o_turned, gq_turned, gk_sum, gv_sum = refs
    low_count = place.low_count
    count, columns = q_in.shape[1:]
    heads = columns // HD
    length = low_count * count
    begin = (3 * place.groups + group) * columns
    w_out = w_in[:, begin : begin + columns]

    def slot(f):
        crel = (f % low_count) ^ place.low()
        j = place.slot(f)
        return crel, at(j * span, span, 128)

    for f in range(length // span):
        to = slice(f * span, (f + 1) * span)
        crel, lines = slot(f)
        for source, kept in ((q_in, qs), (k_in, ks), (v_in, vs)):
            found = source[crel, lines, :]
            for h in range(heads):
                kept[h, to, :] = found[:, h * HD : (h + 1) * HD]
        cot = cot_in[0][lines, :]
        for o in range(1, low_count):
            cot = jnp.where(crel == o, cot_in[o][lines, :], cot)
        found = dot(cot, w_out, NN).astype(BF16)
        for h in range(heads):
            gs[h, to, :] = found[:, h * HD : (h + 1) * HD]

    def one_head(h, carry):
        keys = ks[h]
        values = vs[h]
        keys_turned = keys.astype(F32).T.astype(BF16)
        values_turned = values.astype(F32).T.astype(BF16)
        for i in range(length // TILE):
            here = slice(i * TILE, (i + 1) * TILE)
            query = qs[h, here, :]
            grad = gs[h, here, :]
            first = first_in[:, here]
            tiles = [slice(j * TILE, (j + 1) * TILE) for j in range(i + 1)]
            scores, grads = [], []
            for j, tile in enumerate(tiles):
                raw = dot(keys[tile], query, NT) * (0.125 * 1.4426950408889634)
                key_index = j * TILE + lax.broadcasted_iota(I32, (TILE, TILE), 0)
                seen = key_index >= first
                if j == i:
                    query_index = i * TILE + lax.broadcasted_iota(I32, (TILE, TILE), 1)
                    seen = seen & (key_index <= query_index)
                scores.append(jnp.where(seen, raw, NEG))
            top = functools.reduce(
                jnp.maximum, [jnp.max(raw, axis=0, keepdims=True) for raw in scores]
            )
            weights = [jnp.exp2(raw - top) for raw in scores]
            share = 1.0 / sum(jnp.sum(w, axis=0, keepdims=True) for w in weights)
            grads = [dot(values[tile], grad, NT) for tile in tiles]
            carried = share * sum(
                jnp.sum(w * g, axis=0, keepdims=True) for w, g in zip(weights, grads)
            )
            out, gq = None, None
            for j, tile in enumerate(tiles):
                probs = weights[j] * share
                low = probs.astype(BF16)
                grad_scores = (probs * (grads[j] - carried)).astype(BF16)
                out_part = dot(values_turned[:, tile], low, NN)
                gq_part = dot(keys_turned[:, tile], grad_scores, NN)
                gk_part = dot(grad_scores, query, NN)
                gv_part = dot(low, grad, NN)
                out = out_part if j == 0 else out + out_part
                gq = gq_part if j == 0 else gq + gq_part
                if j < i:
                    gk_sum[h, tile, :] += gk_part
                    gv_sum[h, tile, :] += gv_part
                else:
                    gk_sum[h, tile, :] = gk_part
                    gv_sum[h, tile, :] = gv_part
            o_turned[h, :, here] = out
            gq_turned[h, :, here] = gq
        return carry

    lax.fori_loop(0, heads, one_head, 0)
    total = jnp.zeros((1, 3 * columns), F32)
    for f in range(length // span):
        crel, lines = slot(f)
        to = slice(f * span, (f + 1) * span)
        o_out[crel, lines, :] = jnp.concatenate(
            [o_turned[h, :, to].T for h in range(heads)], axis=1
        ).astype(BF16)
        both = jnp.concatenate(
            [gq_turned[h, :, to].T for h in range(heads)] + [gk_sum[h, to, :] for h in range(heads)],
            axis=1,
        )
        both = both * 0.125
        copies = 2 * columns // 128
        cos_cols = jnp.concatenate([cos_in[crel, lines, :]] * copies, axis=1)
        sin_cols = jnp.concatenate([sin_in[crel, lines, :]] * copies, axis=1)
        both = both * cos_cols - turned(both) * sin_cols
        value = jnp.concatenate([gv_sum[h, to, :] for h in range(heads)], axis=1)
        grad = jnp.concatenate([both, value], axis=1).astype(BF16)
        g_out[crel, lines, :] = grad
        total = total + jnp.sum(grad.astype(F32), axis=0, keepdims=True)
    sums[...] = jnp.concatenate([total, jnp.zeros((7, 3 * columns), F32)], axis=0)


def attention(place, group, span, q, k, v, cot, w, first, cosine, sine):
    count, columns = q.shape[1:]
    low_count = place.low_count
    heads = columns // HD
    length = low_count * count
    outs = [
        jax.ShapeDtypeStruct((low_count, count, columns), BF16),
        jax.ShapeDtypeStruct((low_count, count, 3 * columns), BF16),
        jax.ShapeDtypeStruct((8, 3 * columns), F32),
    ]
    args = [q, k, v, w, first, cosine, sine, *cot]
    return place.line.call(
        functools.partial(attention_kernel, place, group, span),
        f"attention_{group}",
        (1,),
        [whole(a.shape) for a in args],
        [whole(a.shape) for a in outs],
        outs,
        [pltpu.VMEM((heads, length, HD), BF16)] * 4
        + [pltpu.VMEM((heads, HD, length), F32)] * 2
        + [pltpu.VMEM((heads, length, HD), F32)] * 2,
        args,
        vmem=16 * (length // 1024),
    )


def back_kernel(place, groups, *refs):
    normed, hidden, grad_up = refs[:3]
    attended, grad_qkv = refs[3 : 3 + groups], refs[3 + groups : 3 + 2 * groups]
    vec, second = refs[3 + 2 * groups : 5 + 2 * groups]
    keep, send, sums = refs[-3:]
    step = pl.program_id(0)
    width = normed.shape[2]

    @pl.when(step == 0)
    def _():
        sums[...] = jnp.zeros_like(sums)

    two = dot(grad_up[0], second[:, :width], NT)
    out = dot(hidden[0], second[:, width:], NT)
    both = two * vec[2:3, :]
    source = normed[0].astype(F32)
    sums[2:3, :] += jnp.sum(two * source, axis=0, keepdims=True)
    sums[3:4, :] += jnp.sum(two, axis=0, keepdims=True)
    if groups:
        first = refs[5 + 2 * groups]
        cols = place.heads * HD
        one = None
        for h in range(groups):
            term = dot(grad_qkv[h][0], first[:, 3 * cols * h : 3 * cols * (h + 1)], NT)
            one = term if one is None else one + term
            begin = (3 * groups + h) * cols
            out = out + dot(attended[h][0], first[:, begin : begin + cols], NT)
        both = both + one * vec[0:1, :]
        sums[0:1, :] += jnp.sum(one * source, axis=0, keepdims=True)
        sums[1:2, :] += jnp.sum(one, axis=0, keepdims=True)
    split = pl.num_programs(0) // place.low_count

    @pl.when(step < split)
    def _():
        keep[0] = out.astype(BF16)
        keep[1] = both.astype(BF16)

    @pl.when(step >= split)
    def _():
        send[0, 0] = out.astype(BF16)
        send[0, 1] = both.astype(BF16)


def back(place, z, normed, hidden, grad_up, attended, grad_qkv, vec, second, first):
    low_count = place.low_count
    groups, count, width = normed.shape
    split = 2
    lines = count // split
    by_step = lambda cols: pl.BlockSpec((1, lines, cols), lambda g: (g // split, g % split, 0))
    args = [normed, hidden, grad_up, *attended, *grad_qkv]
    fixed = [vec, second] + ([first] if attended else [])

    def sent(g):
        later = jnp.maximum(g - split, 0)
        return (later // split, 0, later % split, 0)

    return place.line.call(
        functools.partial(back_kernel, place, len(attended)),
        f"back_{z}",
        (groups * split,),
        [by_step(v.shape[2]) for v in args] + [whole(v.shape) for v in fixed],
        [
            pl.BlockSpec((2, lines, width), lambda g: (0, jnp.minimum(g, split - 1), 0)),
            pl.BlockSpec((1, 2, lines, width), sent),
            whole((8, width)),
        ],
        [
            jax.ShapeDtypeStruct((2, count, width), BF16),
            jax.ShapeDtypeStruct((low_count - 1, 2, count, width), BF16),
            jax.ShapeDtypeStruct((8, width), F32),
        ],
        [],
        args + fixed,
        vmem=24,
    )


def store_rows(place, rows, block, value, scratch, columns):
    low_count = place.low_count
    for s in range(place.seqs):
        owner = place.owner(s)
        for o in range(low_count):
            begin = owner * (low_count * rows) + (place.low() ^ o) * rows
            scratch[s, o * block : o * block + rows, columns] = value[at(begin, rows, 16), :].astype(BF16)


def product(lefts, rights):
    each = len(lefts) // len(rights)
    total = None
    for i, left in enumerate(lefts):
        lines = left.shape[0]
        right = rights[i // each][(i % each) * lines : (i % each + 1) * lines, :]
        term = dot(left[...], right, TN)
        total = term if total is None else total + term
    return total


def second_grads_kernel(place, rows, count, *refs):
    two, grad_up, hidden = [refs[k * count : (k + 1) * count] for k in range(3)]
    cot, (keep, send, total, turned_rows) = refs[3 * count : -4], refs[-4:]
    step = pl.program_id(0)
    width = two[0].shape[1]
    half = place.seqs // 2

    def one(left, right, columns):
        total[...] = product(left, right)
        store_rows(place, rows, rows, total, turned_rows, columns)

    @pl.when(step == 0)
    def _():
        one(two, grad_up, slice(0, width))

    @pl.when(step == 1)
    def _():
        one(cot, hidden, slice(width, 2 * width))
        keep[...] = turned_rows[:half]
        send[...] = turned_rows[half:]


def second_grads(place, rows, two, grad_up, cot, hidden):
    width = two[0].shape[2]
    flat = [v.reshape(-1, width) for v in (*two, *grad_up, *hidden)] + [p for c in cot for p in c]
    half = (place.seqs // 2, place.low_count * rows, 2 * width)
    return place.line.call(
        functools.partial(second_grads_kernel, place, rows, len(two)),
        "second_grads",
        (2,),
        [whole(v.shape) for v in flat],
        [whole(half)] * 2,
        [jax.ShapeDtypeStruct(half, BF16)] * 2,
        [pltpu.VMEM((width, width), F32), pltpu.VMEM((2 * half[0],) + half[1:], BF16)],
        flat,
        vmem=20,
    )


def first_grads_kernel(place, rows, count, one, *refs):
    grad_qkv, attended, refs = refs[:count], refs[count : 2 * count], refs[2 * count :]
    cot, (keep, send, total, ordered) = refs[:-4], refs[-4:]
    half = place.seqs // 2
    step = place.heads * HD
    for h in range(count):
        total[:, : 3 * step] = dot(one[...], grad_qkv[h][...], TN)
        total[:, 3 * step :] = product(cot, [attended[h]])
        store_rows(place, rows, rows, total, ordered, slice(4 * step * h, 4 * step * (h + 1)))
    keep[...] = ordered[:half]
    send[...] = ordered[half:]


def first_grads(place, number, rows, one, cot, grad_qkv, attended):
    width = one.shape[2]
    step = place.heads * HD
    count = len(attended)
    args = [v.reshape(-1, v.shape[2]) for v in (one, *grad_qkv, *attended)] + list(cot)
    half = (place.seqs // 2, place.low_count * rows, 4 * step * count)
    return place.line.call(
        functools.partial(first_grads_kernel, place, rows, count),
        f"first_grads_{number}",
        (1,),
        [whole(v.shape) for v in args],
        [whole(half)] * 2,
        [jax.ShapeDtypeStruct(half, BF16)] * 2,
        [pltpu.VMEM((width, 4 * step), F32), pltpu.VMEM((2 * half[0],) + half[1:], BF16)],
        args,
        vmem=16,
    )


def vectors_kernel(place, rows, *refs):
    sums_qkv = refs[: place.groups]
    sums_back = refs[place.groups : place.groups + place.pair]
    sums_middle = refs[place.groups + place.pair : -4]
    keep, send, lines_kept, ordered = refs[-4:]
    seqs, low_count, parts = place.seqs, place.low_count, place.parts
    width = keep.shape[2]
    step = place.heads * HD
    half = seqs // 2
    back = sum(s[...] for s in sums_back)
    up = sum(s[0:1, :] for s in sums_middle)
    grad = sums_middle[0][1:2, :] * (1.0 / low_count)
    zero = jnp.zeros((1, step), F32)
    all_qkv = jnp.concatenate(
        [
            jnp.where(place.low() == k, sums_qkv[h][0:1, g * step : (g + 1) * step], zero)
            for g in range(3)
            for k in range(low_count)
            for h in range(place.groups)
        ],
        axis=1,
    )
    all_up = jnp.concatenate([jnp.where(place.part() == k, up, 0.0) for k in range(parts)], axis=1)
    lines = [(back[r : r + 1], rows) for r in range(4)]
    lines += [(all_qkv, 3 * rows), (grad, rows), (all_up, 4 * rows)]
    for n in range(place.shards):
        made = [
            jnp.concatenate(
                [v[:, n * size : (n + 1) * size], jnp.zeros((1, width - size), F32)], axis=1
            )
            for v, size in lines
        ]
        made.append(jnp.zeros((VEC - len(made), width), F32))
        lines_kept[n] = jnp.concatenate(made, axis=0)
    for s in range(seqs):
        for o in range(low_count):
            n = place.owner(s) * low_count + (place.low() ^ o)
            ordered[s, o * VEC : (o + 1) * VEC, :] = lines_kept[n].astype(BF16)
    keep[...] = ordered[:half]
    send[...] = ordered[half:]


def vector_grads(place, rows, width, sums_qkv, sums_back, sums_middle):
    half = (place.seqs // 2, place.low_count * VEC, width)
    args = [*sums_qkv, *sums_back, *sums_middle]
    return place.line.call(
        functools.partial(vectors_kernel, place, rows),
        "vector_grads",
        (1,),
        [whole(v.shape) for v in args],
        [whole(half)] * 2,
        [jax.ShapeDtypeStruct(half, BF16)] * 2,
        [
            pltpu.VMEM((place.shards, VEC, width), F32),
            pltpu.VMEM((2 * half[0],) + half[1:], BF16),
        ],
        args,
        vmem=16,
    )


def tokens_kernel(place, source, cot, vec, *rest):
    blocks, (out, grad_in) = rest[: place.seqs], rest[place.seqs :]
    for j in range(place.seqs):
        s = place.owner(j)
        x = source[s].astype(F32)
        out[s] = (x + blocks[j][0].astype(F32) + vec[4:5, :]).astype(BF16)
        mean = jnp.mean(x, axis=1, keepdims=True)
        centred = x - mean
        scale = lax.rsqrt(jnp.mean(centred * centred, axis=1, keepdims=True) + EPS)
        normed = centred * scale
        e = blocks[j][1].astype(F32)
        pulled = (
            e
            - jnp.mean(e, axis=1, keepdims=True)
            - normed * jnp.mean(e * normed, axis=1, keepdims=True)
        ) * scale
        grad_in[s] = (cot[s].astype(F32) + pulled).astype(BF16)


def finish_tokens(place, source, cot, vec, blocks):
    return place.line.call(
        functools.partial(tokens_kernel, place),
        "finish_tokens",
        (1,),
        [whole(source.shape)] * 2 + [whole(vec.shape)] + [whole(b.shape) for b in blocks],
        [whole(source.shape)] * 2,
        [jax.ShapeDtypeStruct(source.shape, BF16)] * 2,
        [],
        [source, cot, vec] + blocks,
    )


def first_end_kernel(place, rows, counts, *refs):
    found, refs = refs[: 2 * len(counts)], refs[2 * len(counts) + 1 :]
    w_qkv, w_out, vectors = refs[0], refs[1], refs[2:]
    low_count, groups = place.low_count, place.groups
    width = w_out.shape[1]
    step = place.heads * HD
    even = (lax.axis_index("rep") % 2) == 0
    total = None
    first = 0
    for i, count in enumerate(counts):
        for o in range(low_count):
            mine, other = found[2 * i][o].astype(F32), found[2 * i + 1][o].astype(F32)
            piece = jnp.concatenate(
                [jnp.where(even, mine, other), jnp.where(even, other, mine)], axis=1
            )
            for k in range(low_count):

                @pl.when(place.low() == k)
                def _():
                    for h in range(count):
                        begin = ((k ^ o) * groups + first + h) * step
                        for g in range(3):
                            to = g * width + begin
                            part = (4 * h + g) * step
                            w_qkv[:, to : to + step] = piece[:rows, part : part + step]
                        part = (4 * h + 3) * step
                        w_out[:, begin : begin + step] = piece[:rows, part : part + step]

            if i == len(counts) - 1:
                total = piece[rows:] if total is None else total + piece[rows:]
        first += count
    for r, out in enumerate(vectors):
        out[...] = total[5 if r == 7 else r, : out.shape[0]]


def first_end(place, rows, width, counts, pieces):
    shapes = [(rows, 3 * width), (rows, width)]
    shapes += [(n * rows,) for n in (1, 1, 1, 1, 3, 1, 4, 1)]
    pieces = pieces + [place.line.count]
    return place.line.call(
        functools.partial(first_end_kernel, place, rows, counts),
        "first_end",
        (1,),
        [whole(p.shape) for p in pieces],
        [whole(v) for v in shapes],
        [jax.ShapeDtypeStruct(v, F32) for v in shapes],
        [],
        pieces,
    )


def second_end_kernel(place, *refs):
    pieces = refs[: place.parts]
    w_up, w_down = refs[place.parts :]
    parts = place.parts
    step = w_up.shape[1] // parts
    for r in range(parts):
        t = place.part() ^ r
        w_up[:, at(t * step, step, 128)] = pieces[r][:, :step].astype(F32)
        w_down[:, at(t * step, step, 128)] = pieces[r][:, step:].astype(F32)


def second_end(place, pieces):
    rows, columns = pieces[0].shape
    shape = (rows, columns // 2 * place.parts)
    return place.line.call(
        functools.partial(second_end_kernel, place),
        "second_end",
        (1,),
        [whole(p.shape) for p in pieces],
        [whole(shape)] * 2,
        [jax.ShapeDtypeStruct(shape, F32)] * 2,
        [],
        pieces,
    )


def add(a, b):
    return (a.astype(F32) + b.astype(F32)).astype(BF16)


def on_device(
    layer_input,
    positions,
    cotangent,
    w_qkv,
    w_out,
    w_up,
    w_down,
    ln1_gain,
    ln1_bias,
    ln2_gain,
    ln2_bias,
    qkv_bias,
    out_bias,
    up_bias,
    down_bias,
):
    seqs, span, width = layer_input.shape
    place = Place(seqs, lax.axis_size("fsdp"), lax.axis_size("rep"))
    low_count, pair = place.low_count, place.pair
    rows = w_qkv.shape[0]

    line = place.line
    lows = range(1, low_count)

    def to_low(v):
        return [place.swap_low(v, o) for o in lows]

    class Gather:
        def __init__(self, block):
            self.slots = [block]
            self.coming = [[place.swap_phase(block, p)] for p in range(place.phases)]

        def step(self, more=0):
            count = len(self.coming[0])
            ahead = self.coming[1][:more] if more else []
            got = line.take(*self.coming.pop(0), *ahead)
            if more:
                self.coming[0][:more] = got[count:]
            for later, p in zip(self.coming, range(place.phases - len(self.coming), place.phases)):
                later.extend(place.swap_phase(v, p) for v in got[:count])
            self.slots.extend(got[:count])

    class Scatter:
        def __init__(self, keep, send):
            self.phase = place.phases - 1
            self.kept = [keep[s] for s in range(keep.shape[0])]
            self.got = place.swap_phase(send, self.phase)

        def step(self):
            got = line.take(self.got)[0]
            self.phase -= 1
            half = len(self.kept) // 2
            sums = [add(v, got[s]) for s, v in enumerate(self.kept)]
            if self.phase >= 0:
                self.kept = sums[:half]
                sent = sums[half] if half == 1 else jnp.stack(sums[half:])
                line.hold(sent)
                got = place.swap_phase(sent, self.phase)
                self.got = got[None] if half == 1 else got
            else:
                block = sums[0].reshape(low_count, sums[0].shape[0] // low_count, -1)
                self.kept = [block[0]]
                line.hold(sums[0])
                self.got = [place.swap_low(block[o], o) for o in lows]

        def end(self):
            return jnp.stack(self.kept + list(line.take(*self.got)))

    masks = [m for m in (1, 2, 4, 8, 16) if m < place.reps]
    even = lax.axis_index("rep") % 2 == 0

    class Reps:
        def __init__(self, mine):
            columns = mine.shape[2] // 2
            low_half, high_half = mine[..., :columns], mine[..., columns:]
            self.held = jnp.where(even, low_half, high_half)
            sent = jnp.where(even, high_half, low_half)
            line.hold(sent)
            self.masks = masks[1:]
            self.got = place.swap_rep(sent, 1)

        def step(self):
            self.held = add(self.held, line.take(self.got)[0])
            line.hold(self.held)
            self.got = place.swap_rep(self.held, self.masks.pop(0) if self.masks else 1)

        def end(self):
            return [self.held, line.take(self.got)[0]]

    class Pairs:
        def __init__(self, mine):
            self.mine = mine
            self.masks = masks[1:] + masks[:1]
            self.got = place.swap_rep(mine, self.masks.pop(0))

        def step(self):
            self.mine = add(self.mine, line.take(self.got)[0])
            line.hold(self.mine)
            self.got = place.swap_rep(self.mine, self.masks.pop(0))

        def end(self):
            return self.mine, line.take(self.got)[0]

    split_x = split_tokens(place, layer_input, "split_input")
    coming = [place.swap_slot(split_x[j], j) for j in range(1, seqs)]
    if pair == 2:
        coming.append(place.swap_rep(split_x[0], 1))
    split_c = split_tokens(place, cotangent, "split_cotangent")
    vectors = (ln1_gain, ln1_bias, ln2_gain, ln2_bias, qkv_bias, out_bias, up_bias, down_bias)
    firsts, seconds = split_weights(place, w_qkv, w_out, w_up, w_down, vectors, positions)
    coming_second = [place.swap_low(seconds[o], o) for o in lows]
    coming = line.take(*coming)
    block_x = jnp.concatenate([split_x[0], *coming[: seqs - 1]], axis=0)
    tokens, grads = [[block_x]], []
    coming_x = to_low(block_x)
    if pair == 2:
        rest = jnp.concatenate(coming[: seqs - 1], axis=0)
        line.hold(rest)
        later_x = place.swap_rep(rest, 1)
    sent = lax.optimization_barrier((*split_c[1:], *coming))[: seqs - 1]
    coming_c = [place.swap_slot(v, j) for v, j in zip(sent, range(1, seqs))]
    line.hold(block_x)
    coming_second = line.take(*coming_second)
    block_second = jnp.concatenate([seconds[0], *coming_second], axis=0)
    line.hold(block_second)
    tokens[0].extend(line.take(*coming_x))
    coming_c = line.take(*coming_c)
    second = Gather(line.take(block_second)[0])
    block_c = jnp.concatenate([split_c[0], *coming_c], axis=0)
    line.hold(block_c)
    grads.append([block_c])
    coming_c = to_low(block_c)
    if pair == 2:
        later_x = line.take(later_x)[0]
        other_x = jnp.concatenate([coming[seqs - 1], later_x], axis=0)
        line.hold(other_x)
        coming_x = to_low(other_x)
        other_c = place.swap_rep(after(block_c, later_x), 1)
    grads[0].extend(line.take(*coming_c))
    second.step()
    if pair == 2:
        tokens.append([other_x, *line.take(*coming_x)])
    coming_first = [place.swap_low(v, o) for v, o in zip(line.take(*firsts[1:]), lows)]
    coming_first = line.take(*coming_first)
    block_first = jnp.concatenate([firsts[0], *coming_first], axis=0)
    line.hold(block_first)
    second.step()
    first = Gather(after(block_first, *second.slots))
    if pair == 2:
        other_c = line.take(other_c)[0]
        coming_c = to_low(other_c)

    w_second, vec, bias, lines_kept = second_tables(place, second.slots, rows, width)
    two, normed, hidden, grad_up, sums_middle, sums_back = [[None] * pair for _ in range(6)]

    def forward(z):
        two[z], normed[z], hidden[z], grad_up[z], sums_middle[z] = middle(
            place, z, tokens[z], grads[z], vec, w_second
        )

    def backward(z, attended, grad_qkv, w_first):
        keep, send, sums_back[z] = back(
            place, z, normed[z], hidden[z], grad_up[z], attended, grad_qkv, vec, w_second, w_first
        )
        return keep, [place.swap_low(send[o - 1][r], o) for o in lows for r in range(2)]

    def low_sum(keep, coming):
        coming = line.take(*coming)
        return jnp.stack(
            [sum([v.astype(F32) for v in coming[r::2]], keep[r].astype(F32)) for r in range(2)]
        )

    if pair == 2:
        grads.append([other_c, *line.take(*coming_c)])
        forward(1)
        keep, coming = backward(1, [], [], None)
    first.step(more=1)
    out_pieces, out_found, out_coming = [], [], []

    def next_piece():
        if out_coming:
            out_found.append(line.take(out_coming.pop())[0])
        if out_pieces:
            out_coming.append(place.swap_rep(after(out_pieces.pop(0), *line.ahead), 1))

    if pair == 2:
        line.pause()
        coming = line.take(*coming)
        sums = [
            sum(v.astype(F32) for v in [keep[r]] + list(coming[r::2])).astype(BF16) for r in range(2)
        ]
        cut = 3 * sums[0].shape[0] // 4
        out_pieces += [sums[0][:cut], jnp.concatenate([sums[0][cut:], sums[1]])]
        line.hold(*out_pieces)
        next_piece()
    forward(0)
    second_sums = Scatter(*second_grads(place, rows, two, grad_up, grads, hidden))

    next_piece()
    first.step()
    w_first, seen, cosine, sine = first_tables(place, first.slots, lines_kept, rows, width, span)
    one, heads = front(place, tokens[0], w_first, vec, bias, cosine, sine)
    attended, grad_qkv, sums_qkv = [[None] * place.groups for _ in range(3)]
    cot = grads[0]

    def attend(h):
        attended[h], grad_qkv[h], sums_qkv[h] = attention(
            place, h, span, *heads[h], cot, w_first, seen, cosine, sine
        )

    first_sums, counts = [], []

    def close(number, chosen):
        counts.append(len(chosen))
        first_sums.append(
            Scatter(
                *first_grads(
                    place, number, rows, one, cot,
                    [grad_qkv[h] for h in chosen], [attended[h] for h in chosen],
                )
            )
        )

    last_group = place.groups - 1
    for h in range(last_group):
        attend(h)
        if second_sums.phase >= 0:
            second_sums.step()
        if h == 1:
            next_piece()
    if last_group:
        close(0, list(range(last_group)))
    while second_sums.phase >= 0:
        second_sums.step()
    second_mine = second_sums.end()
    line.hold(second_mine)
    while out_coming:
        next_piece()
    second_reps = Pairs(second_mine) if pair == 2 else Reps(second_mine)
    attend(last_group)
    for v in first_sums:
        v.step()
    close(1, [last_group])
    keep, coming = backward(0, attended, grad_qkv, w_first)

    earlier, last = first_sums[:-1], first_sums[-1]
    for v in earlier:
        v.step()
    last.step()
    vector_sums = Scatter(
        *vector_grads(place, rows, 4 * place.heads * HD, sums_qkv, sums_back, sums_middle)
    )
    line.pause()
    reps = []
    for v in earlier:
        mine = v.end()
        line.hold(mine)
        reps.append(Reps(mine))
    while out_coming:
        next_piece()
    out_sum = low_sum(keep, coming)
    if pair == 2:
        out_sum = out_sum + jnp.concatenate(out_found).reshape(out_sum.shape).astype(F32)
    out_sum = out_sum.astype(BF16).reshape(2, seqs, span, width)
    line.hold(out_sum)
    blocks = [out_sum[:, s] for s in range(seqs)]

    def pass_on(phase):
        chosen = [s for s in range(seqs) if s >> phase & 1]
        got = place.swap_phase(jnp.stack([blocks[s] for s in chosen]), phase)
        return chosen, got

    def passed(chosen, got):
        got = line.take(got)[0]
        for k, s in enumerate(chosen):
            blocks[s] = got[k]

    going = pass_on(0)
    if pair == 2:
        second_reps.step()
    line.pause()
    vector_sums.step()
    last.step()
    line.pause()
    vector_sums.step()
    line.pause()
    mine = jnp.concatenate([last.end(), vector_sums.end()], axis=1)
    line.hold(mine)
    reps.append(Reps(mine))
    line.pause()
    for r in reps[:-1]:
        r.step()
        line.pause()
    reps[-1].step()
    for phase in range(1, place.phases):
        passed(*going)
        going = pass_on(phase)
    line.pause()
    for r in reps:
        while r.masks:
            r.step()
            line.pause()
    for r in reps:
        r.step()
    if pair == 1:
        while second_reps.masks:
            second_reps.step()
            line.pause()
        second_reps.step()
        line.pause()
    if pair == 2:
        pieces = [v[o] for v in second_reps.end() for o in range(low_count)]
    else:
        pieces = second_reps.end()
        pieces = jnp.where(even, pieces[0], pieces[1]), jnp.where(even, pieces[1], pieces[0])
        pieces = list(jnp.concatenate(pieces, axis=2))
    grad_w_up, grad_w_down = second_end(place, pieces)
    passed(*going)
    output, grad_input = finish_tokens(place, layer_input, cotangent, vec, blocks)
    pieces = [p for r in reps for p in r.end()]
    grad_w_qkv, grad_w_out, *vector_outs = first_end(place, rows, width, counts, pieces)
    return (
        output,
        grad_input,
        grad_w_qkv,
        grad_w_out,
        grad_w_up,
        grad_w_down,
        *vector_outs,
    )


def solution(mesh):
    tokens = P("rep", "fsdp", None)
    matrix = P("fsdp", None)
    vector = P("fsdp")
    return jax.shard_map(
        on_device,
        mesh=mesh,
        in_specs=(tokens, P("rep", "fsdp"), tokens) + (matrix,) * 4 + (vector,) * 8,
        out_specs=(tokens, tokens) + (matrix,) * 4 + (vector,) * 8,
        check_vma=False,
    )
```

```python
import functools

import jax
import jax.numpy as jnp
from jax import lax
from jax.experimental import pallas as pl
from jax.experimental.pallas import tpu as pltpu
from jax.sharding import PartitionSpec as P

H = 12
HD = 64
ROT = 16
TILE = 256
VEC = 16
COSTS = {
    "tables_second": 0.1,
    "middle_1": 0.1,
    "back_1": 0.1,
    "second_grads": 0.1,
    "back_0": 2,
    "vector_grads": 10,
    "second_end": 0.3,
    "pause_7": 0.3,
    "pause_8": 0.3,
    "pause_9": 0.3,
    "pause_10": 0.3,
    "pause_11": 0.3,
    "pause_12": 0.3,
    "pause_13": 0.3,
    "tables_first": 0.1,
    "front": 0.1,
}
DEFAULT = 20

EPS = 1e-05
NEG = -1e30

F32 = jnp.float32
BF16 = jnp.bfloat16
I32 = jnp.int32

NN = ((1,), (0,))
NT = ((1,), (1,))
TN = ((0,), (0,))


def dot(a, b, dims):
    return lax.dot_general(a, b, (dims, ((), ())), preferred_element_type=F32)


def at(start, size, multiple):
    return pl.ds(pl.multiple_of(start, multiple), size)


class Place:
    def __init__(self, seqs, shards, reps):
        self.seqs, self.shards, self.reps = seqs, shards, reps
        self.low_count = shards // seqs
        self.pair = 2 if reps % 2 == 0 and H % (2 * self.low_count) == 0 else 1
        self.parts = self.pair * self.low_count
        self.line = Line()
        self.heads = 2 if H // self.low_count % 2 == 0 else 3
        self.groups = H // self.low_count // self.heads
        self.masks = []
        while 2 ** len(self.masks) < seqs:
            self.masks.append(2 ** len(self.masks))
        self.phases = len(self.masks)

    def chip(self):
        return lax.axis_index("fsdp") // self.low_count

    def low(self):
        return lax.axis_index("fsdp") % self.low_count

    def part(self):
        return (lax.axis_index("rep") % self.pair) * self.low_count + self.low()

    def owner(self, slot):
        even = sum(self.masks[p] for p in range(self.phases) if slot >> p & 1)
        odd = sum(self.masks[self.phases - 1 - p] for p in range(self.phases) if slot >> p & 1)
        if even == odd:
            return self.chip() ^ even
        return self.chip() ^ jnp.where(lax.axis_index("fsdp") % 2 == 0, even, odd)

    def slot(self, block):
        j = (block // self.low_count) ^ self.chip()
        other = sum((j >> p & 1) << (self.phases - 1 - p) for p in range(self.phases))
        even = lax.axis_index("fsdp") % 2 == 0 if self.low_count == 1 else block % self.low_count % 2 == 0
        return jnp.where(even, j, other)

    def swap_low(self, v, mask):
        return lax.ppermute(v, "fsdp", [(i, i ^ mask) for i in range(self.shards)])

    def swap_slot(self, v, slot):
        def to(i):
            order = self.masks if i % 2 == 0 else self.masks[::-1]
            return i ^ (sum(m for p, m in enumerate(order) if slot >> p & 1) * self.low_count)

        return lax.ppermute(v, "fsdp", [(i, to(i)) for i in range(self.shards)])

    def swap_phase(self, v, phase):
        def to(i):
            mask = self.masks[phase] if i % 2 == 0 else self.masks[self.phases - 1 - phase]
            return i ^ (mask * self.low_count)

        return lax.ppermute(v, "fsdp", [(i, to(i)) for i in range(self.shards)])

    def swap_rep(self, v, mask):
        return lax.ppermute(v, "rep", [(i, i ^ mask) for i in range(self.reps)])


def after(v, *others):
    return lax.optimization_barrier((v, *others))[0]


def whole(shape):
    return pl.BlockSpec(shape, lambda *_: (0,) * len(shape))


def pause_kernel(source, out):
    out[...] = source[...] + 1.0


class Line:
    def __init__(self):
        self.ahead = []
        self.count = jnp.zeros((8, 128), F32)
        self.pauses = 0

    def take(self, *arrays):
        found = lax.optimization_barrier((*arrays, *self.ahead))[: len(arrays)]
        self.ahead = [min(found, key=lambda v: v.size)]
        return found

    def hold(self, *arrays):
        self.ahead.extend(arrays)

    def pause(self):
        small = jax.ShapeDtypeStruct((8, 128), F32)
        block = whole(small.shape)
        self.pauses += 1
        name = f"pause_{self.pauses}"
        self.count = self.call(pause_kernel, name, (1,), [block], block, small, [], [self.count], 4)

    def call(self, kernel, name, grid, in_specs, out_specs, out_shape, scratch, args, vmem=40):
        args = list(args)
        if self.ahead:
            args[0] = after(args[0], *self.ahead)
        outs = pl.pallas_call(
            kernel,
            grid=grid,
            in_specs=in_specs,
            out_specs=out_specs,
            out_shape=out_shape,
            scratch_shapes=scratch,
            compiler_params=pltpu.CompilerParams(vmem_limit_bytes=vmem * 2**20),
            cost_estimate=pl.CostEstimate(
                flops=(cost := int(COSTS.get(name, DEFAULT) * 1.15e9)),
                bytes_accessed=int(cost // 320),
                transcendentals=0,
            ),
            name=name,
        )(*args)
        self.ahead = [min(jax.tree.leaves(outs), key=lambda v: v.size)]
        return outs


def split_kernel(place, source, *outs):
    for j, out in enumerate(outs):
        out[...] = source[place.owner(j)]


def split_tokens(place, v, name):
    seqs, span, width = v.shape
    return place.line.call(
        functools.partial(split_kernel, place),
        name,
        (1,),
        [whole(v.shape)],
        [whole((span, width))] * seqs,
        [jax.ShapeDtypeStruct((span, width), v.dtype)] * seqs,
        [],
        (v,),
        vmem=58,
    )


def weights_kernel(place, w_qkv, w_out, w_up, w_down, *rest):
    vectors, pos, outs = rest[:8], rest[8], rest[9:]
    rows = w_qkv.shape[0]
    parts, low_count = place.parts, place.low_count
    width = w_out.shape[1]
    step = place.heads * HD
    hidden = w_up.shape[1] // parts
    firsts, seconds = outs[:low_count], outs[low_count:]
    for k in range(low_count):

        @pl.when(place.low() == k)
        def _():
            for o in range(low_count):
                for h in range(place.groups):
                    begin = ((k ^ o) * place.groups + h) * step
                    for g in range(3):
                        to = (3 * h + g) * step
                        firsts[o][:, to : to + step] = w_qkv[
                            :, g * width + begin : g * width + begin + step
                        ]
                    to = (3 * place.groups + h) * step
                    firsts[o][:, to : to + step] = w_out[:, begin : begin + step]

    for o in range(low_count):
        lanes = at((place.part() ^ o) * hidden, hidden, 128)
        seconds[o][:rows, :hidden] = w_up[:, lanes]
        seconds[o][:rows, hidden:] = w_down[:, lanes]

    lanes = seconds[0].shape[1]
    lines = []
    for v in vectors:
        lines.append(
            jnp.concatenate([v[...].astype(F32), jnp.zeros((1, lanes - v.shape[1]), F32)], axis=1)
        )
    span = pos.shape[1]
    for values in (
        [(pos[s : s + 1, :] // 64).astype(F32) for s in range(pos.shape[0])],
        [(pos[s : s + 1, :] % 64).astype(F32) for s in range(pos.shape[0])],
    ):
        lines.append(
            jnp.concatenate(values + [jnp.zeros((1, lanes - span * pos.shape[0]), F32)], axis=1)
        )
    lines.append(jnp.zeros((VEC - len(lines), lanes), F32))
    block = jnp.concatenate(lines, axis=0).astype(BF16)
    for o in range(low_count):
        seconds[o][rows:, :] = block


def split_weights(place, w_qkv, w_out, w_up, w_down, vectors, pos):
    rows = w_qkv.shape[0]
    args = [w_qkv, w_out, w_up, w_down] + [v.reshape(1, -1) for v in vectors] + [pos]
    first = (rows, (w_qkv.shape[1] + w_out.shape[1]) // place.low_count)
    second = (rows + VEC, (w_up.shape[1] + w_down.shape[1]) // place.parts)
    shapes = [first] * place.low_count + [second] * place.low_count
    outs = place.line.call(
        functools.partial(weights_kernel, place),
        "split_weights",
        (1,),
        [whole(v.shape) for v in args],
        [whole(s) for s in shapes],
        [jax.ShapeDtypeStruct(s, BF16) for s in shapes],
        [],
        args,
        vmem=58,
    )
    return outs[: place.low_count], outs[place.low_count :]


def second_tables_kernel(place, rows, *rest):
    slots = rest[: place.seqs]
    w_out, vec_out, bias, lines_kept = rest[place.seqs :]
    seqs, low_count, parts = place.seqs, place.low_count, place.parts
    block = rows + VEC
    width = w_out.shape[0]
    step = place.heads * HD
    low = place.low()
    for s in range(seqs):
        owner = place.owner(s)
        for o in range(low_count):
            found = slots[s][o * block : (o + 1) * block, :]
            l = low ^ o
            w_out[at((owner * low_count + l) * rows, rows, 16), :] = found[:rows]
            lines_kept[owner * low_count + l] = found[rows:].astype(F32)

    def line(row, size):
        return jnp.concatenate(
            [lines_kept[n, row : row + 1, :size] for n in range(place.shards)], axis=1
        )

    for row in range(4):
        vec_out[row : row + 1, :] = line(row, rows)
    vec_out[4:5, :] = line(5, rows) + line(7, rows)
    all_up = line(6, 4 * rows)
    all_qkv = line(4, 3 * rows)
    for k in range(parts):

        @pl.when(place.part() == k)
        def _():
            vec_out[5:6, :] = all_up[:, k * width : (k + 1) * width]

    for k in range(low_count):

        @pl.when(low == k)
        def _():
            for h in range(place.groups):
                for g in range(3):
                    begin = g * width + (k * place.groups + h) * step
                    bias[h : h + 1, g * step : (g + 1) * step] = all_qkv[:, begin : begin + step]

    vec_out[6:, :] = jnp.zeros((2, width), F32)


def second_tables(place, slots, rows, width):
    shapes = [
        jax.ShapeDtypeStruct((width, slots[0].shape[1]), BF16),
        jax.ShapeDtypeStruct((8, width), F32),
        jax.ShapeDtypeStruct((8, 3 * place.heads * HD), F32),
        jax.ShapeDtypeStruct((place.shards, VEC, slots[0].shape[1]), F32),
    ]
    return place.line.call(
        functools.partial(second_tables_kernel, place, rows),
        "tables_second",
        (1,),
        [whole(v.shape) for v in slots],
        [whole(v.shape) for v in shapes],
        shapes,
        [],
        slots,
        vmem=40,
    )


def first_tables_kernel(place, rows, span, inverse, lines_kept, *rest):
    slots = rest[: place.seqs]
    w_out, first_out, cos_out, sin_out = rest[place.seqs :]
    low_count = place.low_count
    low, chip = place.low(), place.chip()
    for s in range(place.seqs):
        owner = place.owner(s)
        for o in range(low_count):
            w_out[at((owner * low_count + (low ^ o)) * rows, rows, 16), :] = slots[s][
                o * rows : (o + 1) * rows, :
            ]
    still = jnp.zeros((HD - ROT, span), F32)
    for f in range(place.shards):
        lanes = at(chip * span, span, 128)
        value = lines_kept[f, 8:9, lanes] * 64.0 + lines_kept[f, 9:10, lanes]
        index = f * span + lax.broadcasted_iota(I32, (1, span), 1)
        first_out[:, f * span : (f + 1) * span] = index - value.astype(I32)
        phase = inverse[...] * value
        cosine, sine = jnp.cos(phase), jnp.sin(phase)
        crel, j = (f % low_count) ^ low, place.slot(f)
        to = at(j * span, span, 128)
        cos_out[crel, to, :] = jnp.concatenate([cosine, cosine, still + 1.0] * 2, axis=0).T
        sin_out[crel, to, :] = jnp.concatenate([-sine, sine, still] * 2, axis=0).T


def first_tables(place, slots, lines_kept, rows, width, span):
    inverse = (10000.0 ** (-jnp.arange(0, ROT, 2, dtype=F32) / ROT)).reshape(-1, 1)
    shapes = [
        jax.ShapeDtypeStruct((width, slots[0].shape[1]), BF16),
        jax.ShapeDtypeStruct((1, place.shards * span), I32),
        jax.ShapeDtypeStruct((place.low_count, place.seqs * span, 128), F32),
        jax.ShapeDtypeStruct((place.low_count, place.seqs * span, 128), F32),
    ]
    args = [inverse, lines_kept] + slots
    return place.line.call(
        functools.partial(first_tables_kernel, place, rows, span),
        "tables_first",
        (1,),
        [whole(v.shape) for v in args],
        [whole(v.shape) for v in shapes],
        shapes,
        [],
        args,
        vmem=16,
    )


def piece_specs(pieces, lines):
    split = pieces[0].shape[0] // lines

    def spec(i, width):
        return pl.BlockSpec(
            (lines, width), lambda g: (jnp.clip(g - i * split, 0, split - 1), 0)
        )

    return [spec(i, v.shape[1]) for i, v in enumerate(pieces)]


def piece_now(refs, steps):
    found = refs[0][...]
    for i in range(1, len(refs)):
        found = jnp.where(pl.program_id(0) >= i * (steps // len(refs)), refs[i][...], found)
    return found


def norm(source):
    source = source.astype(F32)
    centred = source - jnp.mean(source, axis=1, keepdims=True)
    return centred * lax.rsqrt(jnp.mean(centred * centred, axis=1, keepdims=True) + EPS)


def turned(v):
    half = ROT // 2
    columns = v.shape[1]
    lane = lax.broadcasted_iota(I32, v.shape, 1) % HD
    ahead = pltpu.roll(v, columns - half, 1)
    behind = pltpu.roll(v, half, 1)
    return jnp.where(lane < half, ahead, behind)


def front_kernel(place, steps, *refs):
    tokens, refs = refs[: place.low_count], refs[place.low_count :]
    weight, vec, bias, cosine, sine, one_out, *outs = refs
    step = place.heads * HD
    one = (norm(piece_now(tokens, steps)) * vec[0:1, :] + vec[1:2, :]).astype(BF16)
    one_out[0] = one
    copies = 2 * step // 128
    cos_cols = jnp.concatenate([cosine[0]] * copies, axis=1)
    sin_cols = jnp.concatenate([sine[0]] * copies, axis=1)
    for h in range(place.groups):
        q_out, k_out, v_out = outs[3 * h : 3 * h + 3]
        qkv = dot(one, weight[:, 3 * step * h : 3 * step * (h + 1)], NN) + bias[h : h + 1, :]
        both = qkv[:, : 2 * step]
        both = both * cos_cols + turned(both) * sin_cols
        q_out[0] = both[:, :step].astype(BF16)
        k_out[0] = both[:, step:].astype(BF16)
        v_out[0] = qkv[:, 2 * step :].astype(BF16)


def front(place, tokens, weight, vec, bias, cosine, sine):
    groups = len(tokens)
    count, width = tokens[0].shape
    step = place.heads * HD
    split = 2
    lines = count // split
    by_step = lambda cols: pl.BlockSpec((1, lines, cols), lambda g: (g // split, g % split, 0))
    shaped = lambda cols: jax.ShapeDtypeStruct((groups, count, cols), BF16)
    outs = place.line.call(
        functools.partial(front_kernel, place, groups * split),
        "front",
        (groups * split,),
        piece_specs(tokens, lines)
        + [whole(weight.shape), whole(vec.shape), whole(bias.shape)] + [by_step(128)] * 2,
        [by_step(width)] + [by_step(step)] * (3 * place.groups),
        [shaped(width)] + [shaped(step)] * (3 * place.groups),
        [],
        [*tokens, weight, vec, bias, cosine, sine],
        vmem=20,
    )
    return outs[0], [outs[1 + 3 * h : 4 + 3 * h] for h in range(place.groups)]


def middle_kernel(count, steps, *refs):
    tokens, grads, refs = refs[:count], refs[count : 2 * count], refs[2 * count :]
    vec, weight, two_out, normed_out, hidden_out, grad_out, sums = refs

    @pl.when(pl.program_id(0) == 0)
    def _():
        sums[...] = jnp.zeros_like(sums)

    width = weight.shape[0]
    normed = norm(piece_now(tokens, steps))
    normed_out[0] = normed.astype(BF16)
    two = (normed * vec[2:3, :] + vec[3:4, :]).astype(BF16)
    two_out[0] = two
    up = dot(two, weight[:, :width], NN) + vec[5:6, :]
    grad = piece_now(grads, steps)
    grad_hidden = dot(grad, weight[:, width:], NN)
    bell = jnp.exp(-0.5 * up * up)
    below = 1.0 + (0.3275911 * 0.5**0.5) * jnp.abs(up)
    t = pl.reciprocal(below, approx=True)
    t = t * (2.0 - below * t)
    series = t * (
        0.127414796 + t * (-0.142248368 + t * (0.7107068705 + t * (-0.7265760135 + t * 0.5307027145)))
    )
    tail = series * bell
    share = jnp.where(up >= 0.0, 1.0 - tail, tail)
    hidden_out[0] = (up * share).astype(BF16)
    slope = share + up * (bell * 0.3989422804014327)
    grad_up = (grad_hidden * slope).astype(BF16)
    grad_out[0] = grad_up
    sums[0:1, :] += jnp.sum(grad_up.astype(F32), axis=0, keepdims=True)
    sums[1:2, :] += jnp.sum(grad.astype(F32), axis=0, keepdims=True)


def middle(place, z, tokens, grads, vec, weight):
    groups = len(tokens)
    count, width = tokens[0].shape
    split = 2
    lines = count // split
    by_step = pl.BlockSpec((1, lines, width), lambda g: (g // split, g % split, 0))
    return place.line.call(
        functools.partial(middle_kernel, groups, groups * split),
        f"middle_{z}",
        (groups * split,),
        piece_specs(tokens, lines)
        + piece_specs(grads, lines)
        + [whole(vec.shape), whole(weight.shape)],
        [by_step] * 4 + [whole((8, width))],
        [jax.ShapeDtypeStruct((groups, count, width), BF16)] * 4 + [jax.ShapeDtypeStruct((8, width), F32)],
        [],
        [*tokens, *grads, vec, weight],
        vmem=20,
    )


def attention_kernel(
    place, group, span, q_in, k_in, v_in, w_in, first_in, cos_in, sin_in, *refs
):
    cot_in, refs = refs[: place.low_count], refs[place.low_count :]
    o_out, g_out, sums, qs, ks, vs, gs, o_turned, gq_turned, gk_sum, gv_sum = refs
    low_count = place.low_count
    count, columns = q_in.shape[1:]
    heads = columns // HD
    length = low_count * count
    begin = (3 * place.groups + group) * columns
    w_out = w_in[:, begin : begin + columns]

    def slot(f):
        crel = (f % low_count) ^ place.low()
        j = place.slot(f)
        return crel, at(j * span, span, 128)

    for f in range(length // span):
        to = slice(f * span, (f + 1) * span)
        crel, lines = slot(f)
        for source, kept in ((q_in, qs), (k_in, ks), (v_in, vs)):
            found = source[crel, lines, :]
            for h in range(heads):
                kept[h, to, :] = found[:, h * HD : (h + 1) * HD]
        cot = cot_in[0][lines, :]
        for o in range(1, low_count):
            cot = jnp.where(crel == o, cot_in[o][lines, :], cot)
        found = dot(cot, w_out, NN).astype(BF16)
        for h in range(heads):
            gs[h, to, :] = found[:, h * HD : (h + 1) * HD]

    def one_head(h, carry):
        keys = ks[h]
        values = vs[h]
        keys_turned = keys.astype(F32).T.astype(BF16)
        values_turned = values.astype(F32).T.astype(BF16)
        for i in range(length // TILE):
            here = slice(i * TILE, (i + 1) * TILE)
            query = qs[h, here, :]
            grad = gs[h, here, :]
            first = first_in[:, here]
            tiles = [slice(j * TILE, (j + 1) * TILE) for j in range(i + 1)]
            scores, grads = [], []
            for j, tile in enumerate(tiles):
                raw = dot(keys[tile], query, NT) * (0.125 * 1.4426950408889634)
                key_index = j * TILE + lax.broadcasted_iota(I32, (TILE, TILE), 0)
                seen = key_index >= first
                if j == i:
                    query_index = i * TILE + lax.broadcasted_iota(I32, (TILE, TILE), 1)
                    seen = seen & (key_index <= query_index)
                scores.append(jnp.where(seen, raw, NEG))
            top = functools.reduce(
                jnp.maximum, [jnp.max(raw, axis=0, keepdims=True) for raw in scores]
            )
            weights = [jnp.exp2(raw - top) for raw in scores]
            share = 1.0 / sum(jnp.sum(w, axis=0, keepdims=True) for w in weights)
            grads = [dot(values[tile], grad, NT) for tile in tiles]
            carried = share * sum(
                jnp.sum(w * g, axis=0, keepdims=True) for w, g in zip(weights, grads)
            )
            out, gq = None, None
            for j, tile in enumerate(tiles):
                probs = weights[j] * share
                low = probs.astype(BF16)
                grad_scores = (probs * (grads[j] - carried)).astype(BF16)
                out_part = dot(values_turned[:, tile], low, NN)
                gq_part = dot(keys_turned[:, tile], grad_scores, NN)
                gk_part = dot(grad_scores, query, NN)
                gv_part = dot(low, grad, NN)
                out = out_part if j == 0 else out + out_part
                gq = gq_part if j == 0 else gq + gq_part
                if j < i:
                    gk_sum[h, tile, :] += gk_part
                    gv_sum[h, tile, :] += gv_part
                else:
                    gk_sum[h, tile, :] = gk_part
                    gv_sum[h, tile, :] = gv_part
            o_turned[h, :, here] = out
            gq_turned[h, :, here] = gq
        return carry

    lax.fori_loop(0, heads, one_head, 0)
    total = jnp.zeros((1, 3 * columns), F32)
    for f in range(length // span):
        crel, lines = slot(f)
        to = slice(f * span, (f + 1) * span)
        o_out[crel, lines, :] = jnp.concatenate(
            [o_turned[h, :, to].T for h in range(heads)], axis=1
        ).astype(BF16)
        both = jnp.concatenate(
            [gq_turned[h, :, to].T for h in range(heads)] + [gk_sum[h, to, :] for h in range(heads)],
            axis=1,
        )
        both = both * 0.125
        copies = 2 * columns // 128
        cos_cols = jnp.concatenate([cos_in[crel, lines, :]] * copies, axis=1)
        sin_cols = jnp.concatenate([sin_in[crel, lines, :]] * copies, axis=1)
        both = both * cos_cols - turned(both) * sin_cols
        value = jnp.concatenate([gv_sum[h, to, :] for h in range(heads)], axis=1)
        grad = jnp.concatenate([both, value], axis=1).astype(BF16)
        g_out[crel, lines, :] = grad
        total = total + jnp.sum(grad.astype(F32), axis=0, keepdims=True)
    sums[...] = jnp.concatenate([total, jnp.zeros((7, 3 * columns), F32)], axis=0)


def attention(place, group, span, q, k, v, cot, w, first, cosine, sine):
    count, columns = q.shape[1:]
    low_count = place.low_count
    heads = columns // HD
    length = low_count * count
    outs = [
        jax.ShapeDtypeStruct((low_count, count, columns), BF16),
        jax.ShapeDtypeStruct((low_count, count, 3 * columns), BF16),
        jax.ShapeDtypeStruct((8, 3 * columns), F32),
    ]
    args = [q, k, v, w, first, cosine, sine, *cot]
    return place.line.call(
        functools.partial(attention_kernel, place, group, span),
        f"attention_{group}",
        (1,),
        [whole(a.shape) for a in args],
        [whole(a.shape) for a in outs],
        outs,
        [pltpu.VMEM((heads, length, HD), BF16)] * 4
        + [pltpu.VMEM((heads, HD, length), F32)] * 2
        + [pltpu.VMEM((heads, length, HD), F32)] * 2,
        args,
        vmem=16 * (length // 1024),
    )


def back_kernel(place, groups, *refs):
    normed, hidden, grad_up = refs[:3]
    attended, grad_qkv = refs[3 : 3 + groups], refs[3 + groups : 3 + 2 * groups]
    vec, second = refs[3 + 2 * groups : 5 + 2 * groups]
    keep, send, sums = refs[-3:]
    step = pl.program_id(0)
    width = normed.shape[2]

    @pl.when(step == 0)
    def _():
        sums[...] = jnp.zeros_like(sums)

    two = dot(grad_up[0], second[:, :width], NT)
    out = dot(hidden[0], second[:, width:], NT)
    both = two * vec[2:3, :]
    source = normed[0].astype(F32)
    sums[2:3, :] += jnp.sum(two * source, axis=0, keepdims=True)
    sums[3:4, :] += jnp.sum(two, axis=0, keepdims=True)
    if groups:
        first = refs[5 + 2 * groups]
        cols = place.heads * HD
        one = None
        for h in range(groups):
            term = dot(grad_qkv[h][0], first[:, 3 * cols * h : 3 * cols * (h + 1)], NT)
            one = term if one is None else one + term
            begin = (3 * groups + h) * cols
            out = out + dot(attended[h][0], first[:, begin : begin + cols], NT)
        both = both + one * vec[0:1, :]
        sums[0:1, :] += jnp.sum(one * source, axis=0, keepdims=True)
        sums[1:2, :] += jnp.sum(one, axis=0, keepdims=True)
    split = pl.num_programs(0) // place.low_count

    @pl.when(step < split)
    def _():
        keep[0] = out.astype(BF16)
        keep[1] = both.astype(BF16)

    @pl.when(step >= split)
    def _():
        send[0, 0] = out.astype(BF16)
        send[0, 1] = both.astype(BF16)


def back(place, z, normed, hidden, grad_up, attended, grad_qkv, vec, second, first):
    low_count = place.low_count
    groups, count, width = normed.shape
    split = 2
    lines = count // split
    by_step = lambda cols: pl.BlockSpec((1, lines, cols), lambda g: (g // split, g % split, 0))
    args = [normed, hidden, grad_up, *attended, *grad_qkv]
    fixed = [vec, second] + ([first] if attended else [])

    def sent(g):
        later = jnp.maximum(g - split, 0)
        return (later // split, 0, later % split, 0)

    return place.line.call(
        functools.partial(back_kernel, place, len(attended)),
        f"back_{z}",
        (groups * split,),
        [by_step(v.shape[2]) for v in args] + [whole(v.shape) for v in fixed],
        [
            pl.BlockSpec((2, lines, width), lambda g: (0, jnp.minimum(g, split - 1), 0)),
            pl.BlockSpec((1, 2, lines, width), sent),
            whole((8, width)),
        ],
        [
            jax.ShapeDtypeStruct((2, count, width), BF16),
            jax.ShapeDtypeStruct((low_count - 1, 2, count, width), BF16),
            jax.ShapeDtypeStruct((8, width), F32),
        ],
        [],
        args + fixed,
        vmem=24,
    )


def store_rows(place, rows, block, value, scratch, columns):
    low_count = place.low_count
    for s in range(place.seqs):
        owner = place.owner(s)
        for o in range(low_count):
            begin = owner * (low_count * rows) + (place.low() ^ o) * rows
            scratch[s, o * block : o * block + rows, columns] = value[at(begin, rows, 16), :].astype(BF16)


def product(lefts, rights):
    each = len(lefts) // len(rights)
    total = None
    for i, left in enumerate(lefts):
        lines = left.shape[0]
        right = rights[i // each][(i % each) * lines : (i % each + 1) * lines, :]
        term = dot(left[...], right, TN)
        total = term if total is None else total + term
    return total


def second_grads_kernel(place, rows, count, *refs):
    two, grad_up, hidden = [refs[k * count : (k + 1) * count] for k in range(3)]
    cot, (keep, send, total, turned_rows) = refs[3 * count : -4], refs[-4:]
    step = pl.program_id(0)
    width = two[0].shape[1]
    half = place.seqs // 2

    def one(left, right, columns):
        total[...] = product(left, right)
        store_rows(place, rows, rows, total, turned_rows, columns)

    @pl.when(step == 0)
    def _():
        one(two, grad_up, slice(0, width))

    @pl.when(step == 1)
    def _():
        one(cot, hidden, slice(width, 2 * width))
        keep[...] = turned_rows[:half]
        send[...] = turned_rows[half:]


def second_grads(place, rows, two, grad_up, cot, hidden):
    width = two[0].shape[2]
    flat = [v.reshape(-1, width) for v in (*two, *grad_up, *hidden)] + [p for c in cot for p in c]
    half = (place.seqs // 2, place.low_count * rows, 2 * width)
    return place.line.call(
        functools.partial(second_grads_kernel, place, rows, len(two)),
        "second_grads",
        (2,),
        [whole(v.shape) for v in flat],
        [whole(half)] * 2,
        [jax.ShapeDtypeStruct(half, BF16)] * 2,
        [pltpu.VMEM((width, width), F32), pltpu.VMEM((2 * half[0],) + half[1:], BF16)],
        flat,
        vmem=20,
    )


def first_grads_kernel(place, rows, count, one, *refs):
    grad_qkv, attended, refs = refs[:count], refs[count : 2 * count], refs[2 * count :]
    cot, (keep, send, total, ordered) = refs[:-4], refs[-4:]
    half = place.seqs // 2
    step = place.heads * HD
    for h in range(count):
        total[:, : 3 * step] = dot(one[...], grad_qkv[h][...], TN)
        total[:, 3 * step :] = product(cot, [attended[h]])
        store_rows(place, rows, rows, total, ordered, slice(4 * step * h, 4 * step * (h + 1)))
    keep[...] = ordered[:half]
    send[...] = ordered[half:]


def first_grads(place, number, rows, one, cot, grad_qkv, attended):
    width = one.shape[2]
    step = place.heads * HD
    count = len(attended)
    args = [v.reshape(-1, v.shape[2]) for v in (one, *grad_qkv, *attended)] + list(cot)
    half = (place.seqs // 2, place.low_count * rows, 4 * step * count)
    return place.line.call(
        functools.partial(first_grads_kernel, place, rows, count),
        f"first_grads_{number}",
        (1,),
        [whole(v.shape) for v in args],
        [whole(half)] * 2,
        [jax.ShapeDtypeStruct(half, BF16)] * 2,
        [pltpu.VMEM((width, 4 * step), F32), pltpu.VMEM((2 * half[0],) + half[1:], BF16)],
        args,
        vmem=16,
    )


def vectors_kernel(place, rows, *refs):
    sums_qkv = refs[: place.groups]
    sums_back = refs[place.groups : place.groups + place.pair]
    sums_middle = refs[place.groups + place.pair : -4]
    keep, send, lines_kept, ordered = refs[-4:]
    seqs, low_count, parts = place.seqs, place.low_count, place.parts
    width = keep.shape[2]
    step = place.heads * HD
    half = seqs // 2
    back = sum(s[...] for s in sums_back)
    up = sum(s[0:1, :] for s in sums_middle)
    grad = sums_middle[0][1:2, :] * (1.0 / low_count)
    zero = jnp.zeros((1, step), F32)
    all_qkv = jnp.concatenate(
        [
            jnp.where(place.low() == k, sums_qkv[h][0:1, g * step : (g + 1) * step], zero)
            for g in range(3)
            for k in range(low_count)
            for h in range(place.groups)
        ],
        axis=1,
    )
    all_up = jnp.concatenate([jnp.where(place.part() == k, up, 0.0) for k in range(parts)], axis=1)
    lines = [(back[r : r + 1], rows) for r in range(4)]
    lines += [(all_qkv, 3 * rows), (grad, rows), (all_up, 4 * rows)]
    for n in range(place.shards):
        made = [
            jnp.concatenate(
                [v[:, n * size : (n + 1) * size], jnp.zeros((1, width - size), F32)], axis=1
            )
            for v, size in lines
        ]
        made.append(jnp.zeros((VEC - len(made), width), F32))
        lines_kept[n] = jnp.concatenate(made, axis=0)
    for s in range(seqs):
        for o in range(low_count):
            n = place.owner(s) * low_count + (place.low() ^ o)
            ordered[s, o * VEC : (o + 1) * VEC, :] = lines_kept[n].astype(BF16)
    keep[...] = ordered[:half]
    send[...] = ordered[half:]


def vector_grads(place, rows, width, sums_qkv, sums_back, sums_middle):
    half = (place.seqs // 2, place.low_count * VEC, width)
    args = [*sums_qkv, *sums_back, *sums_middle]
    return place.line.call(
        functools.partial(vectors_kernel, place, rows),
        "vector_grads",
        (1,),
        [whole(v.shape) for v in args],
        [whole(half)] * 2,
        [jax.ShapeDtypeStruct(half, BF16)] * 2,
        [
            pltpu.VMEM((place.shards, VEC, width), F32),
            pltpu.VMEM((2 * half[0],) + half[1:], BF16),
        ],
        args,
        vmem=16,
    )


def tokens_kernel(place, source, cot, vec, *rest):
    blocks, (out, grad_in) = rest[: place.seqs], rest[place.seqs :]
    for j in range(place.seqs):
        s = place.owner(j)
        x = source[s].astype(F32)
        out[s] = (x + blocks[j][0].astype(F32) + vec[4:5, :]).astype(BF16)
        mean = jnp.mean(x, axis=1, keepdims=True)
        centred = x - mean
        scale = lax.rsqrt(jnp.mean(centred * centred, axis=1, keepdims=True) + EPS)
        normed = centred * scale
        e = blocks[j][1].astype(F32)
        pulled = (
            e
            - jnp.mean(e, axis=1, keepdims=True)
            - normed * jnp.mean(e * normed, axis=1, keepdims=True)
        ) * scale
        grad_in[s] = (cot[s].astype(F32) + pulled).astype(BF16)


def finish_tokens(place, source, cot, vec, blocks):
    return place.line.call(
        functools.partial(tokens_kernel, place),
        "finish_tokens",
        (1,),
        [whole(source.shape)] * 2 + [whole(vec.shape)] + [whole(b.shape) for b in blocks],
        [whole(source.shape)] * 2,
        [jax.ShapeDtypeStruct(source.shape, BF16)] * 2,
        [],
        [source, cot, vec] + blocks,
    )


def first_end_kernel(place, rows, counts, *refs):
    found, refs = refs[: 2 * len(counts)], refs[2 * len(counts) + 1 :]
    w_qkv, w_out, vectors = refs[0], refs[1], refs[2:]
    low_count, groups = place.low_count, place.groups
    width = w_out.shape[1]
    step = place.heads * HD
    even = (lax.axis_index("rep") % 2) == 0
    total = None
    first = 0
    for i, count in enumerate(counts):
        for o in range(low_count):
            mine, other = found[2 * i][o].astype(F32), found[2 * i + 1][o].astype(F32)
            piece = jnp.concatenate(
                [jnp.where(even, mine, other), jnp.where(even, other, mine)], axis=1
            )
            for k in range(low_count):

                @pl.when(place.low() == k)
                def _():
                    for h in range(count):
                        begin = ((k ^ o) * groups + first + h) * step
                        for g in range(3):
                            to = g * width + begin
                            part = (4 * h + g) * step
                            w_qkv[:, to : to + step] = piece[:rows, part : part + step]
                        part = (4 * h + 3) * step
                        w_out[:, begin : begin + step] = piece[:rows, part : part + step]

            if i == len(counts) - 1:
                total = piece[rows:] if total is None else total + piece[rows:]
        first += count
    for r, out in enumerate(vectors):
        out[...] = total[5 if r == 7 else r, : out.shape[0]]


def first_end(place, rows, width, counts, pieces):
    shapes = [(rows, 3 * width), (rows, width)]
    shapes += [(n * rows,) for n in (1, 1, 1, 1, 3, 1, 4, 1)]
    pieces = pieces + [place.line.count]
    return place.line.call(
        functools.partial(first_end_kernel, place, rows, counts),
        "first_end",
        (1,),
        [whole(p.shape) for p in pieces],
        [whole(v) for v in shapes],
        [jax.ShapeDtypeStruct(v, F32) for v in shapes],
        [],
        pieces,
    )


def second_end_kernel(place, *refs):
    pieces = refs[: place.parts]
    w_up, w_down = refs[place.parts :]
    parts = place.parts
    step = w_up.shape[1] // parts
    for r in range(parts):
        t = place.part() ^ r
        w_up[:, at(t * step, step, 128)] = pieces[r][:, :step].astype(F32)
        w_down[:, at(t * step, step, 128)] = pieces[r][:, step:].astype(F32)


def second_end(place, pieces):
    rows, columns = pieces[0].shape
    shape = (rows, columns // 2 * place.parts)
    return place.line.call(
        functools.partial(second_end_kernel, place),
        "second_end",
        (1,),
        [whole(p.shape) for p in pieces],
        [whole(shape)] * 2,
        [jax.ShapeDtypeStruct(shape, F32)] * 2,
        [],
        pieces,
    )


def add(a, b):
    return (a.astype(F32) + b.astype(F32)).astype(BF16)


def on_device(
    layer_input,
    positions,
    cotangent,
    w_qkv,
    w_out,
    w_up,
    w_down,
    ln1_gain,
    ln1_bias,
    ln2_gain,
    ln2_bias,
    qkv_bias,
    out_bias,
    up_bias,
    down_bias,
):
    seqs, span, width = layer_input.shape
    place = Place(seqs, lax.axis_size("fsdp"), lax.axis_size("rep"))
    low_count, pair = place.low_count, place.pair
    rows = w_qkv.shape[0]

    line = place.line
    lows = range(1, low_count)

    def to_low(v):
        return [place.swap_low(v, o) for o in lows]

    class Gather:
        def __init__(self, block):
            self.slots = [block]
            self.coming = [[place.swap_phase(block, p)] for p in range(place.phases)]

        def step(self, more=0):
            count = len(self.coming[0])
            ahead = self.coming[1][:more] if more else []
            got = line.take(*self.coming.pop(0), *ahead)
            if more:
                self.coming[0][:more] = got[count:]
            for later, p in zip(self.coming, range(place.phases - len(self.coming), place.phases)):
                later.extend(place.swap_phase(v, p) for v in got[:count])
            self.slots.extend(got[:count])

    class Scatter:
        def __init__(self, keep, send):
            self.phase = place.phases - 1
            self.kept = [keep[s] for s in range(keep.shape[0])]
            self.got = place.swap_phase(send, self.phase)

        def step(self):
            got = line.take(self.got)[0]
            self.phase -= 1
            half = len(self.kept) // 2
            sums = [add(v, got[s]) for s, v in enumerate(self.kept)]
            if self.phase >= 0:
                self.kept = sums[:half]
                sent = sums[half] if half == 1 else jnp.stack(sums[half:])
                line.hold(sent)
                got = place.swap_phase(sent, self.phase)
                self.got = got[None] if half == 1 else got
            else:
                block = sums[0].reshape(low_count, sums[0].shape[0] // low_count, -1)
                self.kept = [block[0]]
                line.hold(sums[0])
                self.got = [place.swap_low(block[o], o) for o in lows]

        def end(self):
            return jnp.stack(self.kept + list(line.take(*self.got)))

    masks = [m for m in (1, 2, 4, 8, 16) if m < place.reps]
    even = lax.axis_index("rep") % 2 == 0

    class Reps:
        def __init__(self, mine):
            columns = mine.shape[2] // 2
            low_half, high_half = mine[..., :columns], mine[..., columns:]
            self.held = jnp.where(even, low_half, high_half)
            sent = jnp.where(even, high_half, low_half)
            line.hold(sent)
            self.masks = masks[1:]
            self.got = place.swap_rep(sent, 1)

        def step(self):
            self.held = add(self.held, line.take(self.got)[0])
            line.hold(self.held)
            self.got = place.swap_rep(self.held, self.masks.pop(0) if self.masks else 1)

        def end(self):
            return [self.held, line.take(self.got)[0]]

    class Pairs:
        def __init__(self, mine):
            self.mine = mine
            self.masks = masks[1:] + masks[:1]
            self.got = place.swap_rep(mine, self.masks.pop(0))

        def step(self):
            self.mine = add(self.mine, line.take(self.got)[0])
            line.hold(self.mine)
            self.got = place.swap_rep(self.mine, self.masks.pop(0))

        def end(self):
            return self.mine, line.take(self.got)[0]

    split_x = split_tokens(place, layer_input, "split_input")
    coming = [place.swap_slot(split_x[j], j) for j in range(1, seqs)]
    if pair == 2:
        coming.append(place.swap_rep(split_x[0], 1))
    split_c = split_tokens(place, cotangent, "split_cotangent")
    vectors = (ln1_gain, ln1_bias, ln2_gain, ln2_bias, qkv_bias, out_bias, up_bias, down_bias)
    firsts, seconds = split_weights(place, w_qkv, w_out, w_up, w_down, vectors, positions)
    coming_second = [place.swap_low(seconds[o], o) for o in lows]
    coming = line.take(*coming)
    block_x = jnp.concatenate([split_x[0], *coming[: seqs - 1]], axis=0)
    tokens, grads = [[block_x]], []
    coming_x = to_low(block_x)
    if pair == 2:
        rest = jnp.concatenate(coming[: seqs - 1], axis=0)
        line.hold(rest)
        later_x = place.swap_rep(rest, 1)
    sent = lax.optimization_barrier((*split_c[1:], *coming))[: seqs - 1]
    coming_c = [place.swap_slot(v, j) for v, j in zip(sent, range(1, seqs))]
    line.hold(block_x)
    coming_second = line.take(*coming_second)
    block_second = jnp.concatenate([seconds[0], *coming_second], axis=0)
    line.hold(block_second)
    tokens[0].extend(line.take(*coming_x))
    coming_c = line.take(*coming_c)
    second = Gather(line.take(block_second)[0])
    block_c = jnp.concatenate([split_c[0], *coming_c], axis=0)
    line.hold(block_c)
    grads.append([block_c])
    coming_c = to_low(block_c)
    if pair == 2:
        later_x = line.take(later_x)[0]
        other_x = jnp.concatenate([coming[seqs - 1], later_x], axis=0)
        line.hold(other_x)
        coming_x = to_low(other_x)
        other_c = place.swap_rep(after(block_c, later_x), 1)
    grads[0].extend(line.take(*coming_c))
    second.step()
    if pair == 2:
        tokens.append([other_x, *line.take(*coming_x)])
    coming_first = [place.swap_low(v, o) for v, o in zip(line.take(*firsts[1:]), lows)]
    coming_first = line.take(*coming_first)
    block_first = jnp.concatenate([firsts[0], *coming_first], axis=0)
    line.hold(block_first)
    second.step()
    first = Gather(after(block_first, *second.slots))
    if pair == 2:
        other_c = line.take(other_c)[0]
        coming_c = to_low(other_c)

    w_second, vec, bias, lines_kept = second_tables(place, second.slots, rows, width)
    two, normed, hidden, grad_up, sums_middle, sums_back = [[None] * pair for _ in range(6)]

    def forward(z):
        two[z], normed[z], hidden[z], grad_up[z], sums_middle[z] = middle(
            place, z, tokens[z], grads[z], vec, w_second
        )

    def backward(z, attended, grad_qkv, w_first):
        keep, send, sums_back[z] = back(
            place, z, normed[z], hidden[z], grad_up[z], attended, grad_qkv, vec, w_second, w_first
        )
        return keep, [place.swap_low(send[o - 1][r], o) for o in lows for r in range(2)]

    def low_sum(keep, coming):
        coming = line.take(*coming)
        return jnp.stack(
            [sum([v.astype(F32) for v in coming[r::2]], keep[r].astype(F32)) for r in range(2)]
        )

    if pair == 2:
        grads.append([other_c, *line.take(*coming_c)])
        forward(1)
        keep, coming = backward(1, [], [], None)
    first.step(more=1)
    out_pieces, out_found, out_coming = [], [], []

    def next_piece():
        if out_coming:
            out_found.append(line.take(out_coming.pop())[0])
        if out_pieces:
            out_coming.append(place.swap_rep(after(out_pieces.pop(0), *line.ahead), 1))

    if pair == 2:
        line.pause()
        coming = line.take(*coming)
        sums = [
            sum(v.astype(F32) for v in [keep[r]] + list(coming[r::2])).astype(BF16) for r in range(2)
        ]
        cut = 3 * sums[0].shape[0] // 4
        out_pieces += [sums[0][:cut], jnp.concatenate([sums[0][cut:], sums[1]])]
        line.hold(*out_pieces)
        next_piece()
    forward(0)
    second_sums = Scatter(*second_grads(place, rows, two, grad_up, grads, hidden))

    next_piece()
    first.step()
    w_first, seen, cosine, sine = first_tables(place, first.slots, lines_kept, rows, width, span)
    one, heads = front(place, tokens[0], w_first, vec, bias, cosine, sine)
    attended, grad_qkv, sums_qkv = [[None] * place.groups for _ in range(3)]
    cot = grads[0]

    def attend(h):
        attended[h], grad_qkv[h], sums_qkv[h] = attention(
            place, h, span, *heads[h], cot, w_first, seen, cosine, sine
        )

    first_sums, counts = [], []

    def close(number, chosen):
        counts.append(len(chosen))
        first_sums.append(
            Scatter(
                *first_grads(
                    place, number, rows, one, cot,
                    [grad_qkv[h] for h in chosen], [attended[h] for h in chosen],
                )
            )
        )

    last_group = place.groups - 1
    for h in range(last_group):
        attend(h)
        if second_sums.phase >= 0:
            second_sums.step()
        if h == 1:
            next_piece()
    if last_group:
        close(0, list(range(last_group)))
    while second_sums.phase >= 0:
        second_sums.step()
    second_mine = second_sums.end()
    line.hold(second_mine)
    while out_coming:
        next_piece()
    second_reps = Pairs(second_mine) if pair == 2 else Reps(second_mine)
    attend(last_group)
    for v in first_sums:
        v.step()
    close(1, [last_group])
    keep, coming = backward(0, attended, grad_qkv, w_first)

    earlier, last = first_sums[:-1], first_sums[-1]
    for v in earlier:
        v.step()
    last.step()
    vector_sums = Scatter(
        *vector_grads(place, rows, 4 * place.heads * HD, sums_qkv, sums_back, sums_middle)
    )
    line.pause()
    reps = []
    for v in earlier:
        mine = v.end()
        line.hold(mine)
        reps.append(Reps(mine))
    while out_coming:
        next_piece()
    out_sum = low_sum(keep, coming)
    if pair == 2:
        out_sum = out_sum + jnp.concatenate(out_found).reshape(out_sum.shape).astype(F32)
    out_sum = out_sum.astype(BF16).reshape(2, seqs, span, width)
    line.hold(out_sum)
    blocks = [out_sum[:, s] for s in range(seqs)]

    def pass_on(phase):
        chosen = [s for s in range(seqs) if s >> phase & 1]
        got = place.swap_phase(jnp.stack([blocks[s] for s in chosen]), phase)
        return chosen, got

    def passed(chosen, got):
        got = line.take(got)[0]
        for k, s in enumerate(chosen):
            blocks[s] = got[k]

    going = pass_on(0)
    line.pause()
    vector_sums.step()
    last.step()
    line.pause()
    vector_sums.step()
    line.pause()
    mine = jnp.concatenate([last.end(), vector_sums.end()], axis=1)
    line.hold(mine)
    reps.append(Reps(mine))
    if pair == 2:
        second_reps.step()
    line.pause()
    for r in reps[:-1]:
        r.step()
        line.pause()
    reps[-1].step()
    line.pause()
    for phase in range(1, place.phases):
        passed(*going)
        going = pass_on(phase)
    line.pause()
    for r in reps:
        while r.masks:
            r.step()
            line.pause()
    for r in reps:
        r.step()
    if pair == 1:
        while second_reps.masks:
            second_reps.step()
            line.pause()
        second_reps.step()
        line.pause()
    if pair == 2:
        pieces = [v[o] for v in second_reps.end() for o in range(low_count)]
    else:
        pieces = second_reps.end()
        pieces = jnp.where(even, pieces[0], pieces[1]), jnp.where(even, pieces[1], pieces[0])
        pieces = list(jnp.concatenate(pieces, axis=2))
    grad_w_up, grad_w_down = second_end(place, pieces)
    passed(*going)
    output, grad_input = finish_tokens(place, layer_input, cotangent, vec, blocks)
    pieces = [p for r in reps for p in r.end()]
    grad_w_qkv, grad_w_out, *vector_outs = first_end(place, rows, width, counts, pieces)
    return (
        output,
        grad_input,
        grad_w_qkv,
        grad_w_out,
        grad_w_up,
        grad_w_down,
        *vector_outs,
    )


def solution(mesh):
    tokens = P("rep", "fsdp", None)
    matrix = P("fsdp", None)
    vector = P("fsdp")
    return jax.shard_map(
        on_device,
        mesh=mesh,
        in_specs=(tokens, P("rep", "fsdp"), tokens) + (matrix,) * 4 + (vector,) * 8,
        out_specs=(tokens, tokens) + (matrix,) * 4 + (vector,) * 8,
        check_vma=False,
    )
```

```python
import functools

import jax
import jax.numpy as jnp
from jax import lax
from jax.experimental import pallas as pl
from jax.experimental.pallas import tpu as pltpu
from jax.sharding import PartitionSpec as P

H = 12
HD = 64
ROT = 16
TILE = 256
VEC = 16
COSTS = {
    "tables_second": 0.1,
    "middle_1": 0.1,
    "back_1": 0.1,
    "second_grads": 0.1,
    "back_0": 2,
    "vector_grads": 10,
    "second_end": 0.3,
    "pause_7": 0.3,
    "pause_8": 0.3,
    "pause_9": 0.3,
    "pause_10": 0.3,
    "pause_11": 0.3,
    "pause_12": 0.3,
    "pause_13": 0.3,
    "tables_first": 0.1,
    "front": 0.1,
}
DEFAULT = 20

EPS = 1e-05
NEG = -1e30

F32 = jnp.float32
BF16 = jnp.bfloat16
I32 = jnp.int32

NN = ((1,), (0,))
NT = ((1,), (1,))
TN = ((0,), (0,))


def dot(a, b, dims):
    return lax.dot_general(a, b, (dims, ((), ())), preferred_element_type=F32)


def at(start, size, multiple):
    return pl.ds(pl.multiple_of(start, multiple), size)


class Place:
    def __init__(self, seqs, shards, reps):
        self.seqs, self.shards, self.reps = seqs, shards, reps
        self.low_count = shards // seqs
        self.pair = 2 if reps % 2 == 0 and H % (2 * self.low_count) == 0 else 1
        self.parts = self.pair * self.low_count
        self.line = Line()
        self.heads = 2 if H // self.low_count % 2 == 0 else 3
        self.groups = H // self.low_count // self.heads
        self.masks = []
        while 2 ** len(self.masks) < seqs:
            self.masks.append(2 ** len(self.masks))
        self.phases = len(self.masks)

    def chip(self):
        return lax.axis_index("fsdp") // self.low_count

    def low(self):
        return lax.axis_index("fsdp") % self.low_count

    def part(self):
        return (lax.axis_index("rep") % self.pair) * self.low_count + self.low()

    def owner(self, slot):
        even = sum(self.masks[p] for p in range(self.phases) if slot >> p & 1)
        odd = sum(self.masks[self.phases - 1 - p] for p in range(self.phases) if slot >> p & 1)
        if even == odd:
            return self.chip() ^ even
        return self.chip() ^ jnp.where(lax.axis_index("fsdp") % 2 == 0, even, odd)

    def slot(self, block):
        j = (block // self.low_count) ^ self.chip()
        other = sum((j >> p & 1) << (self.phases - 1 - p) for p in range(self.phases))
        even = lax.axis_index("fsdp") % 2 == 0 if self.low_count == 1 else block % self.low_count % 2 == 0
        return jnp.where(even, j, other)

    def swap_low(self, v, mask):
        return lax.ppermute(v, "fsdp", [(i, i ^ mask) for i in range(self.shards)])

    def swap_slot(self, v, slot):
        def to(i):
            order = self.masks if i % 2 == 0 else self.masks[::-1]
            return i ^ (sum(m for p, m in enumerate(order) if slot >> p & 1) * self.low_count)

        return lax.ppermute(v, "fsdp", [(i, to(i)) for i in range(self.shards)])

    def swap_phase(self, v, phase):
        def to(i):
            mask = self.masks[phase] if i % 2 == 0 else self.masks[self.phases - 1 - phase]
            return i ^ (mask * self.low_count)

        return lax.ppermute(v, "fsdp", [(i, to(i)) for i in range(self.shards)])

    def swap_rep(self, v, mask):
        return lax.ppermute(v, "rep", [(i, i ^ mask) for i in range(self.reps)])


def after(v, *others):
    return lax.optimization_barrier((v, *others))[0]


def whole(shape):
    return pl.BlockSpec(shape, lambda *_: (0,) * len(shape))


def pause_kernel(source, out):
    out[...] = source[...] + 1.0


class Line:
    def __init__(self):
        self.ahead = []
        self.count = jnp.zeros((8, 128), F32)
        self.pauses = 0

    def take(self, *arrays):
        found = lax.optimization_barrier((*arrays, *self.ahead))[: len(arrays)]
        self.ahead = [min(found, key=lambda v: v.size)]
        return found

    def hold(self, *arrays):
        self.ahead.extend(arrays)

    def pause(self):
        small = jax.ShapeDtypeStruct((8, 128), F32)
        block = whole(small.shape)
        self.pauses += 1
        name = f"pause_{self.pauses}"
        self.count = self.call(pause_kernel, name, (1,), [block], block, small, [], [self.count], 4)

    def call(self, kernel, name, grid, in_specs, out_specs, out_shape, scratch, args, vmem=40):
        args = list(args)
        if self.ahead:
            args[0] = after(args[0], *self.ahead)
        outs = pl.pallas_call(
            kernel,
            grid=grid,
            in_specs=in_specs,
            out_specs=out_specs,
            out_shape=out_shape,
            scratch_shapes=scratch,
            compiler_params=pltpu.CompilerParams(vmem_limit_bytes=vmem * 2**20),
            cost_estimate=pl.CostEstimate(
                flops=(cost := int(COSTS.get(name, DEFAULT) * 1.15e9)),
                bytes_accessed=int(cost // 320),
                transcendentals=0,
            ),
            name=name,
        )(*args)
        self.ahead = [min(jax.tree.leaves(outs), key=lambda v: v.size)]
        return outs


def split_kernel(place, source, *outs):
    for j, out in enumerate(outs):
        out[...] = source[place.owner(j)]


def split_tokens(place, v, name):
    seqs, span, width = v.shape
    return place.line.call(
        functools.partial(split_kernel, place),
        name,
        (1,),
        [whole(v.shape)],
        [whole((span, width))] * seqs,
        [jax.ShapeDtypeStruct((span, width), v.dtype)] * seqs,
        [],
        (v,),
        vmem=58,
    )


def weights_kernel(place, w_qkv, w_out, w_up, w_down, *rest):
    vectors, pos, outs = rest[:8], rest[8], rest[9:]
    rows = w_qkv.shape[0]
    parts, low_count = place.parts, place.low_count
    width = w_out.shape[1]
    step = place.heads * HD
    hidden = w_up.shape[1] // parts
    firsts, seconds = outs[:low_count], outs[low_count:]
    for k in range(low_count):

        @pl.when(place.low() == k)
        def _():
            for o in range(low_count):
                for h in range(place.groups):
                    begin = ((k ^ o) * place.groups + h) * step
                    for g in range(3):
                        to = (3 * h + g) * step
                        firsts[o][:, to : to + step] = w_qkv[
                            :, g * width + begin : g * width + begin + step
                        ]
                    to = (3 * place.groups + h) * step
                    firsts[o][:, to : to + step] = w_out[:, begin : begin + step]

    for o in range(low_count):
        lanes = at((place.part() ^ o) * hidden, hidden, 128)
        seconds[o][:rows, :hidden] = w_up[:, lanes]
        seconds[o][:rows, hidden:] = w_down[:, lanes]

    lanes = seconds[0].shape[1]
    lines = []
    for v in vectors:
        lines.append(
            jnp.concatenate([v[...].astype(F32), jnp.zeros((1, lanes - v.shape[1]), F32)], axis=1)
        )
    span = pos.shape[1]
    for values in (
        [(pos[s : s + 1, :] // 64).astype(F32) for s in range(pos.shape[0])],
        [(pos[s : s + 1, :] % 64).astype(F32) for s in range(pos.shape[0])],
    ):
        lines.append(
            jnp.concatenate(values + [jnp.zeros((1, lanes - span * pos.shape[0]), F32)], axis=1)
        )
    lines.append(jnp.zeros((VEC - len(lines), lanes), F32))
    block = jnp.concatenate(lines, axis=0).astype(BF16)
    for o in range(low_count):
        seconds[o][rows:, :] = block


def split_weights(place, w_qkv, w_out, w_up, w_down, vectors, pos):
    rows = w_qkv.shape[0]
    args = [w_qkv, w_out, w_up, w_down] + [v.reshape(1, -1) for v in vectors] + [pos]
    first = (rows, (w_qkv.shape[1] + w_out.shape[1]) // place.low_count)
    second = (rows + VEC, (w_up.shape[1] + w_down.shape[1]) // place.parts)
    shapes = [first] * place.low_count + [second] * place.low_count
    outs = place.line.call(
        functools.partial(weights_kernel, place),
        "split_weights",
        (1,),
        [whole(v.shape) for v in args],
        [whole(s) for s in shapes],
        [jax.ShapeDtypeStruct(s, BF16) for s in shapes],
        [],
        args,
        vmem=58,
    )
    return outs[: place.low_count], outs[place.low_count :]


def second_tables_kernel(place, rows, *rest):
    slots = rest[: place.seqs]
    w_out, vec_out, bias, lines_kept = rest[place.seqs :]
    seqs, low_count, parts = place.seqs, place.low_count, place.parts
    block = rows + VEC
    width = w_out.shape[0]
    step = place.heads * HD
    low = place.low()
    for s in range(seqs):
        owner = place.owner(s)
        for o in range(low_count):
            found = slots[s][o * block : (o + 1) * block, :]
            l = low ^ o
            w_out[at((owner * low_count + l) * rows, rows, 16), :] = found[:rows]
            lines_kept[owner * low_count + l] = found[rows:].astype(F32)

    def line(row, size):
        return jnp.concatenate(
            [lines_kept[n, row : row + 1, :size] for n in range(place.shards)], axis=1
        )

    for row in range(4):
        vec_out[row : row + 1, :] = line(row, rows)
    vec_out[4:5, :] = line(5, rows) + line(7, rows)
    all_up = line(6, 4 * rows)
    all_qkv = line(4, 3 * rows)
    for k in range(parts):

        @pl.when(place.part() == k)
        def _():
            vec_out[5:6, :] = all_up[:, k * width : (k + 1) * width]

    for k in range(low_count):

        @pl.when(low == k)
        def _():
            for h in range(place.groups):
                for g in range(3):
                    begin = g * width + (k * place.groups + h) * step
                    bias[h : h + 1, g * step : (g + 1) * step] = all_qkv[:, begin : begin + step]

    vec_out[6:, :] = jnp.zeros((2, width), F32)


def second_tables(place, slots, rows, width):
    shapes = [
        jax.ShapeDtypeStruct((width, slots[0].shape[1]), BF16),
        jax.ShapeDtypeStruct((8, width), F32),
        jax.ShapeDtypeStruct((8, 3 * place.heads * HD), F32),
        jax.ShapeDtypeStruct((place.shards, VEC, slots[0].shape[1]), F32),
    ]
    return place.line.call(
        functools.partial(second_tables_kernel, place, rows),
        "tables_second",
        (1,),
        [whole(v.shape) for v in slots],
        [whole(v.shape) for v in shapes],
        shapes,
        [],
        slots,
        vmem=40,
    )


def first_tables_kernel(place, rows, span, inverse, lines_kept, *rest):
    slots = rest[: place.seqs]
    w_out, first_out, cos_out, sin_out = rest[place.seqs :]
    low_count = place.low_count
    low, chip = place.low(), place.chip()
    for s in range(place.seqs):
        owner = place.owner(s)
        for o in range(low_count):
            w_out[at((owner * low_count + (low ^ o)) * rows, rows, 16), :] = slots[s][
                o * rows : (o + 1) * rows, :
            ]
    still = jnp.zeros((HD - ROT, span), F32)
    for f in range(place.shards):
        lanes = at(chip * span, span, 128)
        value = lines_kept[f, 8:9, lanes] * 64.0 + lines_kept[f, 9:10, lanes]
        index = f * span + lax.broadcasted_iota(I32, (1, span), 1)
        first_out[:, f * span : (f + 1) * span] = index - value.astype(I32)
        phase = inverse[...] * value
        cosine, sine = jnp.cos(phase), jnp.sin(phase)
        crel, j = (f % low_count) ^ low, place.slot(f)
        to = at(j * span, span, 128)
        cos_out[crel, to, :] = jnp.concatenate([cosine, cosine, still + 1.0] * 2, axis=0).T
        sin_out[crel, to, :] = jnp.concatenate([-sine, sine, still] * 2, axis=0).T


def first_tables(place, slots, lines_kept, rows, width, span):
    inverse = (10000.0 ** (-jnp.arange(0, ROT, 2, dtype=F32) / ROT)).reshape(-1, 1)
    shapes = [
        jax.ShapeDtypeStruct((width, slots[0].shape[1]), BF16),
        jax.ShapeDtypeStruct((1, place.shards * span), I32),
        jax.ShapeDtypeStruct((place.low_count, place.seqs * span, 128), F32),
        jax.ShapeDtypeStruct((place.low_count, place.seqs * span, 128), F32),
    ]
    args = [inverse, lines_kept] + slots
    return place.line.call(
        functools.partial(first_tables_kernel, place, rows, span),
        "tables_first",
        (1,),
        [whole(v.shape) for v in args],
        [whole(v.shape) for v in shapes],
        shapes,
        [],
        args,
        vmem=16,
    )


def piece_specs(pieces, lines):
    split = pieces[0].shape[0] // lines

    def spec(i, width):
        return pl.BlockSpec(
            (lines, width), lambda g: (jnp.clip(g - i * split, 0, split - 1), 0)
        )

    return [spec(i, v.shape[1]) for i, v in enumerate(pieces)]


def piece_now(refs, steps):
    found = refs[0][...]
    for i in range(1, len(refs)):
        found = jnp.where(pl.program_id(0) >= i * (steps // len(refs)), refs[i][...], found)
    return found


def norm(source):
    source = source.astype(F32)
    centred = source - jnp.mean(source, axis=1, keepdims=True)
    return centred * lax.rsqrt(jnp.mean(centred * centred, axis=1, keepdims=True) + EPS)


def turned(v):
    half = ROT // 2
    columns = v.shape[1]
    lane = lax.broadcasted_iota(I32, v.shape, 1) % HD
    ahead = pltpu.roll(v, columns - half, 1)
    behind = pltpu.roll(v, half, 1)
    return jnp.where(lane < half, ahead, behind)


def front_kernel(place, steps, *refs):
    tokens, refs = refs[: place.low_count], refs[place.low_count :]
    weight, vec, bias, cosine, sine, one_out, *outs = refs
    step = place.heads * HD
    one = (norm(piece_now(tokens, steps)) * vec[0:1, :] + vec[1:2, :]).astype(BF16)
    one_out[0] = one
    copies = 2 * step // 128
    cos_cols = jnp.concatenate([cosine[0]] * copies, axis=1)
    sin_cols = jnp.concatenate([sine[0]] * copies, axis=1)
    for h in range(place.groups):
        q_out, k_out, v_out = outs[3 * h : 3 * h + 3]
        qkv = dot(one, weight[:, 3 * step * h : 3 * step * (h + 1)], NN) + bias[h : h + 1, :]
        both = qkv[:, : 2 * step]
        both = both * cos_cols + turned(both) * sin_cols
        q_out[0] = both[:, :step].astype(BF16)
        k_out[0] = both[:, step:].astype(BF16)
        v_out[0] = qkv[:, 2 * step :].astype(BF16)


def front(place, tokens, weight, vec, bias, cosine, sine):
    groups = len(tokens)
    count, width = tokens[0].shape
    step = place.heads * HD
    split = 1
    lines = count // split
    by_step = lambda cols: pl.BlockSpec((1, lines, cols), lambda g: (g // split, g % split, 0))
    shaped = lambda cols: jax.ShapeDtypeStruct((groups, count, cols), BF16)
    outs = place.line.call(
        functools.partial(front_kernel, place, groups * split),
        "front",
        (groups * split,),
        piece_specs(tokens, lines)
        + [whole(weight.shape), whole(vec.shape), whole(bias.shape)] + [by_step(128)] * 2,
        [by_step(width)] + [by_step(step)] * (3 * place.groups),
        [shaped(width)] + [shaped(step)] * (3 * place.groups),
        [],
        [*tokens, weight, vec, bias, cosine, sine],
        vmem=20,
    )
    return outs[0], [outs[1 + 3 * h : 4 + 3 * h] for h in range(place.groups)]


def middle_kernel(count, steps, *refs):
    tokens, grads, refs = refs[:count], refs[count : 2 * count], refs[2 * count :]
    vec, weight, two_out, normed_out, hidden_out, grad_out, sums = refs

    @pl.when(pl.program_id(0) == 0)
    def _():
        sums[...] = jnp.zeros_like(sums)

    width = weight.shape[0]
    normed = norm(piece_now(tokens, steps))
    normed_out[0] = normed.astype(BF16)
    two = (normed * vec[2:3, :] + vec[3:4, :]).astype(BF16)
    two_out[0] = two
    up = dot(two, weight[:, :width], NN) + vec[5:6, :]
    grad = piece_now(grads, steps)
    grad_hidden = dot(grad, weight[:, width:], NN)
    bell = jnp.exp(-0.5 * up * up)
    below = 1.0 + (0.3275911 * 0.5**0.5) * jnp.abs(up)
    t = pl.reciprocal(below, approx=True)
    t = t * (2.0 - below * t)
    series = t * (
        0.127414796 + t * (-0.142248368 + t * (0.7107068705 + t * (-0.7265760135 + t * 0.5307027145)))
    )
    tail = series * bell
    share = jnp.where(up >= 0.0, 1.0 - tail, tail)
    hidden_out[0] = (up * share).astype(BF16)
    slope = share + up * (bell * 0.3989422804014327)
    grad_up = (grad_hidden * slope).astype(BF16)
    grad_out[0] = grad_up
    sums[0:1, :] += jnp.sum(grad_up.astype(F32), axis=0, keepdims=True)
    sums[1:2, :] += jnp.sum(grad.astype(F32), axis=0, keepdims=True)


def middle(place, z, tokens, grads, vec, weight):
    groups = len(tokens)
    count, width = tokens[0].shape
    split = 1
    lines = count // split
    by_step = pl.BlockSpec((1, lines, width), lambda g: (g // split, g % split, 0))
    return place.line.call(
        functools.partial(middle_kernel, groups, groups * split),
        f"middle_{z}",
        (groups * split,),
        piece_specs(tokens, lines)
        + piece_specs(grads, lines)
        + [whole(vec.shape), whole(weight.shape)],
        [by_step] * 4 + [whole((8, width))],
        [jax.ShapeDtypeStruct((groups, count, width), BF16)] * 4 + [jax.ShapeDtypeStruct((8, width), F32)],
        [],
        [*tokens, *grads, vec, weight],
        vmem=20,
    )


def attention_kernel(
    place, group, span, q_in, k_in, v_in, w_in, first_in, cos_in, sin_in, *refs
):
    cot_in, refs = refs[: place.low_count], refs[place.low_count :]
    o_out, g_out, sums, qs, ks, vs, gs, o_turned, gq_turned, gk_sum, gv_sum = refs
    low_count = place.low_count
    count, columns = q_in.shape[1:]
    heads = columns // HD
    length = low_count * count
    begin = (3 * place.groups + group) * columns
    w_out = w_in[:, begin : begin + columns]

    def slot(f):
        crel = (f % low_count) ^ place.low()
        j = place.slot(f)
        return crel, at(j * span, span, 128)

    for f in range(length // span):
        to = slice(f * span, (f + 1) * span)
        crel, lines = slot(f)
        for source, kept in ((q_in, qs), (k_in, ks), (v_in, vs)):
            found = source[crel, lines, :]
            for h in range(heads):
                kept[h, to, :] = found[:, h * HD : (h + 1) * HD]
        cot = cot_in[0][lines, :]
        for o in range(1, low_count):
            cot = jnp.where(crel == o, cot_in[o][lines, :], cot)
        found = dot(cot, w_out, NN).astype(BF16)
        for h in range(heads):
            gs[h, to, :] = found[:, h * HD : (h + 1) * HD]

    def one_head(h, carry):
        keys = ks[h]
        values = vs[h]
        keys_turned = keys.astype(F32).T.astype(BF16)
        values_turned = values.astype(F32).T.astype(BF16)
        for i in range(length // TILE):
            here = slice(i * TILE, (i + 1) * TILE)
            query = qs[h, here, :]
            grad = gs[h, here, :]
            first = first_in[:, here]
            tiles = [slice(j * TILE, (j + 1) * TILE) for j in range(i + 1)]
            scores, grads = [], []
            for j, tile in enumerate(tiles):
                raw = dot(keys[tile], query, NT) * (0.125 * 1.4426950408889634)
                key_index = j * TILE + lax.broadcasted_iota(I32, (TILE, TILE), 0)
                seen = key_index >= first
                if j == i:
                    query_index = i * TILE + lax.broadcasted_iota(I32, (TILE, TILE), 1)
                    seen = seen & (key_index <= query_index)
                scores.append(jnp.where(seen, raw, NEG))
            top = functools.reduce(
                jnp.maximum, [jnp.max(raw, axis=0, keepdims=True) for raw in scores]
            )
            weights = [jnp.exp2(raw - top) for raw in scores]
            share = 1.0 / sum(jnp.sum(w, axis=0, keepdims=True) for w in weights)
            grads = [dot(values[tile], grad, NT) for tile in tiles]
            carried = share * sum(
                jnp.sum(w * g, axis=0, keepdims=True) for w, g in zip(weights, grads)
            )
            out, gq = None, None
            for j, tile in enumerate(tiles):
                probs = weights[j] * share
                low = probs.astype(BF16)
                grad_scores = (probs * (grads[j] - carried)).astype(BF16)
                out_part = dot(values_turned[:, tile], low, NN)
                gq_part = dot(keys_turned[:, tile], grad_scores, NN)
                gk_part = dot(grad_scores, query, NN)
                gv_part = dot(low, grad, NN)
                out = out_part if j == 0 else out + out_part
                gq = gq_part if j == 0 else gq + gq_part
                if j < i:
                    gk_sum[h, tile, :] += gk_part
                    gv_sum[h, tile, :] += gv_part
                else:
                    gk_sum[h, tile, :] = gk_part
                    gv_sum[h, tile, :] = gv_part
            o_turned[h, :, here] = out
            gq_turned[h, :, here] = gq
        return carry

    lax.fori_loop(0, heads, one_head, 0)
    total = jnp.zeros((1, 3 * columns), F32)
    for f in range(length // span):
        crel, lines = slot(f)
        to = slice(f * span, (f + 1) * span)
        o_out[crel, lines, :] = jnp.concatenate(
            [o_turned[h, :, to].T for h in range(heads)], axis=1
        ).astype(BF16)
        both = jnp.concatenate(
            [gq_turned[h, :, to].T for h in range(heads)] + [gk_sum[h, to, :] for h in range(heads)],
            axis=1,
        )
        both = both * 0.125
        copies = 2 * columns // 128
        cos_cols = jnp.concatenate([cos_in[crel, lines, :]] * copies, axis=1)
        sin_cols = jnp.concatenate([sin_in[crel, lines, :]] * copies, axis=1)
        both = both * cos_cols - turned(both) * sin_cols
        value = jnp.concatenate([gv_sum[h, to, :] for h in range(heads)], axis=1)
        grad = jnp.concatenate([both, value], axis=1).astype(BF16)
        g_out[crel, lines, :] = grad
        total = total + jnp.sum(grad.astype(F32), axis=0, keepdims=True)
    sums[...] = jnp.concatenate([total, jnp.zeros((7, 3 * columns), F32)], axis=0)


def attention(place, group, span, q, k, v, cot, w, first, cosine, sine):
    count, columns = q.shape[1:]
    low_count = place.low_count
    heads = columns // HD
    length = low_count * count
    outs = [
        jax.ShapeDtypeStruct((low_count, count, columns), BF16),
        jax.ShapeDtypeStruct((low_count, count, 3 * columns), BF16),
        jax.ShapeDtypeStruct((8, 3 * columns), F32),
    ]
    args = [q, k, v, w, first, cosine, sine, *cot]
    return place.line.call(
        functools.partial(attention_kernel, place, group, span),
        f"attention_{group}",
        (1,),
        [whole(a.shape) for a in args],
        [whole(a.shape) for a in outs],
        outs,
        [pltpu.VMEM((heads, length, HD), BF16)] * 4
        + [pltpu.VMEM((heads, HD, length), F32)] * 2
        + [pltpu.VMEM((heads, length, HD), F32)] * 2,
        args,
        vmem=16 * (length // 1024),
    )


def back_kernel(place, groups, *refs):
    normed, hidden, grad_up = refs[:3]
    attended, grad_qkv = refs[3 : 3 + groups], refs[3 + groups : 3 + 2 * groups]
    vec, second = refs[3 + 2 * groups : 5 + 2 * groups]
    keep, send, sums = refs[-3:]
    step = pl.program_id(0)
    width = normed.shape[2]

    @pl.when(step == 0)
    def _():
        sums[...] = jnp.zeros_like(sums)

    two = dot(grad_up[0], second[:, :width], NT)
    out = dot(hidden[0], second[:, width:], NT)
    both = two * vec[2:3, :]
    source = normed[0].astype(F32)
    sums[2:3, :] += jnp.sum(two * source, axis=0, keepdims=True)
    sums[3:4, :] += jnp.sum(two, axis=0, keepdims=True)
    if groups:
        first = refs[5 + 2 * groups]
        cols = place.heads * HD
        one = None
        for h in range(groups):
            term = dot(grad_qkv[h][0], first[:, 3 * cols * h : 3 * cols * (h + 1)], NT)
            one = term if one is None else one + term
            begin = (3 * groups + h) * cols
            out = out + dot(attended[h][0], first[:, begin : begin + cols], NT)
        both = both + one * vec[0:1, :]
        sums[0:1, :] += jnp.sum(one * source, axis=0, keepdims=True)
        sums[1:2, :] += jnp.sum(one, axis=0, keepdims=True)
    split = pl.num_programs(0) // place.low_count

    @pl.when(step < split)
    def _():
        keep[0] = out.astype(BF16)
        keep[1] = both.astype(BF16)

    @pl.when(step >= split)
    def _():
        send[0, 0] = out.astype(BF16)
        send[0, 1] = both.astype(BF16)


def back(place, z, normed, hidden, grad_up, attended, grad_qkv, vec, second, first):
    low_count = place.low_count
    groups, count, width = normed.shape
    split = 1
    lines = count // split
    by_step = lambda cols: pl.BlockSpec((1, lines, cols), lambda g: (g // split, g % split, 0))
    args = [normed, hidden, grad_up, *attended, *grad_qkv]
    fixed = [vec, second] + ([first] if attended else [])

    def sent(g):
        later = jnp.maximum(g - split, 0)
        return (later // split, 0, later % split, 0)

    return place.line.call(
        functools.partial(back_kernel, place, len(attended)),
        f"back_{z}",
        (groups * split,),
        [by_step(v.shape[2]) for v in args] + [whole(v.shape) for v in fixed],
        [
            pl.BlockSpec((2, lines, width), lambda g: (0, jnp.minimum(g, split - 1), 0)),
            pl.BlockSpec((1, 2, lines, width), sent),
            whole((8, width)),
        ],
        [
            jax.ShapeDtypeStruct((2, count, width), BF16),
            jax.ShapeDtypeStruct((low_count - 1, 2, count, width), BF16),
            jax.ShapeDtypeStruct((8, width), F32),
        ],
        [],
        args + fixed,
        vmem=24,
    )


def store_rows(place, rows, block, value, scratch, columns):
    low_count = place.low_count
    for s in range(place.seqs):
        owner = place.owner(s)
        for o in range(low_count):
            begin = owner * (low_count * rows) + (place.low() ^ o) * rows
            scratch[s, o * block : o * block + rows, columns] = value[at(begin, rows, 16), :].astype(BF16)


def product(lefts, rights):
    each = len(lefts) // len(rights)
    total = None
    for i, left in enumerate(lefts):
        lines = left.shape[0]
        right = rights[i // each][(i % each) * lines : (i % each + 1) * lines, :]
        term = dot(left[...], right, TN)
        total = term if total is None else total + term
    return total


def second_grads_kernel(place, rows, count, *refs):
    two, grad_up, hidden = [refs[k * count : (k + 1) * count] for k in range(3)]
    cot, (keep, send, total, turned_rows) = refs[3 * count : -4], refs[-4:]
    step = pl.program_id(0)
    width = two[0].shape[1]
    half = place.seqs // 2

    def one(left, right, columns):
        total[...] = product(left, right)
        store_rows(place, rows, rows, total, turned_rows, columns)

    @pl.when(step == 0)
    def _():
        one(two, grad_up, slice(0, width))

    @pl.when(step == 1)
    def _():
        one(cot, hidden, slice(width, 2 * width))
        keep[...] = turned_rows[:half]
        send[...] = turned_rows[half:]


def second_grads(place, rows, two, grad_up, cot, hidden):
    width = two[0].shape[2]
    flat = [v.reshape(-1, width) for v in (*two, *grad_up, *hidden)] + [p for c in cot for p in c]
    half = (place.seqs // 2, place.low_count * rows, 2 * width)
    return place.line.call(
        functools.partial(second_grads_kernel, place, rows, len(two)),
        "second_grads",
        (2,),
        [whole(v.shape) for v in flat],
        [whole(half)] * 2,
        [jax.ShapeDtypeStruct(half, BF16)] * 2,
        [pltpu.VMEM((width, width), F32), pltpu.VMEM((2 * half[0],) + half[1:], BF16)],
        flat,
        vmem=20,
    )


def first_grads_kernel(place, rows, count, one, *refs):
    grad_qkv, attended, refs = refs[:count], refs[count : 2 * count], refs[2 * count :]
    cot, (keep, send, total, ordered) = refs[:-4], refs[-4:]
    half = place.seqs // 2
    step = place.heads * HD
    for h in range(count):
        total[:, : 3 * step] = dot(one[...], grad_qkv[h][...], TN)
        total[:, 3 * step :] = product(cot, [attended[h]])
        store_rows(place, rows, rows, total, ordered, slice(4 * step * h, 4 * step * (h + 1)))
    keep[...] = ordered[:half]
    send[...] = ordered[half:]


def first_grads(place, number, rows, one, cot, grad_qkv, attended):
    width = one.shape[2]
    step = place.heads * HD
    count = len(attended)
    args = [v.reshape(-1, v.shape[2]) for v in (one, *grad_qkv, *attended)] + list(cot)
    half = (place.seqs // 2, place.low_count * rows, 4 * step * count)
    return place.line.call(
        functools.partial(first_grads_kernel, place, rows, count),
        f"first_grads_{number}",
        (1,),
        [whole(v.shape) for v in args],
        [whole(half)] * 2,
        [jax.ShapeDtypeStruct(half, BF16)] * 2,
        [pltpu.VMEM((width, 4 * step), F32), pltpu.VMEM((2 * half[0],) + half[1:], BF16)],
        args,
        vmem=16,
    )


def vectors_kernel(place, rows, *refs):
    sums_qkv = refs[: place.groups]
    sums_back = refs[place.groups : place.groups + place.pair]
    sums_middle = refs[place.groups + place.pair : -4]
    keep, send, lines_kept, ordered = refs[-4:]
    seqs, low_count, parts = place.seqs, place.low_count, place.parts
    width = keep.shape[2]
    step = place.heads * HD
    half = seqs // 2
    back = sum(s[...] for s in sums_back)
    up = sum(s[0:1, :] for s in sums_middle)
    grad = sums_middle[0][1:2, :] * (1.0 / low_count)
    zero = jnp.zeros((1, step), F32)
    all_qkv = jnp.concatenate(
        [
            jnp.where(place.low() == k, sums_qkv[h][0:1, g * step : (g + 1) * step], zero)
            for g in range(3)
            for k in range(low_count)
            for h in range(place.groups)
        ],
        axis=1,
    )
    all_up = jnp.concatenate([jnp.where(place.part() == k, up, 0.0) for k in range(parts)], axis=1)
    lines = [(back[r : r + 1], rows) for r in range(4)]
    lines += [(all_qkv, 3 * rows), (grad, rows), (all_up, 4 * rows)]
    for n in range(place.shards):
        made = [
            jnp.concatenate(
                [v[:, n * size : (n + 1) * size], jnp.zeros((1, width - size), F32)], axis=1
            )
            for v, size in lines
        ]
        made.append(jnp.zeros((VEC - len(made), width), F32))
        lines_kept[n] = jnp.concatenate(made, axis=0)
    for s in range(seqs):
        for o in range(low_count):
            n = place.owner(s) * low_count + (place.low() ^ o)
            ordered[s, o * VEC : (o + 1) * VEC, :] = lines_kept[n].astype(BF16)
    keep[...] = ordered[:half]
    send[...] = ordered[half:]


def vector_grads(place, rows, width, sums_qkv, sums_back, sums_middle):
    half = (place.seqs // 2, place.low_count * VEC, width)
    args = [*sums_qkv, *sums_back, *sums_middle]
    return place.line.call(
        functools.partial(vectors_kernel, place, rows),
        "vector_grads",
        (1,),
        [whole(v.shape) for v in args],
        [whole(half)] * 2,
        [jax.ShapeDtypeStruct(half, BF16)] * 2,
        [
            pltpu.VMEM((place.shards, VEC, width), F32),
            pltpu.VMEM((2 * half[0],) + half[1:], BF16),
        ],
        args,
        vmem=16,
    )


def tokens_kernel(place, source, cot, vec, *rest):
    blocks, (out, grad_in) = rest[: place.seqs], rest[place.seqs :]
    for j in range(place.seqs):
        s = place.owner(j)
        x = source[s].astype(F32)
        out[s] = (x + blocks[j][0].astype(F32) + vec[4:5, :]).astype(BF16)
        mean = jnp.mean(x, axis=1, keepdims=True)
        centred = x - mean
        scale = lax.rsqrt(jnp.mean(centred * centred, axis=1, keepdims=True) + EPS)
        normed = centred * scale
        e = blocks[j][1].astype(F32)
        pulled = (
            e
            - jnp.mean(e, axis=1, keepdims=True)
            - normed * jnp.mean(e * normed, axis=1, keepdims=True)
        ) * scale
        grad_in[s] = (cot[s].astype(F32) + pulled).astype(BF16)


def finish_tokens(place, source, cot, vec, blocks):
    return place.line.call(
        functools.partial(tokens_kernel, place),
        "finish_tokens",
        (1,),
        [whole(source.shape)] * 2 + [whole(vec.shape)] + [whole(b.shape) for b in blocks],
        [whole(source.shape)] * 2,
        [jax.ShapeDtypeStruct(source.shape, BF16)] * 2,
        [],
        [source, cot, vec] + blocks,
    )


def first_end_kernel(place, rows, counts, *refs):
    found, refs = refs[: 2 * len(counts)], refs[2 * len(counts) + 1 :]
    w_qkv, w_out, vectors = refs[0], refs[1], refs[2:]
    low_count, groups = place.low_count, place.groups
    width = w_out.shape[1]
    step = place.heads * HD
    even = (lax.axis_index("rep") % 2) == 0
    total = None
    first = 0
    for i, count in enumerate(counts):
        for o in range(low_count):
            mine, other = found[2 * i][o].astype(F32), found[2 * i + 1][o].astype(F32)
            piece = jnp.concatenate(
                [jnp.where(even, mine, other), jnp.where(even, other, mine)], axis=1
            )
            for k in range(low_count):

                @pl.when(place.low() == k)
                def _():
                    for h in range(count):
                        begin = ((k ^ o) * groups + first + h) * step
                        for g in range(3):
                            to = g * width + begin
                            part = (4 * h + g) * step
                            w_qkv[:, to : to + step] = piece[:rows, part : part + step]
                        part = (4 * h + 3) * step
                        w_out[:, begin : begin + step] = piece[:rows, part : part + step]

            if i == len(counts) - 1:
                total = piece[rows:] if total is None else total + piece[rows:]
        first += count
    for r, out in enumerate(vectors):
        out[...] = total[5 if r == 7 else r, : out.shape[0]]


def first_end(place, rows, width, counts, pieces):
    shapes = [(rows, 3 * width), (rows, width)]
    shapes += [(n * rows,) for n in (1, 1, 1, 1, 3, 1, 4, 1)]
    pieces = pieces + [place.line.count]
    return place.line.call(
        functools.partial(first_end_kernel, place, rows, counts),
        "first_end",
        (1,),
        [whole(p.shape) for p in pieces],
        [whole(v) for v in shapes],
        [jax.ShapeDtypeStruct(v, F32) for v in shapes],
        [],
        pieces,
    )


def second_end_kernel(place, *refs):
    pieces = refs[: place.parts]
    w_up, w_down = refs[place.parts :]
    parts = place.parts
    step = w_up.shape[1] // parts
    for r in range(parts):
        t = place.part() ^ r
        w_up[:, at(t * step, step, 128)] = pieces[r][:, :step].astype(F32)
        w_down[:, at(t * step, step, 128)] = pieces[r][:, step:].astype(F32)


def second_end(place, pieces):
    rows, columns = pieces[0].shape
    shape = (rows, columns // 2 * place.parts)
    return place.line.call(
        functools.partial(second_end_kernel, place),
        "second_end",
        (1,),
        [whole(p.shape) for p in pieces],
        [whole(shape)] * 2,
        [jax.ShapeDtypeStruct(shape, F32)] * 2,
        [],
        pieces,
    )


def add(a, b):
    return (a.astype(F32) + b.astype(F32)).astype(BF16)


def on_device(
    layer_input,
    positions,
    cotangent,
    w_qkv,
    w_out,
    w_up,
    w_down,
    ln1_gain,
    ln1_bias,
    ln2_gain,
    ln2_bias,
    qkv_bias,
    out_bias,
    up_bias,
    down_bias,
):
    seqs, span, width = layer_input.shape
    place = Place(seqs, lax.axis_size("fsdp"), lax.axis_size("rep"))
    low_count, pair = place.low_count, place.pair
    rows = w_qkv.shape[0]

    line = place.line
    lows = range(1, low_count)

    def to_low(v):
        return [place.swap_low(v, o) for o in lows]

    class Gather:
        def __init__(self, block):
            self.slots = [block]
            self.coming = [[place.swap_phase(block, p)] for p in range(place.phases)]

        def step(self, more=0):
            count = len(self.coming[0])
            ahead = self.coming[1][:more] if more else []
            got = line.take(*self.coming.pop(0), *ahead)
            if more:
                self.coming[0][:more] = got[count:]
            for later, p in zip(self.coming, range(place.phases - len(self.coming), place.phases)):
                later.extend(place.swap_phase(v, p) for v in got[:count])
            self.slots.extend(got[:count])

    class Scatter:
        def __init__(self, keep, send):
            self.phase = place.phases - 1
            self.kept = [keep[s] for s in range(keep.shape[0])]
            self.got = place.swap_phase(send, self.phase)

        def step(self):
            got = line.take(self.got)[0]
            self.phase -= 1
            half = len(self.kept) // 2
            sums = [add(v, got[s]) for s, v in enumerate(self.kept)]
            if self.phase >= 0:
                self.kept = sums[:half]
                sent = sums[half] if half == 1 else jnp.stack(sums[half:])
                line.hold(sent)
                got = place.swap_phase(sent, self.phase)
                self.got = got[None] if half == 1 else got
            else:
                block = sums[0].reshape(low_count, sums[0].shape[0] // low_count, -1)
                self.kept = [block[0]]
                line.hold(sums[0])
                self.got = [place.swap_low(block[o], o) for o in lows]

        def end(self):
            return jnp.stack(self.kept + list(line.take(*self.got)))

    masks = [m for m in (1, 2, 4, 8, 16) if m < place.reps]
    even = lax.axis_index("rep") % 2 == 0

    class Reps:
        def __init__(self, mine):
            columns = mine.shape[2] // 2
            low_half, high_half = mine[..., :columns], mine[..., columns:]
            self.held = jnp.where(even, low_half, high_half)
            sent = jnp.where(even, high_half, low_half)
            line.hold(sent)
            self.masks = masks[1:]
            self.got = place.swap_rep(sent, 1)

        def step(self):
            self.held = add(self.held, line.take(self.got)[0])
            line.hold(self.held)
            self.got = place.swap_rep(self.held, self.masks.pop(0) if self.masks else 1)

        def end(self):
            return [self.held, line.take(self.got)[0]]

    class Pairs:
        def __init__(self, mine):
            self.mine = mine
            self.masks = masks[1:] + masks[:1]
            self.got = place.swap_rep(mine, self.masks.pop(0))

        def step(self):
            self.mine = add(self.mine, line.take(self.got)[0])
            line.hold(self.mine)
            self.got = place.swap_rep(self.mine, self.masks.pop(0))

        def end(self):
            return self.mine, line.take(self.got)[0]

    split_x = split_tokens(place, layer_input, "split_input")
    coming = [place.swap_slot(split_x[j], j) for j in range(1, seqs)]
    if pair == 2:
        coming.append(place.swap_rep(split_x[0], 1))
    split_c = split_tokens(place, cotangent, "split_cotangent")
    vectors = (ln1_gain, ln1_bias, ln2_gain, ln2_bias, qkv_bias, out_bias, up_bias, down_bias)
    firsts, seconds = split_weights(place, w_qkv, w_out, w_up, w_down, vectors, positions)
    coming_second = [place.swap_low(seconds[o], o) for o in lows]
    coming = line.take(*coming)
    block_x = jnp.concatenate([split_x[0], *coming[: seqs - 1]], axis=0)
    tokens, grads = [[block_x]], []
    coming_x = to_low(block_x)
    if pair == 2:
        rest = jnp.concatenate(coming[: seqs - 1], axis=0)
        line.hold(rest)
        later_x = place.swap_rep(rest, 1)
    sent = lax.optimization_barrier((*split_c[1:], *coming))[: seqs - 1]
    coming_c = [place.swap_slot(v, j) for v, j in zip(sent, range(1, seqs))]
    line.hold(block_x)
    coming_second = line.take(*coming_second)
    block_second = jnp.concatenate([seconds[0], *coming_second], axis=0)
    line.hold(block_second)
    tokens[0].extend(line.take(*coming_x))
    coming_c = line.take(*coming_c)
    second = Gather(line.take(block_second)[0])
    block_c = jnp.concatenate([split_c[0], *coming_c], axis=0)
    line.hold(block_c)
    grads.append([block_c])
    coming_c = to_low(block_c)
    if pair == 2:
        later_x = line.take(later_x)[0]
        other_x = jnp.concatenate([coming[seqs - 1], later_x], axis=0)
        line.hold(other_x)
        coming_x = to_low(other_x)
        other_c = place.swap_rep(after(block_c, later_x), 1)
    grads[0].extend(line.take(*coming_c))
    second.step()
    if pair == 2:
        tokens.append([other_x, *line.take(*coming_x)])
    coming_first = [place.swap_low(v, o) for v, o in zip(line.take(*firsts[1:]), lows)]
    coming_first = line.take(*coming_first)
    block_first = jnp.concatenate([firsts[0], *coming_first], axis=0)
    line.hold(block_first)
    second.step()
    first = Gather(after(block_first, *second.slots))
    if pair == 2:
        other_c = line.take(other_c)[0]
        coming_c = to_low(other_c)

    w_second, vec, bias, lines_kept = second_tables(place, second.slots, rows, width)
    two, normed, hidden, grad_up, sums_middle, sums_back = [[None] * pair for _ in range(6)]

    def forward(z):
        two[z], normed[z], hidden[z], grad_up[z], sums_middle[z] = middle(
            place, z, tokens[z], grads[z], vec, w_second
        )

    def backward(z, attended, grad_qkv, w_first):
        keep, send, sums_back[z] = back(
            place, z, normed[z], hidden[z], grad_up[z], attended, grad_qkv, vec, w_second, w_first
        )
        return keep, [place.swap_low(send[o - 1][r], o) for o in lows for r in range(2)]

    def low_sum(keep, coming):
        coming = line.take(*coming)
        return jnp.stack(
            [sum([v.astype(F32) for v in coming[r::2]], keep[r].astype(F32)) for r in range(2)]
        )

    if pair == 2:
        grads.append([other_c, *line.take(*coming_c)])
        forward(1)
        keep, coming = backward(1, [], [], None)
    first.step(more=1)
    out_pieces, out_found, out_coming = [], [], []

    def next_piece():
        if out_coming:
            out_found.append(line.take(out_coming.pop())[0])
        if out_pieces:
            out_coming.append(place.swap_rep(after(out_pieces.pop(0), *line.ahead), 1))

    if pair == 2:
        line.pause()
        coming = line.take(*coming)
        sums = [
            sum(v.astype(F32) for v in [keep[r]] + list(coming[r::2])).astype(BF16) for r in range(2)
        ]
        cut = 3 * sums[0].shape[0] // 4
        out_pieces += [sums[0][:cut], jnp.concatenate([sums[0][cut:], sums[1]])]
        line.hold(*out_pieces)
        next_piece()
    forward(0)
    second_sums = Scatter(*second_grads(place, rows, two, grad_up, grads, hidden))

    next_piece()
    first.step()
    w_first, seen, cosine, sine = first_tables(place, first.slots, lines_kept, rows, width, span)
    one, heads = front(place, tokens[0], w_first, vec, bias, cosine, sine)
    attended, grad_qkv, sums_qkv = [[None] * place.groups for _ in range(3)]
    cot = grads[0]

    def attend(h):
        attended[h], grad_qkv[h], sums_qkv[h] = attention(
            place, h, span, *heads[h], cot, w_first, seen, cosine, sine
        )

    first_sums, counts = [], []

    def close(number, chosen):
        counts.append(len(chosen))
        first_sums.append(
            Scatter(
                *first_grads(
                    place, number, rows, one, cot,
                    [grad_qkv[h] for h in chosen], [attended[h] for h in chosen],
                )
            )
        )

    last_group = place.groups - 1
    for h in range(last_group):
        attend(h)
        if second_sums.phase >= 0:
            second_sums.step()
        if h == 1:
            next_piece()
    if last_group:
        close(0, list(range(last_group)))
    while second_sums.phase >= 0:
        second_sums.step()
    second_mine = second_sums.end()
    line.hold(second_mine)
    while out_coming:
        next_piece()
    second_reps = Pairs(second_mine) if pair == 2 else Reps(second_mine)
    attend(last_group)
    for v in first_sums:
        v.step()
    close(1, [last_group])
    keep, coming = backward(0, attended, grad_qkv, w_first)

    earlier, last = first_sums[:-1], first_sums[-1]
    for v in earlier:
        v.step()
    last.step()
    vector_sums = Scatter(
        *vector_grads(place, rows, 4 * place.heads * HD, sums_qkv, sums_back, sums_middle)
    )
    line.pause()
    reps = []
    for v in earlier:
        mine = v.end()
        line.hold(mine)
        reps.append(Reps(mine))
    while out_coming:
        next_piece()
    out_sum = low_sum(keep, coming)
    if pair == 2:
        out_sum = out_sum + jnp.concatenate(out_found).reshape(out_sum.shape).astype(F32)
    out_sum = out_sum.astype(BF16).reshape(2, seqs, span, width)
    line.hold(out_sum)
    blocks = [out_sum[:, s] for s in range(seqs)]

    def pass_on(phase):
        chosen = [s for s in range(seqs) if s >> phase & 1]
        got = place.swap_phase(jnp.stack([blocks[s] for s in chosen]), phase)
        return chosen, got

    def passed(chosen, got):
        got = line.take(got)[0]
        for k, s in enumerate(chosen):
            blocks[s] = got[k]

    going = pass_on(0)
    line.pause()
    vector_sums.step()
    last.step()
    line.pause()
    vector_sums.step()
    line.pause()
    mine = jnp.concatenate([last.end(), vector_sums.end()], axis=1)
    line.hold(mine)
    reps.append(Reps(mine))
    if pair == 2:
        second_reps.step()
    line.pause()
    for r in reps[:-1]:
        r.step()
        line.pause()
    reps[-1].step()
    line.pause()
    for phase in range(1, place.phases):
        passed(*going)
        going = pass_on(phase)
    line.pause()
    for r in reps:
        while r.masks:
            r.step()
            line.pause()
    for r in reps:
        r.step()
    if pair == 1:
        while second_reps.masks:
            second_reps.step()
            line.pause()
        second_reps.step()
        line.pause()
    if pair == 2:
        pieces = [v[o] for v in second_reps.end() for o in range(low_count)]
    else:
        pieces = second_reps.end()
        pieces = jnp.where(even, pieces[0], pieces[1]), jnp.where(even, pieces[1], pieces[0])
        pieces = list(jnp.concatenate(pieces, axis=2))
    grad_w_up, grad_w_down = second_end(place, pieces)
    passed(*going)
    output, grad_input = finish_tokens(place, layer_input, cotangent, vec, blocks)
    pieces = [p for r in reps for p in r.end()]
    grad_w_qkv, grad_w_out, *vector_outs = first_end(place, rows, width, counts, pieces)
    return (
        output,
        grad_input,
        grad_w_qkv,
        grad_w_out,
        grad_w_up,
        grad_w_down,
        *vector_outs,
    )


def solution(mesh):
    tokens = P("rep", "fsdp", None)
    matrix = P("fsdp", None)
    vector = P("fsdp")
    return jax.shard_map(
        on_device,
        mesh=mesh,
        in_specs=(tokens, P("rep", "fsdp"), tokens) + (matrix,) * 4 + (vector,) * 8,
        out_specs=(tokens, tokens) + (matrix,) * 4 + (vector,) * 8,
        check_vma=False,
    )
```
